32 devices in a mesh: zg: 4 (over z), zl: 8 (over y, x, core).
Axes of the slice: x: 2, y: 2, z: 4, core: 2. Of those that a mesh axis runs over, the one named last changes fastest.
Arguments:
- brick_data: float32 [512, 16, 256], P(('zg', 'zl')), may hold values from -6 to 6
- brick_xy: int32 [2, 512], P(None, ('zg', 'zl')), may hold values from 0 to 31, as said below
- brick_live: int32 [1, 32], P(None, ('zg', 'zl')), may hold values from 1 to 16, as said below
Outputs:
- pressure_real: float32 [64, 257, 512], P(('zg', 'zl'))
- pressure_imag: float32 [64, 257, 512], P(('zg', 'zl'))
The draws below stay inside these ranges and needn't reach their ends.
Inputs may be any that keep to these rules, and one draw needn't show every extreme that they name: brick_live[q, d] counts the live slots of owner d in layer q; the live ones are the first; in every layer some owner has all 16 slots live. `brick_xy`: all slots of one brick layer of one z group (live or not) sit at distinct brick positions.
All inputs are finite; a program needn't handle non-finite values.
Results may differ from the reference program's by a relative error of at most 0.00011.
Values sent between devices are 32-bit elements; how exact they have to be, the bound alone decides.
A program may use at most 64 MiB of HBM per device.

```python
import math
import jax
import jax.numpy as jnp
from jax import lax

PLANE = 512
BRICK = 16
CAP = 16
KX = 257
LAYERS = 1
NZ = 64
BRICKS = 512
N_ZG = 4
N_ZL = 8
DEVICES = 32


def draw_brick_live(key, part):
    first = jax.random.randint(jax.random.fold_in(key, 11), (LAYERS, DEVICES), 1, CAP + 1)
    second = jax.random.randint(jax.random.fold_in(key, 12), (LAYERS, DEVICES), 1, CAP + 1)
    counts = jnp.minimum(first, second)
    busiest = jax.random.randint(jax.random.fold_in(key, 13), (LAYERS, 1), 0, DEVICES)
    owners = jnp.arange(DEVICES, dtype=jnp.int32)[None, :]
    return jnp.where(owners == busiest, CAP, counts).astype(jnp.int32)


def draw_brick_xy(key, part):
    groups = DEVICES // N_ZL
    blocks = PLANE // BRICK
    keys = jax.random.split(jax.random.fold_in(key, 21), groups * LAYERS)
    orders = jax.vmap(lambda single: jax.random.permutation(single, blocks * blocks))(keys)
    chosen = orders[:, :N_ZL * CAP].reshape(groups, LAYERS, N_ZL, CAP)
    chosen = jnp.transpose(chosen, (0, 2, 1, 3)).reshape(-1)
    return jnp.stack([chosen % blocks, chosen // blocks]).astype(jnp.int32)


def block_levels(stream_key, extent, shards, smallest, largest):
    loudness, own = 1.0, jax.random.fold_in(stream_key, 6)
    for axis_at, shards_of in shards:
        draws = jnp.exp(jax.random.uniform(jax.random.fold_in(own, axis_at), (shards_of,), jnp.float32, smallest / len(shards), largest / len(shards)))
        loudness = loudness * jnp.repeat(draws, extent[axis_at] // shards_of).reshape([-1 if axis == axis_at else 1 for axis in range(len(extent))])
    return loudness


def gaussian(stream_key, shape, spread, most, shards=(), kind=jnp.bfloat16):
    loudness = block_levels(stream_key, shape, shards, -0.22, 0.18) if shards else 1.0
    values = jax.random.normal(stream_key, shape, jnp.float32) * spread * loudness
    return jnp.minimum(jnp.maximum(values, -most), most).astype(kind)


def setup_inputs(seed: int = 0) -> dict:
    seeds = jax.random.split(jax.random.key(seed), 4)
    brick_data = gaussian(seeds[0], (BRICKS, BRICK, BRICK * BRICK), 1.0, 6.0, ((0, 32),), jnp.float32)
    brick_xy = draw_brick_xy(jax.random.fold_in(seeds[3], 71), 0)
    brick_live = draw_brick_live(jax.random.fold_in(seeds[3], 71), 0)
    return dict(brick_data=brick_data, brick_xy=brick_xy, brick_live=brick_live)


SCREEN = 0.25

def reverse_bits(values, digits):
    result = jnp.zeros_like(values)
    for digit in range(digits):
        result = result | (values >> digit & 1) << digits - 1 - digit
    return result

def group_slab(inputs):
    group_data, group_slots = inputs
    blocks = PLANE // BRICK
    slab = jnp.zeros((LAYERS * blocks * blocks, BRICK, BRICK * BRICK), group_data.dtype)
    slab = slab.at[group_slots].add(group_data)
    slab = slab.reshape(LAYERS, blocks, blocks, BRICK, BRICK, BRICK)
    slab = jnp.transpose(slab, (0, 3, 1, 4, 2, 5)).reshape(LAYERS * BRICK, PLANE, PLANE)
    return jnp.fft.fft(jnp.fft.rfft(slab, axis=2), axis=1)

def reference(brick_data, brick_xy, brick_live):
    owners = N_ZG * N_ZL
    blocks = PLANE // BRICK
    live = jnp.arange(CAP, dtype=jnp.int32)[None, None, :] < jnp.transpose(brick_live)[:, :, None]
    masked = brick_data.reshape(owners, LAYERS, CAP, BRICK, BRICK * BRICK) * live[:, :, :, None, None].astype(brick_data.dtype)
    layer_ids = jnp.arange(LAYERS, dtype=jnp.int32)[None, :, None]
    places = (brick_xy[1] * blocks + brick_xy[0]).reshape(owners, LAYERS, CAP)
    slots = (layer_ids * (blocks * blocks) + places).reshape(N_ZG, -1).astype(jnp.int32)
    group_data = masked.reshape(N_ZG, N_ZL * LAYERS * CAP, BRICK, BRICK * BRICK)
    spectrum = lax.map(group_slab, (group_data, slots))
    spectrum = jnp.fft.fft(spectrum.reshape(NZ, PLANE, KX), axis=0)
    order = reverse_bits(jnp.arange(NZ, dtype=jnp.int32), NZ.bit_length() - 1)
    spectrum = jnp.transpose(spectrum[order], (0, 2, 1))
    along_z = 4.0 * jnp.sin(jnp.pi * order.astype(jnp.float32) / NZ) ** 2
    along_x = 4.0 * jnp.sin(jnp.pi * jnp.arange(KX, dtype=jnp.float32) / PLANE) ** 2
    along_y = 4.0 * jnp.sin(jnp.pi * jnp.arange(PLANE, dtype=jnp.float32) / PLANE) ** 2
    denom = along_z[:, None, None] + along_x[None, :, None] + along_y[None, None, :] + SCREEN
    factor = -(1.0 / math.sqrt(PLANE * PLANE * NZ)) / denom
    pressure_real = (jnp.real(spectrum) * factor).astype(jnp.float32)
    pressure_imag = (jnp.imag(spectrum) * factor).astype(jnp.float32)
    return (pressure_real, pressure_imag)
```

```python
import functools
import math

import jax
import jax.numpy as jnp
import ml_dtypes
import numpy as np
from jax import lax
from jax.experimental import pallas as pl
from jax.experimental.pallas import tpu as pltpu
from jax.sharding import PartitionSpec as P

PLANE = 512
ZLOC = 2


SCREEN = 0.25
HIGHEST = lax.Precision.HIGHEST
MESH = pl.DeviceIdType.MESH


def swapped(array, axis, distance):
    return lax.ppermute(array, axis, [(i, i ^ 1 << distance) for i in range(lax.axis_size(axis))])


def bit_count(number):
    return number.bit_length() - 1


def reverse_bits(values, digits):
    result = jnp.zeros_like(values)
    for digit in range(digits):
        result = result | (values >> digit & 1) << digits - 1 - digit
    return result


def dft_tables(length, freq_count):
    points = jnp.arange(length, dtype=jnp.int32)[:, None]
    freqs = jnp.arange(freq_count, dtype=jnp.int32)[None, :]
    angles = 2.0 * jnp.pi / length * (points * freqs % length).astype(jnp.float32)
    return (jnp.cos(angles), jnp.sin(angles))


def rotate(values, angles):
    cosine = jnp.cos(angles)
    sine = jnp.sin(angles)
    return (values[0] * cosine + values[1] * sine, values[1] * cosine - values[0] * sine)


def section_angles(z_rows, half, total):
    exponent = z_rows % half * (total // (2 * half))
    return (2.0 * jnp.pi / total * exponent.astype(jnp.float32))[:, None, None]


def combine_pair(mine, theirs, upper, angles):
    summed = (mine[0] + theirs[0], mine[1] + theirs[1])
    turned = rotate((theirs[0] - mine[0], theirs[1] - mine[1]), angles)
    return (jnp.where(upper, turned[0], summed[0]), jnp.where(upper, turned[1], summed[1]))


def local_sections(values, total):
    count = values[0].shape[0]
    shape = values[0].shape
    half = count // 2
    while half >= 1:
        split_real = values[0].reshape((count // (2 * half), 2, half) + shape[1:])
        split_imag = values[1].reshape((count // (2 * half), 2, half) + shape[1:])
        offsets = jnp.arange(half, dtype=jnp.int32) * (total // (2 * half))
        angles = (2.0 * jnp.pi / total * offsets.astype(jnp.float32))[None, :, None, None]
        summed_real = split_real[:, 0] + split_real[:, 1]
        summed_imag = split_imag[:, 0] + split_imag[:, 1]
        turned = rotate(
            (split_real[:, 0] - split_real[:, 1], split_imag[:, 0] - split_imag[:, 1]), angles
        )
        values = (
            jnp.stack([summed_real, turned[0]], axis=1).reshape(shape),
            jnp.stack([summed_imag, turned[1]], axis=1).reshape(shape),
        )
        half = half // 2
    return values


def on_device_wide(brick_data, brick_xy, brick_live):
    layers = brick_live.shape[0]
    capacity = brick_data.shape[0] // layers
    brick = brick_data.shape[1]
    area = brick_data.shape[2]
    zlocal = ZLOC
    per_layer = brick // zlocal
    ngroup = lax.axis_size("zg")
    nplane = lax.axis_size("zl")
    total = zlocal * ngroup * nplane
    width = PLANE
    blocks = width // brick
    kx_count = width // 2 + 1
    group_idx = lax.axis_index("zg")
    plane_idx = lax.axis_index("zl")
    live = (jnp.arange(capacity, dtype=jnp.int32)[None, :] < brick_live).astype(jnp.float32)
    masked = (
        brick_data.reshape(layers, capacity, per_layer, zlocal, area) * live[:, :, None, None, None]
    )
    outgoing = jnp.transpose(masked, (0, 2, 1, 3, 4)).reshape(
        layers * per_layer, capacity, zlocal, area
    )
    block_ids = (
        (brick_xy[1] * blocks + brick_xy[0]).astype(jnp.float32).reshape(layers, 1, capacity)
    )
    block_out = jnp.broadcast_to(block_ids, (layers, per_layer, capacity)).reshape(
        layers * per_layer, capacity
    )
    pieces, places = (
        lax.all_to_all(outgoing, "zl", split_axis=0, concat_axis=0, tiled=True),
        lax.all_to_all(block_out, "zl", split_axis=0, concat_axis=0, tiled=True),
    )
    slot_ids = places.astype(jnp.int32).reshape(-1)
    incoming = jnp.transpose(pieces, (2, 0, 1, 3)).reshape(zlocal, -1, area)
    blockgrid = (
        jnp.zeros((zlocal, blocks * blocks, area), jnp.float32).at[:, slot_ids, :].add(incoming)
    )
    blockgrid = blockgrid.reshape(zlocal, blocks, blocks, brick, brick)
    cos_x, sin_x = dft_tables(width, kx_count)
    cos_x = cos_x.reshape(blocks, brick, kx_count)
    sin_x = sin_x.reshape(blocks, brick, kx_count)
    first_real = jnp.einsum("zabuv,bvk->zkau", blockgrid, cos_x, precision=HIGHEST).reshape(
        zlocal * kx_count, width
    )
    first_imag = -jnp.einsum("zabuv,bvk->zkau", blockgrid, sin_x, precision=HIGHEST).reshape(
        zlocal * kx_count, width
    )
    cos_y, sin_y = dft_tables(width, width)
    second_real = jnp.dot(first_real, cos_y, precision=HIGHEST) + jnp.dot(
        first_imag, sin_y, precision=HIGHEST
    )
    second_imag = jnp.dot(first_imag, cos_y, precision=HIGHEST) - jnp.dot(
        first_real, sin_y, precision=HIGHEST
    )
    values = (
        second_real.reshape(zlocal, kx_count, width),
        second_imag.reshape(zlocal, kx_count, width),
    )
    device = group_idx * nplane + plane_idx
    z_rows = device * zlocal + jnp.arange(zlocal, dtype=jnp.int32)
    gbits = bit_count(ngroup)
    pbits = bit_count(nplane)
    for level in reversed(range(gbits)):
        half = zlocal * nplane * (1 << level)
        theirs = swapped((values[0], values[1]), "zg", level)
        upper = group_idx >> level & 1 == 1
        values = combine_pair(values, theirs, upper, section_angles(z_rows, half, total))
    plane_values = values
    for level in reversed(range(pbits)):
        half = zlocal * (1 << level)
        theirs = swapped((plane_values[0], plane_values[1]), "zl", level)
        upper = plane_idx >> level & 1 == 1
        plane_values = combine_pair(
            plane_values, theirs, upper, section_angles(z_rows, half, total)
        )
    plane_values = local_sections(plane_values, total)
    values = plane_values
    kz_rows = reverse_bits(z_rows, bit_count(total))
    along_z = 4.0 * jnp.sin(jnp.pi * kz_rows.astype(jnp.float32) / total) ** 2
    along_x = 4.0 * jnp.sin(jnp.pi * jnp.arange(kx_count, dtype=jnp.float32) / width) ** 2
    along_y = 4.0 * jnp.sin(jnp.pi * jnp.arange(width, dtype=jnp.float32) / width) ** 2
    denom = along_z[:, None, None] + along_x[None, :, None] + along_y[None, None, :] + SCREEN
    factor = -(1.0 / math.sqrt(width * width * total)) / denom
    return (values[0] * factor, values[1] * factor)


def transposed_blocks(tiles, width):
    tiles = list(tiles)
    block = lax.broadcasted_iota(jnp.int32, tiles[0].shape, tiles[0].ndim - 1) // width
    lanes = tiles[0].shape[-1]
    step = len(tiles) // 2
    while step:
        high = (block & step) != 0
        for i in range(len(tiles)):
            if not i & step:
                low, up = tiles[i], tiles[i + step]
                tiles[i] = jnp.where(high, pltpu.roll(up, step * width, low.ndim - 1), low)
                tiles[i + step] = jnp.where(
                    high, up, pltpu.roll(low, lanes - step * width, low.ndim - 1)
                )
        step //= 2
    return tiles


def exchange_kernel(
    ngroup, nplane, capacity, coef, data, place, out, raw, ready, zsend, zrecv, psend, precv
):
    group, plane = lax.axis_index("zg"), lax.axis_index("zl")
    quads = capacity // 4
    depth = data.shape[0] // quads
    barrier = pltpu.get_barrier_semaphore()

    def greet(g, p):
        pl.semaphore_signal(barrier, inc=1, device_id=(g, p), device_id_type=MESH)

    for k in range(1, nplane):
        greet(group, lax.rem(plane + k, nplane))
    pl.when(group > 0)(lambda: greet(group - 1, plane))
    pl.when(group < ngroup - 1)(lambda: greet(group + 1, plane))
    ends = jnp.where(group > 0, 1, 0) + jnp.where(group < ngroup - 1, 1, 0)
    pl.semaphore_wait(barrier, nplane - 1 + ends)

    def along(side, t):
        chunk = jnp.where(side == 0, group - t, group + t)
        target = jnp.where(side == 0, group + 1, group - 1)
        inside = (chunk >= 0) & (chunk < ngroup) & (target >= 0) & (target < ngroup)
        safe = jnp.clip(chunk, 0, ngroup - 1)
        copy = pltpu.make_async_remote_copy(
            src_ref=raw.at[safe],
            dst_ref=raw.at[safe],
            send_sem=zsend.at[side, t],
            recv_sem=zrecv.at[side, t],
            device_id=(jnp.clip(target, 0, ngroup - 1), plane),
            device_id_type=MESH,
        )
        return inside, copy

    def to_peer(chunk, k):
        return pltpu.make_async_remote_copy(
            src_ref=ready.at[chunk, k],
            dst_ref=out.at[plane, chunk],
            send_sem=psend.at[chunk, k],
            recv_sem=precv.at[chunk, k],
            device_id=(group, lax.rem(plane + k, nplane)),
            device_id_type=MESH,
        )

    def sums(chunk, peer, target):
        row = chunk * nplane + peer
        real = [coef[row, 2 * z] for z in range(depth)]
        imag = [coef[row, 2 * z + 1] for z in range(depth)]
        for quad in range(quads):
            parts = []
            for table in (real, imag):
                for parity in range(2):
                    total = None
                    for z in range(parity, depth, 2):
                        term = raw[chunk, quad * depth + z] * table[z]
                        total = term if total is None else total + term
                    parts.append(total)
            tiles = (parts[0] + parts[1], parts[2] + parts[3], parts[0] - parts[1], parts[2] - parts[3])
            for i, tile in enumerate(transposed_blocks(tiles, 32)):
                target[quad * 4 + i] = tile
        target[capacity] = raw[chunk, quads * depth]

    def share(chunk):
        def one(k, carry):
            sums(chunk, lax.rem(plane + k, nplane), ready.at[chunk, k])
            to_peer(chunk, k).start()
            return carry

        lax.fori_loop(1, nplane, one, 0)
        sums(chunk, plane, out.at[plane, chunk])

    raw[group, : quads * depth] = data[...]
    raw[group, quads * depth] = place[...]
    for side in range(2):
        inside, copy = along(side, 0)
        pl.when(inside)(copy.start)
    share(group)

    def arrival(i, carry):
        t, side = i // 2, lax.rem(i, 2)
        chunk = jnp.where(side == 0, group - 1 - t, group + 1 + t)

        @pl.when((chunk >= 0) & (chunk < ngroup))
        def _():
            safe = jnp.clip(chunk, 0, ngroup - 1)
            pltpu.make_async_remote_copy(
                src_ref=raw.at[safe],
                dst_ref=raw.at[safe],
                send_sem=zsend.at[side, t],
                recv_sem=zrecv.at[side, t],
                device_id=(group, plane),
                device_id_type=MESH,
            ).wait_recv()

            @pl.when(t < ngroup - 2)
            def _():
                inside, copy = along(side, jnp.minimum(t + 1, ngroup - 2))
                pl.when(inside)(copy.start)

            share(safe)

        return carry

    lax.fori_loop(0, 2 * (ngroup - 1), arrival, 0)

    for side in range(2):
        for t in range(ngroup - 1):
            inside, copy = along(side, t)
            pl.when(inside)(copy.wait_send)

    def finish(i, carry):
        copy = to_peer(i // (nplane - 1), 1 + lax.rem(i, nplane - 1))
        copy.wait_send()
        copy.wait_recv()
        return carry

    lax.fori_loop(0, ngroup * (nplane - 1), finish, 0)


def split(values):
    high = values.astype(jnp.bfloat16)
    return high, (values - high.astype(jnp.float32)).astype(jnp.bfloat16)


def dot3(left, right, dims):
    def one(a, b):
        return lax.dot_general(a, b, (dims, ((), ())), preferred_element_type=jnp.float32)

    return one(left[0], right[0]) + (one(left[0], right[1]) + one(left[1], right[0]))


def spectrum_kernel(
    nplane, ngroup, capacity, blocks, evens, scale,
    places, along_z, bricks, tx_even, tx_odd, ty, along_x, along_y, out_real, out_imag, grid, rows, woven,
):
    step = pl.program_id(0)
    half = rows.shape[-1] // 2

    @pl.when(step == 0)
    def _():
        def clear(i, carry):
            grid[pl.ds(i * 32, 32)] = jnp.zeros((32,) + grid.shape[1:], jnp.float32)
            return carry

        lax.fori_loop(0, grid.shape[0] // 32, clear, 0)

        def place(i, carry):
            source, chunk = i // ngroup, lax.rem(i, ngroup)
            ids = [places[i * capacity + c] for c in range(capacity)]
            values = [grid[ids[c]] + bricks[source, chunk, c] for c in range(capacity)]
            for c in range(capacity):
                grid[ids[c]] = values[c]
            return carry

        lax.fori_loop(0, nplane * ngroup, place, 0)

        def arrange(yb, carry):
            for h in range(2):
                first = transposed_blocks([grid[yb * blocks + h * 8 + i] for i in range(8)], 16)
                second = transposed_blocks(
                    [grid[yb * blocks + (h + 2) * 8 + i] for i in range(8)], 16
                )
                for j in range(8):
                    kz, ri, parity = j // 4, j // 2 % 2, j % 2
                    at = (pl.ds(pl.multiple_of(yb * 8, 8), 8), pl.ds(ri * half + h * 128, 128))
                    rows[(0, kz, parity) + at] = first[j] + second[j]
                    rows[(1, kz, parity) + at] = first[j] - second[j]
            return carry

        lax.fori_loop(0, blocks, arrange, 0)

    for odd in range(2):
        table = tx_odd if odd else tx_even
        count = evens[odd]
        padded = table.shape[1] // 2
        products = []
        for parity in range(2):
            field = split(rows[odd, step, parity])
            first = dot3((table[0], table[1]), field, ((1,), (1,)))
            first = jnp.concatenate([first[:padded], first[padded:]], axis=1)
            products.append(dot3(split(first), (ty[parity, 0], ty[parity, 1]), ((1,), (0,))))
        total, rest = products[0] + products[1], products[0] - products[1]
        axis_x = along_x[odd, :padded, :1]
        denom = along_z[step] + axis_x + along_y[...] + SCREEN
        factor = scale / denom
        width = total.shape[1] // 2
        for part, at in ((0, 0), (1, width)):
            value = jnp.concatenate([total[:, at : at + width], rest[:, at : at + width]], axis=1)
            value = value * factor
            for tile in range(value.shape[1] // 128):
                woven[part, tile, pl.ds(odd, count, stride=2), :] = value[
                    :count, tile * 128 : tile * 128 + 128
                ]
    for part, out in ((0, out_real), (1, out_imag)):
        for tile in range(out.shape[2] // 128):
            out[0, :, tile * 128 : tile * 128 + 128] = woven[part, tile, : out.shape[1]]


def parted(table):
    high = table.astype(ml_dtypes.bfloat16)
    low = (table - high.astype(np.float64)).astype(ml_dtypes.bfloat16)
    return np.stack([high, low])


def x_tables(width):
    tables = []
    for odd in range(2):
        count = width // 4 + 1 - odd
        padded = -(-count // 8) * 8
        kx = 2 * np.arange(padded)[:, None] + odd
        angles = 2 * np.pi / width * (kx * np.arange(width // 2)[None, :] % width)
        cosine, sine = np.cos(angles), np.sin(angles)
        tables.append(parted(np.block([[cosine, sine], [-sine, cosine]])))
    return tables


def y_tables(width):
    tables = []
    for parity in range(2):
        y = 2 * np.arange(width // 2)[:, None] + parity
        angles = 2 * np.pi / width * (y * np.arange(width // 2)[None, :] % width)
        cosine, sine = np.cos(angles), np.sin(angles)
        tables.append(parted(np.block([[cosine, -sine], [sine, cosine]])))
    return np.stack(tables)


def kz_of(rows, total):
    digits = bit_count(total)
    return sum((rows >> d & 1) << digits - 1 - d for d in range(digits))


def on_device_once(brick_data, brick_xy, brick_live):
    capacity, brick, area = brick_data.shape
    ngroup, nplane = lax.axis_size("zg"), lax.axis_size("zl")
    total = ZLOC * ngroup * nplane
    width = PLANE
    blocks = width // brick
    group, plane = lax.axis_index("zg"), lax.axis_index("zl")
    quads = capacity // 4

    kz = kz_of(np.arange(total), total).reshape(ngroup, nplane, ZLOC)
    z = np.arange(ngroup * brick).reshape(ngroup, 1, brick)
    angles = 2 * np.pi / total * (kz[:, None, :, None, 0] * z[None] % total)
    coef = np.stack([np.cos(angles), -np.sin(angles)], axis=-1)
    coef = coef.reshape(ngroup, ngroup * nplane, 2 * brick).astype(np.float32)
    coef = lax.dynamic_index_in_dim(jnp.asarray(coef), group, 0, keepdims=False)
    along_z = (4 * np.sin(np.pi * kz / total) ** 2).reshape(-1, ZLOC).astype(np.float32)
    along_z = lax.dynamic_index_in_dim(
        jnp.asarray(along_z), group * nplane + plane, 0, keepdims=False
    )

    live = jnp.arange(capacity, dtype=jnp.int32)[:, None, None] < brick_live[0, 0]
    data = jnp.where(live, brick_data, 0.0).reshape(quads, 4, brick, 8, 32)
    data = jnp.transpose(data, (0, 2, 3, 1, 4)).reshape(quads * brick, 8, 128)
    place = (brick_xy[1] * blocks + brick_xy[0]).astype(jnp.float32)
    place = jnp.pad(place[None, :], ((0, 7), (0, 128 - capacity)))

    vmem = pl.BlockSpec(memory_space=pltpu.VMEM)
    smem = pl.BlockSpec(memory_space=pltpu.SMEM)
    arrived = pl.pallas_call(
        functools.partial(exchange_kernel, ngroup, nplane, capacity),
        out_shape=jax.ShapeDtypeStruct((nplane, ngroup, capacity + 1, 8, 128), jnp.float32),
        in_specs=[smem, vmem, vmem],
        out_specs=vmem,
        scratch_shapes=[
            pltpu.VMEM((ngroup, quads * brick + 1, 8, 128), jnp.float32),
            pltpu.VMEM((ngroup, nplane, capacity + 1, 8, 128), jnp.float32),
            pltpu.SemaphoreType.DMA((2, ngroup - 1)),
            pltpu.SemaphoreType.DMA((2, ngroup - 1)),
            pltpu.SemaphoreType.DMA((ngroup, nplane)),
            pltpu.SemaphoreType.DMA((ngroup, nplane)),
        ],
        compiler_params=pltpu.CompilerParams(
            collective_id=0, has_side_effects=True, vmem_limit_bytes=32 * 2**20
        ),
        name="exchange",
    )(coef, data, place)

    places = arrived[:, :, capacity, 0, :capacity].astype(jnp.int32).reshape(-1)
    tx_even, tx_odd = x_tables(width)
    evens = (width // 4 + 1, width // 4)
    axis = 4 * np.sin(np.pi * np.arange(width) / width) ** 2
    along_x = np.zeros((2, tx_even.shape[1] // 2, 128), np.float32)
    for odd in range(2):
        along_x[odd, : evens[odd]] = axis[odd : width // 2 + 1 : 2][:, None]
    along_y = axis[None, :].astype(np.float32)

    def whole(array):
        return pl.BlockSpec(array.shape, lambda i, n=array.ndim: (0,) * n)

    tables = [jnp.asarray(t) for t in (tx_even, tx_odd, y_tables(width), along_x, along_y)]
    out = jax.ShapeDtypeStruct((ZLOC, width // 2 + 1, width), jnp.float32)
    out_spec = pl.BlockSpec((1, width // 2 + 1, width), lambda i: (i, 0, 0))
    scale = -1.0 / math.sqrt(width * width * total)
    return pl.pallas_call(
        functools.partial(spectrum_kernel, nplane, ngroup, capacity, blocks, evens, scale),
        grid=(ZLOC,),
        out_shape=(out, out),
        in_specs=[smem, smem, whole(arrived)] + [whole(t) for t in tables],
        out_specs=(out_spec, out_spec),
        scratch_shapes=[
            pltpu.VMEM((blocks * blocks, 8, 128), jnp.float32),
            pltpu.VMEM((2, ZLOC, 2, width // 2, width), jnp.float32),
            pltpu.VMEM((2, width // 128, width // 2 + 8, 128), jnp.float32),
        ],
        compiler_params=pltpu.CompilerParams(vmem_limit_bytes=48 * 2**20),
        name="spectrum",
    )(places, along_z, arrived, *tables)


def on_device(brick_data, brick_xy, brick_live):
    layers = brick_live.shape[0]
    slots, brick, area = brick_data.shape
    nplane, ngroup = lax.axis_size("zl"), lax.axis_size("zg")
    one_layer = layers == 1 and nplane * ZLOC == brick and brick == 16 and slots == 16
    fits = slots * nplane * ngroup * area * 2 * ZLOC * 4 <= 4 * 2**20
    if one_layer and fits and ngroup > 1:
        return on_device_once(brick_data, brick_xy, brick_live)
    return on_device_wide(brick_data, brick_xy, brick_live)


def solution(mesh):
    in_specs = (P(("zg", "zl"), None, None), P(None, ("zg", "zl")), P(None, ("zg", "zl")))
    out_specs = (P(("zg", "zl"), None, None), P(("zg", "zl"), None, None))
    return jax.shard_map(
        on_device, mesh=mesh, in_specs=in_specs, out_specs=out_specs, check_vma=False
    )
```

```python
import functools
import math

import jax
import jax.numpy as jnp
import ml_dtypes
import numpy as np
from jax import lax
from jax.experimental import pallas as pl
from jax.experimental.pallas import tpu as pltpu
from jax.sharding import PartitionSpec as P

PLANE = 512
ZLOC = 2


SCREEN = 0.25
HIGHEST = lax.Precision.HIGHEST
MESH = pl.DeviceIdType.MESH


def swapped(array, axis, distance):
    return lax.ppermute(array, axis, [(i, i ^ 1 << distance) for i in range(lax.axis_size(axis))])


def bit_count(number):
    return number.bit_length() - 1


def reverse_bits(values, digits):
    result = jnp.zeros_like(values)
    for digit in range(digits):
        result = result | (values >> digit & 1) << digits - 1 - digit
    return result


def dft_tables(length, freq_count):
    points = jnp.arange(length, dtype=jnp.int32)[:, None]
    freqs = jnp.arange(freq_count, dtype=jnp.int32)[None, :]
    angles = 2.0 * jnp.pi / length * (points * freqs % length).astype(jnp.float32)
    return (jnp.cos(angles), jnp.sin(angles))


def rotate(values, angles):
    cosine = jnp.cos(angles)
    sine = jnp.sin(angles)
    return (values[0] * cosine + values[1] * sine, values[1] * cosine - values[0] * sine)


def section_angles(z_rows, half, total):
    exponent = z_rows % half * (total // (2 * half))
    return (2.0 * jnp.pi / total * exponent.astype(jnp.float32))[:, None, None]


def combine_pair(mine, theirs, upper, angles):
    summed = (mine[0] + theirs[0], mine[1] + theirs[1])
    turned = rotate((theirs[0] - mine[0], theirs[1] - mine[1]), angles)
    return (jnp.where(upper, turned[0], summed[0]), jnp.where(upper, turned[1], summed[1]))


def local_sections(values, total):
    count = values[0].shape[0]
    shape = values[0].shape
    half = count // 2
    while half >= 1:
        split_real = values[0].reshape((count // (2 * half), 2, half) + shape[1:])
        split_imag = values[1].reshape((count // (2 * half), 2, half) + shape[1:])
        offsets = jnp.arange(half, dtype=jnp.int32) * (total // (2 * half))
        angles = (2.0 * jnp.pi / total * offsets.astype(jnp.float32))[None, :, None, None]
        summed_real = split_real[:, 0] + split_real[:, 1]
        summed_imag = split_imag[:, 0] + split_imag[:, 1]
        turned = rotate(
            (split_real[:, 0] - split_real[:, 1], split_imag[:, 0] - split_imag[:, 1]), angles
        )
        values = (
            jnp.stack([summed_real, turned[0]], axis=1).reshape(shape),
            jnp.stack([summed_imag, turned[1]], axis=1).reshape(shape),
        )
        half = half // 2
    return values


def on_device_wide(brick_data, brick_xy, brick_live):
    layers = brick_live.shape[0]
    capacity = brick_data.shape[0] // layers
    brick = brick_data.shape[1]
    area = brick_data.shape[2]
    zlocal = ZLOC
    per_layer = brick // zlocal
    ngroup = lax.axis_size("zg")
    nplane = lax.axis_size("zl")
    total = zlocal * ngroup * nplane
    width = PLANE
    blocks = width // brick
    kx_count = width // 2 + 1
    group_idx = lax.axis_index("zg")
    plane_idx = lax.axis_index("zl")
    live = (jnp.arange(capacity, dtype=jnp.int32)[None, :] < brick_live).astype(jnp.float32)
    masked = (
        brick_data.reshape(layers, capacity, per_layer, zlocal, area) * live[:, :, None, None, None]
    )
    outgoing = jnp.transpose(masked, (0, 2, 1, 3, 4)).reshape(
        layers * per_layer, capacity, zlocal, area
    )
    block_ids = (
        (brick_xy[1] * blocks + brick_xy[0]).astype(jnp.float32).reshape(layers, 1, capacity)
    )
    block_out = jnp.broadcast_to(block_ids, (layers, per_layer, capacity)).reshape(
        layers * per_layer, capacity
    )
    pieces, places = (
        lax.all_to_all(outgoing, "zl", split_axis=0, concat_axis=0, tiled=True),
        lax.all_to_all(block_out, "zl", split_axis=0, concat_axis=0, tiled=True),
    )
    slot_ids = places.astype(jnp.int32).reshape(-1)
    incoming = jnp.transpose(pieces, (2, 0, 1, 3)).reshape(zlocal, -1, area)
    blockgrid = (
        jnp.zeros((zlocal, blocks * blocks, area), jnp.float32).at[:, slot_ids, :].add(incoming)
    )
    blockgrid = blockgrid.reshape(zlocal, blocks, blocks, brick, brick)
    cos_x, sin_x = dft_tables(width, kx_count)
    cos_x = cos_x.reshape(blocks, brick, kx_count)
    sin_x = sin_x.reshape(blocks, brick, kx_count)
    first_real = jnp.einsum("zabuv,bvk->zkau", blockgrid, cos_x, precision=HIGHEST).reshape(
        zlocal * kx_count, width
    )
    first_imag = -jnp.einsum("zabuv,bvk->zkau", blockgrid, sin_x, precision=HIGHEST).reshape(
        zlocal * kx_count, width
    )
    cos_y, sin_y = dft_tables(width, width)
    second_real = jnp.dot(first_real, cos_y, precision=HIGHEST) + jnp.dot(
        first_imag, sin_y, precision=HIGHEST
    )
    second_imag = jnp.dot(first_imag, cos_y, precision=HIGHEST) - jnp.dot(
        first_real, sin_y, precision=HIGHEST
    )
    values = (
        second_real.reshape(zlocal, kx_count, width),
        second_imag.reshape(zlocal, kx_count, width),
    )
    device = group_idx * nplane + plane_idx
    z_rows = device * zlocal + jnp.arange(zlocal, dtype=jnp.int32)
    gbits = bit_count(ngroup)
    pbits = bit_count(nplane)
    for level in reversed(range(gbits)):
        half = zlocal * nplane * (1 << level)
        theirs = swapped((values[0], values[1]), "zg", level)
        upper = group_idx >> level & 1 == 1
        values = combine_pair(values, theirs, upper, section_angles(z_rows, half, total))
    plane_values = values
    for level in reversed(range(pbits)):
        half = zlocal * (1 << level)
        theirs = swapped((plane_values[0], plane_values[1]), "zl", level)
        upper = plane_idx >> level & 1 == 1
        plane_values = combine_pair(
            plane_values, theirs, upper, section_angles(z_rows, half, total)
        )
    plane_values = local_sections(plane_values, total)
    values = plane_values
    kz_rows = reverse_bits(z_rows, bit_count(total))
    along_z = 4.0 * jnp.sin(jnp.pi * kz_rows.astype(jnp.float32) / total) ** 2
    along_x = 4.0 * jnp.sin(jnp.pi * jnp.arange(kx_count, dtype=jnp.float32) / width) ** 2
    along_y = 4.0 * jnp.sin(jnp.pi * jnp.arange(width, dtype=jnp.float32) / width) ** 2
    denom = along_z[:, None, None] + along_x[None, :, None] + along_y[None, None, :] + SCREEN
    factor = -(1.0 / math.sqrt(width * width * total)) / denom
    return (values[0] * factor, values[1] * factor)


def kz_of(row, total):
    digits = bit_count(total)
    return sum(
        lax.rem(lax.div(row, jnp.int32(1 << d)), jnp.int32(2)) * (1 << digits - 1 - d)
        for d in range(digits)
    )


def transposed_blocks(tiles, width):
    tiles = list(tiles)
    block = lax.broadcasted_iota(jnp.int32, tiles[0].shape, tiles[0].ndim - 1) // width
    lanes = tiles[0].shape[-1]
    step = len(tiles) // 2
    while step:
        high = (block & step) != 0
        for i in range(len(tiles)):
            if not i & step:
                low, up = tiles[i], tiles[i + step]
                tiles[i] = jnp.where(high, pltpu.roll(up, step * width, low.ndim - 1), low)
                tiles[i + step] = jnp.where(
                    high, up, pltpu.roll(low, lanes - step * width, low.ndim - 1)
                )
        step //= 2
    return tiles


def exchange_kernel(
    ngroup, nplane, capacity, blocks, cosines, live, data, xy, out, raw, ready, zsend, zrecv, psend, precv
):
    group, plane = lax.axis_index("zg"), lax.axis_index("zl")
    quads = capacity // 4
    depth = data.shape[1]
    total = cosines.shape[0]
    barrier = pltpu.get_barrier_semaphore()

    def greet(g, p):
        pl.semaphore_signal(barrier, inc=1, device_id=(g, p), device_id_type=MESH)

    for k in range(1, nplane):
        greet(group, lax.rem(plane + k, nplane))
    pl.when(group > 0)(lambda: greet(group - 1, plane))
    pl.when(group < ngroup - 1)(lambda: greet(group + 1, plane))
    ends = jnp.where(group > 0, 1, 0) + jnp.where(group < ngroup - 1, 1, 0)
    pl.semaphore_wait(barrier, nplane - 1 + ends)

    def along(side, t):
        chunk = jnp.where(side == 0, group - t, group + t)
        target = jnp.where(side == 0, group + 1, group - 1)
        inside = (chunk >= 0) & (chunk < ngroup) & (target >= 0) & (target < ngroup)
        safe = jnp.clip(chunk, 0, ngroup - 1)
        copy = pltpu.make_async_remote_copy(
            src_ref=raw.at[safe],
            dst_ref=raw.at[safe],
            send_sem=zsend.at[side, t],
            recv_sem=zrecv.at[side, t],
            device_id=(jnp.clip(target, 0, ngroup - 1), plane),
            device_id_type=MESH,
        )
        return inside, copy

    def to_peer(chunk, k):
        return pltpu.make_async_remote_copy(
            src_ref=ready.at[chunk, k],
            dst_ref=out.at[plane, chunk],
            send_sem=psend.at[chunk, k],
            recv_sem=precv.at[chunk, k],
            device_id=(group, lax.rem(plane + k, nplane)),
            device_id_type=MESH,
        )

    def sums(chunk, peer, target):
        kz = kz_of((group * nplane + peer) * ZLOC, total)
        turns = [lax.rem(kz * (chunk * depth + z), total) for z in range(depth)]
        real = [cosines[turn] for turn in turns]
        imag = [cosines[lax.rem(turn + total // 4, total)] for turn in turns]
        for quad in range(quads):
            parts = []
            for table in (real, imag):
                for parity in range(2):
                    summed = None
                    for z in range(parity, depth, 2):
                        term = raw[chunk, pl.ds((quad * depth + z) * 8, 8)] * table[z]
                        summed = term if summed is None else summed + term
                    parts.append(summed)
            tiles = (parts[0] + parts[1], parts[2] + parts[3], parts[0] - parts[1], parts[2] - parts[3])
            for i, tile in enumerate(transposed_blocks(tiles, 32)):
                target[quad * 4 + i] = tile
        target[capacity] = raw[chunk, pl.ds(quads * depth * 8, 8)]

    def share(chunk):
        def one(k, carry):
            sums(chunk, lax.rem(plane + k, nplane), ready.at[chunk, k])
            to_peer(chunk, k).start()
            return carry

        lax.fori_loop(1, nplane, one, 0)
        sums(chunk, plane, out.at[plane, chunk])

    for quad in range(quads):
        for z in range(0, depth, 8):
            for half in range(2):
                tiles = []
                for slot in range(quad * 4, quad * 4 + 4):
                    keep = jnp.where(slot < live[0, 0], 1.0, 0.0)
                    tiles.append(data[slot, z : z + 8, half * 128 : half * 128 + 128] * keep)
                for i, tile in enumerate(transposed_blocks(tiles, 32)):
                    row = (quad * depth + z) * 8 + half * 4 + i
                    raw[group, pl.ds(row, 8, stride=8), :] = tile
    place = (xy[1:2, :] * blocks + xy[0:1, :]).astype(jnp.float32)
    place = jnp.concatenate([place, jnp.zeros((1, 128 - capacity), jnp.float32)], axis=1)
    raw[group, pl.ds(quads * depth * 8, 8)] = jnp.broadcast_to(place, (8, 128))
    for side in range(2):
        inside, copy = along(side, 0)
        pl.when(inside)(copy.start)
    share(group)

    def arrival(i, carry):
        t, side = i // 2, lax.rem(i, 2)
        chunk = jnp.where(side == 0, group - 1 - t, group + 1 + t)

        @pl.when((chunk >= 0) & (chunk < ngroup))
        def _():
            safe = jnp.clip(chunk, 0, ngroup - 1)
            pltpu.make_async_remote_copy(
                src_ref=raw.at[safe],
                dst_ref=raw.at[safe],
                send_sem=zsend.at[side, t],
                recv_sem=zrecv.at[side, t],
                device_id=(group, plane),
                device_id_type=MESH,
            ).wait_recv()

            @pl.when(t < ngroup - 2)
            def _():
                inside, copy = along(side, jnp.minimum(t + 1, ngroup - 2))
                pl.when(inside)(copy.start)

            share(safe)

        return carry

    lax.fori_loop(0, 2 * (ngroup - 1), arrival, 0)

    for side in range(2):
        for t in range(ngroup - 1):
            inside, copy = along(side, t)
            pl.when(inside)(copy.wait_send)

    def finish(i, carry):
        copy = to_peer(i // (nplane - 1), 1 + lax.rem(i, nplane - 1))
        copy.wait_send()
        copy.wait_recv()
        return carry

    lax.fori_loop(0, ngroup * (nplane - 1), finish, 0)


def split(values):
    high = values.astype(jnp.bfloat16)
    return high, (values - high.astype(jnp.float32)).astype(jnp.bfloat16)


def spectrum_kernel(
    nplane, ngroup, capacity, blocks, evens, scale,
    places, along_z, bricks, tx_even, tx_odd, ty, along_x, along_y, out_real, out_imag,
    grid, rows, lines,
):
    half = rows.shape[-1] // 2
    width = rows.shape[-1]
    device = lax.axis_index("zg") * nplane + lax.axis_index("zl")
    total = along_z.shape[0]

    def clear(i, carry):
        grid[pl.ds(i * 32, 32)] = jnp.zeros((32,) + grid.shape[1:], jnp.float32)
        return carry

    lax.fori_loop(0, grid.shape[0] // 32, clear, 0)

    def place(i, carry):
        source, chunk = i // ngroup, lax.rem(i, ngroup)
        ids = [places[i * capacity + c] for c in range(capacity)]
        values = [grid[ids[c]] + bricks[source, chunk, c] for c in range(capacity)]
        for c in range(capacity):
            grid[ids[c]] = values[c]
        return carry

    lax.fori_loop(0, nplane * ngroup, place, 0)

    def arrange(yb, carry):
        for h in range(2):
            first = transposed_blocks([grid[yb * blocks + h * 8 + i] for i in range(8)], 16)
            second = transposed_blocks([grid[yb * blocks + (h + 2) * 8 + i] for i in range(8)], 16)
            for j in range(8):
                kz, ri, parity = j // 4, j // 2 % 2, j % 2
                at = (pl.ds(pl.multiple_of(yb * 8, 8), 8), pl.ds(ri * half + h * 128, 128))
                rows[(0, kz, parity) + at] = first[j] + second[j]
                rows[(1, kz, parity) + at] = first[j] - second[j]
        return carry

    lax.fori_loop(0, blocks, arrange, 0)

    def product(a, b, dims):
        return lax.dot_general(a, b, (dims, ((), ())), preferred_element_type=jnp.float32)

    padded = along_x.shape[1]
    for parity in range(2):
        for odd in range(2):
            table = tx_odd if odd else tx_even
            count = table.shape[0] // 2
            for kz in range(ZLOC):
                high, low = split(rows[odd, kz, parity])
                both = product(table[...], high, ((1,), (1,)))
                first = both[:count] + (both[count:] + product(table[:count], low, ((1,), (1,))))
                at = pl.ds((odd * ZLOC + kz) * padded, padded)
                lines[parity, at, :half] = first[:padded]
                lines[parity, at, half:] = first[padded:]

    results = []
    for parity in range(2):
        high, low = split(lines[parity])
        count = high.shape[0]
        both = product(jnp.concatenate([high, low], axis=0), ty[parity, 0], ((1,), (0,)))
        results.append(both[:count] + (both[count:] + product(high, ty[parity, 1], ((1,), (0,)))))
    lines[0] = results[0] + results[1]
    lines[1] = results[0] - results[1]

    tiles = width // 128
    for odd in range(2):
        for kz in range(ZLOC):
            at = pl.ds((odd * ZLOC + kz) * padded, padded)
            for tile in range(tiles):
                lanes = pl.ds(tile * 128, 128)
                denom = along_z[kz_of(device * ZLOC + kz, total)] + along_x[odd] + along_y[:, lanes] + SCREEN
                factor = scale / denom
                sign, lane = tile // (tiles // 2), tile % (tiles // 2) * 128
                for out, start in ((out_real, 0), (out_imag, half)):
                    value = lines[sign, at, pl.ds(start + lane, 128)] * factor
                    row = (odd * tiles + tile) * ZLOC + kz
                    out[pl.ds(row, evens[odd], stride=2 * tiles * ZLOC), :] = value[: evens[odd]]


def parted(table):
    high = table.astype(ml_dtypes.bfloat16)
    low = (table - high.astype(np.float64)).astype(ml_dtypes.bfloat16)
    return high, low


def x_tables(width):
    tables = []
    for odd in range(2):
        padded = -(-(width // 4 + 1) // 8) * 8
        kx = 2 * np.arange(padded)[:, None] + odd
        angles = 2 * np.pi / width * (kx * np.arange(width // 2)[None, :] % width)
        cosine, sine = np.cos(angles), np.sin(angles)
        tables.append(np.concatenate(parted(np.block([[cosine, sine], [-sine, cosine]]))))
    return tables


def y_tables(width):
    tables = []
    for parity in range(2):
        y = 2 * np.arange(width // 2)[:, None] + parity
        angles = 2 * np.pi / width * (y * np.arange(width // 2)[None, :] % width)
        cosine, sine = np.cos(angles), np.sin(angles)
        tables.append(np.stack(parted(np.block([[cosine, -sine], [sine, cosine]]))))
    return np.stack(tables)


def on_device_once(brick_data, brick_xy, brick_live):
    capacity, brick, area = brick_data.shape
    ngroup, nplane = lax.axis_size("zg"), lax.axis_size("zl")
    total = ZLOC * ngroup * nplane
    width = PLANE
    blocks = width // brick
    quads = capacity // 4
    turns = np.arange(total) / total
    cosines = jnp.asarray(np.cos(2 * np.pi * turns).astype(np.float32))
    along_z = jnp.asarray((4 * np.sin(np.pi * turns) ** 2).astype(np.float32))

    vmem = pl.BlockSpec(memory_space=pltpu.VMEM)
    smem = pl.BlockSpec(memory_space=pltpu.SMEM)
    arrived = pl.pallas_call(
        functools.partial(exchange_kernel, ngroup, nplane, capacity, blocks),
        out_shape=jax.ShapeDtypeStruct((nplane, ngroup, capacity + 1, 8, 128), jnp.float32),
        in_specs=[smem, smem, vmem, vmem],
        out_specs=vmem,
        scratch_shapes=[
            pltpu.VMEM((ngroup, (quads * brick + 1) * 8, 128), jnp.float32),
            pltpu.VMEM((ngroup, nplane, capacity + 1, 8, 128), jnp.float32),
            pltpu.SemaphoreType.DMA((2, ngroup - 1)),
            pltpu.SemaphoreType.DMA((2, ngroup - 1)),
            pltpu.SemaphoreType.DMA((ngroup, nplane)),
            pltpu.SemaphoreType.DMA((ngroup, nplane)),
        ],
        compiler_params=pltpu.CompilerParams(
            collective_id=0, has_side_effects=True, vmem_limit_bytes=12 * 2**20
        ),
        name="exchange",
    )(cosines, brick_live, brick_data, brick_xy)

    places = arrived[:, :, capacity, 0, :capacity].astype(jnp.int32).reshape(-1)
    tx_even, tx_odd = x_tables(width)
    evens = (width // 4 + 1, width // 4)
    axis = 4 * np.sin(np.pi * np.arange(width) / width) ** 2
    along_x = np.zeros((2, tx_even.shape[0] // 4, 128), np.float32)
    for odd in range(2):
        along_x[odd, : evens[odd]] = axis[odd : width // 2 + 1 : 2][:, None]
    along_y = axis[None, :].astype(np.float32)

    tables = [jnp.asarray(t) for t in (tx_even, tx_odd, y_tables(width), along_x, along_y)]
    kx_count = width // 2 + 1
    out = jax.ShapeDtypeStruct((kx_count * width // 128 * ZLOC, 128), jnp.float32)
    scale = -1.0 / math.sqrt(width * width * total)
    results = pl.pallas_call(
        functools.partial(spectrum_kernel, nplane, ngroup, capacity, blocks, evens, scale),
        out_shape=(out, out),
        in_specs=[smem, smem] + [vmem] * 6,
        out_specs=(vmem, vmem),
        scratch_shapes=[
            pltpu.VMEM((blocks * blocks, 8, 128), jnp.float32),
            pltpu.VMEM((2, ZLOC, 2, width // 2, width), jnp.float32),
            pltpu.VMEM((2, 2 * ZLOC * along_x.shape[1], width), jnp.float32),
        ],
        compiler_params=pltpu.CompilerParams(vmem_limit_bytes=32 * 2**20),
        name="spectrum",
    )(places, along_z, arrived, *tables)

    def ordered(result):
        result = result.reshape(kx_count, width // 128, ZLOC, 128)
        return jnp.transpose(result, (2, 0, 1, 3)).reshape(ZLOC, kx_count, width)

    return tuple(ordered(result) for result in results)


def on_device(brick_data, brick_xy, brick_live):
    layers = brick_live.shape[0]
    slots, brick, area = brick_data.shape
    nplane, ngroup = lax.axis_size("zl"), lax.axis_size("zg")
    one_layer = layers == 1 and nplane * ZLOC == brick and brick == 16 and slots == 16
    fits = slots * nplane * ngroup * area * 2 * ZLOC * 4 <= 4 * 2**20
    if one_layer and fits and ngroup > 1:
        return on_device_once(brick_data, brick_xy, brick_live)
    return on_device_wide(brick_data, brick_xy, brick_live)


def solution(mesh):
    in_specs = (P(("zg", "zl"), None, None), P(None, ("zg", "zl")), P(None, ("zg", "zl")))
    out_specs = (P(("zg", "zl"), None, None), P(("zg", "zl"), None, None))
    return jax.shard_map(
        on_device, mesh=mesh, in_specs=in_specs, out_specs=out_specs, check_vma=False
    )
```

```python
import functools
import math

import jax
import jax.numpy as jnp
import ml_dtypes
import numpy as np
from jax import lax
from jax.experimental import pallas as pl
from jax.experimental.pallas import tpu as pltpu
from jax.sharding import PartitionSpec as P

PLANE = 512
ZLOC = 2


SCREEN = 0.25
HIGHEST = lax.Precision.HIGHEST
MESH = pl.DeviceIdType.MESH


def swapped(array, axis, distance):
    return lax.ppermute(array, axis, [(i, i ^ 1 << distance) for i in range(lax.axis_size(axis))])


def bit_count(number):
    return number.bit_length() - 1


def reverse_bits(values, digits):
    result = jnp.zeros_like(values)
    for digit in range(digits):
        result = result | (values >> digit & 1) << digits - 1 - digit
    return result


def dft_tables(length, freq_count):
    points = jnp.arange(length, dtype=jnp.int32)[:, None]
    freqs = jnp.arange(freq_count, dtype=jnp.int32)[None, :]
    angles = 2.0 * jnp.pi / length * (points * freqs % length).astype(jnp.float32)
    return (jnp.cos(angles), jnp.sin(angles))


def rotate(values, angles):
    cosine = jnp.cos(angles)
    sine = jnp.sin(angles)
    return (values[0] * cosine + values[1] * sine, values[1] * cosine - values[0] * sine)


def section_angles(z_rows, half, total):
    exponent = z_rows % half * (total // (2 * half))
    return (2.0 * jnp.pi / total * exponent.astype(jnp.float32))[:, None, None]


def combine_pair(mine, theirs, upper, angles):
    summed = (mine[0] + theirs[0], mine[1] + theirs[1])
    turned = rotate((theirs[0] - mine[0], theirs[1] - mine[1]), angles)
    return (jnp.where(upper, turned[0], summed[0]), jnp.where(upper, turned[1], summed[1]))


def local_sections(values, total):
    count = values[0].shape[0]
    shape = values[0].shape
    half = count // 2
    while half >= 1:
        split_real = values[0].reshape((count // (2 * half), 2, half) + shape[1:])
        split_imag = values[1].reshape((count // (2 * half), 2, half) + shape[1:])
        offsets = jnp.arange(half, dtype=jnp.int32) * (total // (2 * half))
        angles = (2.0 * jnp.pi / total * offsets.astype(jnp.float32))[None, :, None, None]
        summed_real = split_real[:, 0] + split_real[:, 1]
        summed_imag = split_imag[:, 0] + split_imag[:, 1]
        turned = rotate(
            (split_real[:, 0] - split_real[:, 1], split_imag[:, 0] - split_imag[:, 1]), angles
        )
        values = (
            jnp.stack([summed_real, turned[0]], axis=1).reshape(shape),
            jnp.stack([summed_imag, turned[1]], axis=1).reshape(shape),
        )
        half = half // 2
    return values


def on_device_wide(brick_data, brick_xy, brick_live):
    layers = brick_live.shape[0]
    capacity = brick_data.shape[0] // layers
    brick = brick_data.shape[1]
    area = brick_data.shape[2]
    zlocal = ZLOC
    per_layer = brick // zlocal
    ngroup = lax.axis_size("zg")
    nplane = lax.axis_size("zl")
    total = zlocal * ngroup * nplane
    width = PLANE
    blocks = width // brick
    kx_count = width // 2 + 1
    group_idx = lax.axis_index("zg")
    plane_idx = lax.axis_index("zl")
    live = (jnp.arange(capacity, dtype=jnp.int32)[None, :] < brick_live).astype(jnp.float32)
    masked = (
        brick_data.reshape(layers, capacity, per_layer, zlocal, area) * live[:, :, None, None, None]
    )
    outgoing = jnp.transpose(masked, (0, 2, 1, 3, 4)).reshape(
        layers * per_layer, capacity, zlocal, area
    )
    block_ids = (
        (brick_xy[1] * blocks + brick_xy[0]).astype(jnp.float32).reshape(layers, 1, capacity)
    )
    block_out = jnp.broadcast_to(block_ids, (layers, per_layer, capacity)).reshape(
        layers * per_layer, capacity
    )
    pieces, places = (
        lax.all_to_all(outgoing, "zl", split_axis=0, concat_axis=0, tiled=True),
        lax.all_to_all(block_out, "zl", split_axis=0, concat_axis=0, tiled=True),
    )
    slot_ids = places.astype(jnp.int32).reshape(-1)
    incoming = jnp.transpose(pieces, (2, 0, 1, 3)).reshape(zlocal, -1, area)
    blockgrid = (
        jnp.zeros((zlocal, blocks * blocks, area), jnp.float32).at[:, slot_ids, :].add(incoming)
    )
    blockgrid = blockgrid.reshape(zlocal, blocks, blocks, brick, brick)
    cos_x, sin_x = dft_tables(width, kx_count)
    cos_x = cos_x.reshape(blocks, brick, kx_count)
    sin_x = sin_x.reshape(blocks, brick, kx_count)
    first_real = jnp.einsum("zabuv,bvk->zkau", blockgrid, cos_x, precision=HIGHEST).reshape(
        zlocal * kx_count, width
    )
    first_imag = -jnp.einsum("zabuv,bvk->zkau", blockgrid, sin_x, precision=HIGHEST).reshape(
        zlocal * kx_count, width
    )
    cos_y, sin_y = dft_tables(width, width)
    second_real = jnp.dot(first_real, cos_y, precision=HIGHEST) + jnp.dot(
        first_imag, sin_y, precision=HIGHEST
    )
    second_imag = jnp.dot(first_imag, cos_y, precision=HIGHEST) - jnp.dot(
        first_real, sin_y, precision=HIGHEST
    )
    values = (
        second_real.reshape(zlocal, kx_count, width),
        second_imag.reshape(zlocal, kx_count, width),
    )
    device = group_idx * nplane + plane_idx
    z_rows = device * zlocal + jnp.arange(zlocal, dtype=jnp.int32)
    gbits = bit_count(ngroup)
    pbits = bit_count(nplane)
    for level in reversed(range(gbits)):
        half = zlocal * nplane * (1 << level)
        theirs = swapped((values[0], values[1]), "zg", level)
        upper = group_idx >> level & 1 == 1
        values = combine_pair(values, theirs, upper, section_angles(z_rows, half, total))
    plane_values = values
    for level in reversed(range(pbits)):
        half = zlocal * (1 << level)
        theirs = swapped((plane_values[0], plane_values[1]), "zl", level)
        upper = plane_idx >> level & 1 == 1
        plane_values = combine_pair(
            plane_values, theirs, upper, section_angles(z_rows, half, total)
        )
    plane_values = local_sections(plane_values, total)
    values = plane_values
    kz_rows = reverse_bits(z_rows, bit_count(total))
    along_z = 4.0 * jnp.sin(jnp.pi * kz_rows.astype(jnp.float32) / total) ** 2
    along_x = 4.0 * jnp.sin(jnp.pi * jnp.arange(kx_count, dtype=jnp.float32) / width) ** 2
    along_y = 4.0 * jnp.sin(jnp.pi * jnp.arange(width, dtype=jnp.float32) / width) ** 2
    denom = along_z[:, None, None] + along_x[None, :, None] + along_y[None, None, :] + SCREEN
    factor = -(1.0 / math.sqrt(width * width * total)) / denom
    return (values[0] * factor, values[1] * factor)


def kz_of(row, total):
    digits = bit_count(total)
    return sum(
        lax.rem(lax.div(row, jnp.int32(1 << d)), jnp.int32(2)) * (1 << digits - 1 - d)
        for d in range(digits)
    )


def reversed_bits(row, digits):
    return sum((row >> d & 1) << digits - 1 - d for d in range(digits))


def transposed_blocks(tiles, width):
    tiles = list(tiles)
    block = lax.broadcasted_iota(jnp.int32, tiles[0].shape, tiles[0].ndim - 1) // width
    lanes = tiles[0].shape[-1]
    step = len(tiles) // 2
    while step:
        high = (block & step) != 0
        for i in range(len(tiles)):
            if not i & step:
                low, up = tiles[i], tiles[i + step]
                tiles[i] = jnp.where(high, pltpu.roll(up, step * width, low.ndim - 1), low)
                tiles[i + step] = jnp.where(
                    high, up, pltpu.roll(low, lanes - step * width, low.ndim - 1)
                )
        step //= 2
    return tiles


def exchange_kernel(
    ngroup, nplane, capacity, blocks,
    coef, live, bricks, xy, out, data, raw, ready, zsend, zrecv, psend, precv, loaded,
):
    group, plane = lax.axis_index("zg"), lax.axis_index("zl")
    quads = capacity // 4
    depth = data.shape[1]
    load = pltpu.make_async_copy(bricks, data, loaded)
    load.start()
    barrier = pltpu.get_barrier_semaphore()

    def greet(g, p):
        pl.semaphore_signal(barrier, inc=1, device_id=(g, p), device_id_type=MESH)

    for k in range(1, nplane):
        greet(group, lax.rem(plane + k, nplane))
    pl.when(group > 0)(lambda: greet(group - 1, plane))
    pl.when(group < ngroup - 1)(lambda: greet(group + 1, plane))
    ends = jnp.where(group > 0, 1, 0) + jnp.where(group < ngroup - 1, 1, 0)
    pl.semaphore_wait(barrier, nplane - 1 + ends)

    def along(side, t):
        chunk = jnp.where(side == 0, group - t, group + t)
        target = jnp.where(side == 0, group + 1, group - 1)
        inside = (chunk >= 0) & (chunk < ngroup) & (target >= 0) & (target < ngroup)
        safe = jnp.clip(chunk, 0, ngroup - 1)
        copy = pltpu.make_async_remote_copy(
            src_ref=raw.at[safe],
            dst_ref=raw.at[safe],
            send_sem=zsend.at[side, t],
            recv_sem=zrecv.at[side, t],
            device_id=(jnp.clip(target, 0, ngroup - 1), plane),
            device_id_type=MESH,
        )
        return inside, copy

    def to_peer(chunk, k):
        return pltpu.make_async_remote_copy(
            src_ref=ready.at[chunk, k],
            dst_ref=out.at[plane, chunk],
            send_sem=psend.at[chunk, k],
            recv_sem=precv.at[chunk, k],
            device_id=(group, lax.rem(plane + k, nplane)),
            device_id_type=MESH,
        )

    def sums(chunk, peer, target):
        first = ((group * ngroup + chunk) * nplane + peer) * 2 * depth
        real = [coef[first + 2 * z] for z in range(depth)]
        imag = [coef[first + 2 * z + 1] for z in range(depth)]
        for quad in range(quads):
            parts = []
            for table in (real, imag):
                for parity in range(2):
                    summed = None
                    for z in range(parity, depth, 2):
                        term = raw[chunk, pl.ds((quad * depth + z) * 8, 8)] * table[z]
                        summed = term if summed is None else summed + term
                    parts.append(summed)
            tiles = (parts[0] + parts[1], parts[2] + parts[3], parts[0] - parts[1], parts[2] - parts[3])
            for i, tile in enumerate(transposed_blocks(tiles, 32)):
                target[quad * 4 + i] = tile
        target[capacity] = raw[chunk, pl.ds(quads * depth * 8, 8)]

    def share(chunk):
        def one(k, carry):
            sums(chunk, lax.rem(plane + k, nplane), ready.at[chunk, k])
            to_peer(chunk, k).start()
            return carry

        lax.fori_loop(1, nplane, one, 0)
        sums(chunk, plane, out.at[plane, chunk])

    load.wait()
    for quad in range(quads):
        for z in range(0, depth, 8):
            for half in range(2):
                tiles = []
                for slot in range(quad * 4, quad * 4 + 4):
                    keep = jnp.where(slot < live[0, 0], 1.0, 0.0)
                    tiles.append(data[slot, z : z + 8, half * 128 : half * 128 + 128] * keep)
                for i, tile in enumerate(transposed_blocks(tiles, 32)):
                    row = (quad * depth + z) * 8 + half * 4 + i
                    raw[group, pl.ds(row, 8, stride=8), :] = tile
    place = (xy[1:2, :] * blocks + xy[0:1, :]).astype(jnp.float32)
    place = jnp.concatenate([place, jnp.zeros((1, 128 - capacity), jnp.float32)], axis=1)
    raw[group, pl.ds(quads * depth * 8, 8)] = jnp.broadcast_to(place, (8, 128))
    for side in range(2):
        inside, copy = along(side, 0)
        pl.when(inside)(copy.start)
    share(group)

    def arrival(i, carry):
        t, side = i // 2, lax.rem(i, 2)
        chunk = jnp.where(side == 0, group - 1 - t, group + 1 + t)

        @pl.when((chunk >= 0) & (chunk < ngroup))
        def _():
            safe = jnp.clip(chunk, 0, ngroup - 1)
            pltpu.make_async_remote_copy(
                src_ref=raw.at[safe],
                dst_ref=raw.at[safe],
                send_sem=zsend.at[side, t],
                recv_sem=zrecv.at[side, t],
                device_id=(group, plane),
                device_id_type=MESH,
            ).wait_recv()

            @pl.when(t < ngroup - 2)
            def _():
                inside, copy = along(side, jnp.minimum(t + 1, ngroup - 2))
                pl.when(inside)(copy.start)

            share(safe)

        return carry

    lax.fori_loop(0, 2 * (ngroup - 1), arrival, 0)

    for side in range(2):
        for t in range(ngroup - 1):
            inside, copy = along(side, t)
            pl.when(inside)(copy.wait_send)

    def finish(i, carry):
        copy = to_peer(i // (nplane - 1), 1 + lax.rem(i, nplane - 1))
        copy.wait_send()
        copy.wait_recv()
        return carry

    lax.fori_loop(0, ngroup * (nplane - 1), finish, 0)


def split(values):
    high = values.astype(jnp.bfloat16)
    return high, (values - high.astype(jnp.float32)).astype(jnp.bfloat16)


def spectrum_kernel(
    nplane, ngroup, capacity, blocks, evens, scale,
    places, along_z, bricks, along_x, along_y, tx_hbm, ty_hbm, out_real, out_imag,
    grid, rows, lines, tx, ty, loaded,
):
    half = rows.shape[-1] // 2
    width = rows.shape[-1]
    device = lax.axis_index("zg") * nplane + lax.axis_index("zl")
    total = along_z.shape[0]

    loads = (
        pltpu.make_async_copy(tx_hbm, tx, loaded.at[0]),
        pltpu.make_async_copy(ty_hbm, ty, loaded.at[1]),
    )
    for load in loads:
        load.start()

    def clear(i, carry):
        grid[pl.ds(i * 32, 32)] = jnp.zeros((32,) + grid.shape[1:], jnp.float32)
        return carry

    lax.fori_loop(0, grid.shape[0] // 32, clear, 0)

    def place(i, carry):
        source, chunk = i // ngroup, lax.rem(i, ngroup)
        ids = [places[i * capacity + c] for c in range(capacity)]
        values = [grid[ids[c]] + bricks[source, chunk, c] for c in range(capacity)]
        for c in range(capacity):
            grid[ids[c]] = values[c]
        return carry

    lax.fori_loop(0, nplane * ngroup, place, 0)

    batch = 4

    def arrange(step, carry):
        for h in range(2):
            first, second = (
                transposed_blocks(
                    [
                        jnp.stack(
                            [
                                grid[(step * batch + n) * blocks + at * 8 + i]
                                for n in range(batch)
                            ]
                        )
                        for i in range(8)
                    ],
                    16,
                )
                for at in (h, h + 2)
            )
            for j in range(8):
                kz, ri, parity = j // 4, j // 2 % 2, j % 2
                lanes = pl.ds(ri * half + h * 128, 128)
                at = pl.ds(pl.multiple_of(step * batch * 8, batch * 8), batch * 8)
                rows[0, kz, parity, at, lanes] = (first[j] + second[j]).reshape(-1, 128)
                rows[1, kz, parity, at, lanes] = (first[j] - second[j]).reshape(-1, 128)
        return carry

    lax.fori_loop(0, blocks // batch, arrange, 0)
    for load in loads:
        load.wait()

    def product(a, b, dims):
        return lax.dot_general(a, b, (dims, ((), ())), preferred_element_type=jnp.float32)

    padded = along_x.shape[1]
    for parity in range(2):
        for odd in range(2):
            table = tx.at[odd]
            count = table.shape[0] // 2
            for kz in range(ZLOC):
                high, low = split(rows[odd, kz, parity])
                both = product(table[...], high, ((1,), (1,)))
                first = both[:count] + (both[count:] + product(table[:count], low, ((1,), (1,))))
                at = pl.ds((odd * ZLOC + kz) * padded, padded)
                lines[parity, at, :half] = first[:padded]
                lines[parity, at, half:] = first[padded:]

    results = []
    for parity in range(2):
        high, low = split(lines[parity])
        count = high.shape[0]
        both = product(jnp.concatenate([high, low], axis=0), ty[parity, 0], ((1,), (0,)))
        results.append(both[:count] + (both[count:] + product(high, ty[parity, 1], ((1,), (0,)))))
    lines[0] = results[0] + results[1]
    lines[1] = results[0] - results[1]

    tiles = width // 128
    for odd in range(2):
        for kz in range(ZLOC):
            at = pl.ds((odd * ZLOC + kz) * padded, padded)
            for tile in range(tiles):
                lanes = pl.ds(tile * 128, 128)
                denom = along_z[kz_of(device * ZLOC + kz, total)] + along_x[odd] + along_y[:, lanes] + SCREEN
                factor = scale / denom
                sign, lane = tile // (tiles // 2), tile % (tiles // 2) * 128
                for out, start in ((out_real, 0), (out_imag, half)):
                    value = lines[sign, at, pl.ds(start + lane, 128)] * factor
                    row = (odd * tiles + tile) * ZLOC + kz
                    out[pl.ds(row, evens[odd], stride=2 * tiles * ZLOC), :] = value[: evens[odd]]


def parted(table):
    high = table.astype(ml_dtypes.bfloat16)
    low = (table - high.astype(np.float64)).astype(ml_dtypes.bfloat16)
    return high, low


def x_tables(width):
    tables = []
    for odd in range(2):
        padded = -(-(width // 4 + 1) // 8) * 8
        kx = 2 * np.arange(padded)[:, None] + odd
        angles = 2 * np.pi / width * (kx * np.arange(width // 2)[None, :] % width)
        cosine, sine = np.cos(angles), np.sin(angles)
        tables.append(np.concatenate(parted(np.block([[cosine, sine], [-sine, cosine]]))))
    return tables


def y_tables(width):
    tables = []
    for parity in range(2):
        y = 2 * np.arange(width // 2)[:, None] + parity
        angles = 2 * np.pi / width * (y * np.arange(width // 2)[None, :] % width)
        cosine, sine = np.cos(angles), np.sin(angles)
        tables.append(np.stack(parted(np.block([[cosine, -sine], [sine, cosine]]))))
    return np.stack(tables)


def on_device_once(brick_data, brick_xy, brick_live):
    capacity, brick, area = brick_data.shape
    ngroup, nplane = lax.axis_size("zg"), lax.axis_size("zl")
    total = ZLOC * ngroup * nplane
    width = PLANE
    blocks = width // brick
    quads = capacity // 4
    turns = np.arange(total) / total
    kz = np.array([reversed_bits(row, bit_count(total)) for row in range(0, total, ZLOC)])
    angles = kz.reshape(ngroup, 1, nplane, 1) * np.arange(ngroup * brick).reshape(-1, 1, brick)
    angles = 2 * np.pi / total * (angles % total)
    coef = np.stack([np.cos(angles), -np.sin(angles)], axis=-1).astype(np.float32).reshape(-1)
    along_z = jnp.asarray((4 * np.sin(np.pi * turns) ** 2).astype(np.float32))

    vmem = pl.BlockSpec(memory_space=pltpu.VMEM)
    smem = pl.BlockSpec(memory_space=pltpu.SMEM)
    hbm = pl.BlockSpec(memory_space=pltpu.HBM)
    arrived = pl.pallas_call(
        functools.partial(exchange_kernel, ngroup, nplane, capacity, blocks),
        out_shape=jax.ShapeDtypeStruct((nplane, ngroup, capacity + 1, 8, 128), jnp.float32),
        in_specs=[smem, smem, hbm, vmem],
        out_specs=vmem,
        scratch_shapes=[
            pltpu.VMEM(brick_data.shape, jnp.float32),
            pltpu.VMEM((ngroup, (quads * brick + 1) * 8, 128), jnp.float32),
            pltpu.VMEM((ngroup, nplane, capacity + 1, 8, 128), jnp.float32),
            pltpu.SemaphoreType.DMA((2, ngroup - 1)),
            pltpu.SemaphoreType.DMA((2, ngroup - 1)),
            pltpu.SemaphoreType.DMA((ngroup, nplane)),
            pltpu.SemaphoreType.DMA((ngroup, nplane)),
            pltpu.SemaphoreType.DMA,
        ],
        compiler_params=pltpu.CompilerParams(
            collective_id=0, has_side_effects=True, vmem_limit_bytes=60 * 2**20
        ),
        name="exchange",
    )(jnp.asarray(coef), brick_live, brick_data, brick_xy)

    places = arrived[:, :, capacity, 0, :capacity].astype(jnp.int32).reshape(-1)
    tx = np.stack(x_tables(width))
    evens = (width // 4 + 1, width // 4)
    axis = 4 * np.sin(np.pi * np.arange(width) / width) ** 2
    along_x = np.zeros((2, tx.shape[1] // 4, 128), np.float32)
    for odd in range(2):
        along_x[odd, : evens[odd]] = axis[odd : width // 2 + 1 : 2][:, None]
    along_y = axis[None, :].astype(np.float32)

    ty = y_tables(width)
    tables = [jnp.asarray(t) for t in (along_x, along_y, tx, ty)]
    kx_count = width // 2 + 1
    out = jax.ShapeDtypeStruct((kx_count * width // 128 * ZLOC, 128), jnp.float32)
    scale = -1.0 / math.sqrt(width * width * total)
    results = pl.pallas_call(
        functools.partial(spectrum_kernel, nplane, ngroup, capacity, blocks, evens, scale),
        out_shape=(out, out),
        in_specs=[smem, smem, vmem, vmem, vmem, hbm, hbm],
        out_specs=(vmem, vmem),
        scratch_shapes=[
            pltpu.VMEM((blocks * blocks, 8, 128), jnp.float32),
            pltpu.VMEM((2, ZLOC, 2, width // 2, width), jnp.float32),
            pltpu.VMEM((2, 2 * ZLOC * along_x.shape[1], width), jnp.float32),
            pltpu.VMEM(tx.shape, tx.dtype),
            pltpu.VMEM(ty.shape, ty.dtype),
            pltpu.SemaphoreType.DMA((2,)),
        ],
        compiler_params=pltpu.CompilerParams(vmem_limit_bytes=60 * 2**20),
        name="spectrum",
    )(places, along_z, arrived, *tables)

    def ordered(result):
        result = result.reshape(kx_count, width // 128, ZLOC, 128)
        return jnp.transpose(result, (2, 0, 1, 3)).reshape(ZLOC, kx_count, width)

    return tuple(ordered(result) for result in results)


def on_device(brick_data, brick_xy, brick_live):
    layers = brick_live.shape[0]
    slots, brick, area = brick_data.shape
    nplane, ngroup = lax.axis_size("zl"), lax.axis_size("zg")
    one_layer = layers == 1 and nplane * ZLOC == brick and brick == 16 and slots == 16
    fits = slots * nplane * ngroup * area * 2 * ZLOC * 4 <= 4 * 2**20
    if one_layer and fits and ngroup > 1:
        return on_device_once(brick_data, brick_xy, brick_live)
    return on_device_wide(brick_data, brick_xy, brick_live)


def solution(mesh):
    in_specs = (P(("zg", "zl"), None, None), P(None, ("zg", "zl")), P(None, ("zg", "zl")))
    out_specs = (P(("zg", "zl"), None, None), P(("zg", "zl"), None, None))
    return jax.shard_map(
        on_device, mesh=mesh, in_specs=in_specs, out_specs=out_specs, check_vma=False
    )
```

```python
import functools
import math

import jax
import jax.numpy as jnp
import ml_dtypes
import numpy as np
from jax import lax
from jax.experimental import pallas as pl
from jax.experimental.pallas import tpu as pltpu
from jax.sharding import PartitionSpec as P

PLANE = 512
ZLOC = 2


SCREEN = 0.25
HIGHEST = lax.Precision.HIGHEST
MESH = pl.DeviceIdType.MESH


def swapped(array, axis, distance):
    return lax.ppermute(array, axis, [(i, i ^ 1 << distance) for i in range(lax.axis_size(axis))])


def bit_count(number):
    return number.bit_length() - 1


def reverse_bits(values, digits):
    result = jnp.zeros_like(values)
    for digit in range(digits):
        result = result | (values >> digit & 1) << digits - 1 - digit
    return result


def dft_tables(length, freq_count):
    points = jnp.arange(length, dtype=jnp.int32)[:, None]
    freqs = jnp.arange(freq_count, dtype=jnp.int32)[None, :]
    angles = 2.0 * jnp.pi / length * (points * freqs % length).astype(jnp.float32)
    return (jnp.cos(angles), jnp.sin(angles))


def rotate(values, angles):
    cosine = jnp.cos(angles)
    sine = jnp.sin(angles)
    return (values[0] * cosine + values[1] * sine, values[1] * cosine - values[0] * sine)


def section_angles(z_rows, half, total):
    exponent = z_rows % half * (total // (2 * half))
    return (2.0 * jnp.pi / total * exponent.astype(jnp.float32))[:, None, None]


def combine_pair(mine, theirs, upper, angles):
    summed = (mine[0] + theirs[0], mine[1] + theirs[1])
    turned = rotate((theirs[0] - mine[0], theirs[1] - mine[1]), angles)
    return (jnp.where(upper, turned[0], summed[0]), jnp.where(upper, turned[1], summed[1]))


def local_sections(values, total):
    count = values[0].shape[0]
    shape = values[0].shape
    half = count // 2
    while half >= 1:
        split_real = values[0].reshape((count // (2 * half), 2, half) + shape[1:])
        split_imag = values[1].reshape((count // (2 * half), 2, half) + shape[1:])
        offsets = jnp.arange(half, dtype=jnp.int32) * (total // (2 * half))
        angles = (2.0 * jnp.pi / total * offsets.astype(jnp.float32))[None, :, None, None]
        summed_real = split_real[:, 0] + split_real[:, 1]
        summed_imag = split_imag[:, 0] + split_imag[:, 1]
        turned = rotate(
            (split_real[:, 0] - split_real[:, 1], split_imag[:, 0] - split_imag[:, 1]), angles
        )
        values = (
            jnp.stack([summed_real, turned[0]], axis=1).reshape(shape),
            jnp.stack([summed_imag, turned[1]], axis=1).reshape(shape),
        )
        half = half // 2
    return values


def on_device_wide(brick_data, brick_xy, brick_live):
    layers = brick_live.shape[0]
    capacity = brick_data.shape[0] // layers
    brick = brick_data.shape[1]
    area = brick_data.shape[2]
    zlocal = ZLOC
    per_layer = brick // zlocal
    ngroup = lax.axis_size("zg")
    nplane = lax.axis_size("zl")
    total = zlocal * ngroup * nplane
    width = PLANE
    blocks = width // brick
    kx_count = width // 2 + 1
    group_idx = lax.axis_index("zg")
    plane_idx = lax.axis_index("zl")
    live = (jnp.arange(capacity, dtype=jnp.int32)[None, :] < brick_live).astype(jnp.float32)
    masked = (
        brick_data.reshape(layers, capacity, per_layer, zlocal, area) * live[:, :, None, None, None]
    )
    outgoing = jnp.transpose(masked, (0, 2, 1, 3, 4)).reshape(
        layers * per_layer, capacity, zlocal, area
    )
    block_ids = (
        (brick_xy[1] * blocks + brick_xy[0]).astype(jnp.float32).reshape(layers, 1, capacity)
    )
    block_out = jnp.broadcast_to(block_ids, (layers, per_layer, capacity)).reshape(
        layers * per_layer, capacity
    )
    pieces, places = (
        lax.all_to_all(outgoing, "zl", split_axis=0, concat_axis=0, tiled=True),
        lax.all_to_all(block_out, "zl", split_axis=0, concat_axis=0, tiled=True),
    )
    slot_ids = places.astype(jnp.int32).reshape(-1)
    incoming = jnp.transpose(pieces, (2, 0, 1, 3)).reshape(zlocal, -1, area)
    blockgrid = (
        jnp.zeros((zlocal, blocks * blocks, area), jnp.float32).at[:, slot_ids, :].add(incoming)
    )
    blockgrid = blockgrid.reshape(zlocal, blocks, blocks, brick, brick)
    cos_x, sin_x = dft_tables(width, kx_count)
    cos_x = cos_x.reshape(blocks, brick, kx_count)
    sin_x = sin_x.reshape(blocks, brick, kx_count)
    first_real = jnp.einsum("zabuv,bvk->zkau", blockgrid, cos_x, precision=HIGHEST).reshape(
        zlocal * kx_count, width
    )
    first_imag = -jnp.einsum("zabuv,bvk->zkau", blockgrid, sin_x, precision=HIGHEST).reshape(
        zlocal * kx_count, width
    )
    cos_y, sin_y = dft_tables(width, width)
    second_real = jnp.dot(first_real, cos_y, precision=HIGHEST) + jnp.dot(
        first_imag, sin_y, precision=HIGHEST
    )
    second_imag = jnp.dot(first_imag, cos_y, precision=HIGHEST) - jnp.dot(
        first_real, sin_y, precision=HIGHEST
    )
    values = (
        second_real.reshape(zlocal, kx_count, width),
        second_imag.reshape(zlocal, kx_count, width),
    )
    device = group_idx * nplane + plane_idx
    z_rows = device * zlocal + jnp.arange(zlocal, dtype=jnp.int32)
    gbits = bit_count(ngroup)
    pbits = bit_count(nplane)
    for level in reversed(range(gbits)):
        half = zlocal * nplane * (1 << level)
        theirs = swapped((values[0], values[1]), "zg", level)
        upper = group_idx >> level & 1 == 1
        values = combine_pair(values, theirs, upper, section_angles(z_rows, half, total))
    plane_values = values
    for level in reversed(range(pbits)):
        half = zlocal * (1 << level)
        theirs = swapped((plane_values[0], plane_values[1]), "zl", level)
        upper = plane_idx >> level & 1 == 1
        plane_values = combine_pair(
            plane_values, theirs, upper, section_angles(z_rows, half, total)
        )
    plane_values = local_sections(plane_values, total)
    values = plane_values
    kz_rows = reverse_bits(z_rows, bit_count(total))
    along_z = 4.0 * jnp.sin(jnp.pi * kz_rows.astype(jnp.float32) / total) ** 2
    along_x = 4.0 * jnp.sin(jnp.pi * jnp.arange(kx_count, dtype=jnp.float32) / width) ** 2
    along_y = 4.0 * jnp.sin(jnp.pi * jnp.arange(width, dtype=jnp.float32) / width) ** 2
    denom = along_z[:, None, None] + along_x[None, :, None] + along_y[None, None, :] + SCREEN
    factor = -(1.0 / math.sqrt(width * width * total)) / denom
    return (values[0] * factor, values[1] * factor)


def kz_of(row, total):
    digits = bit_count(total)
    return sum(
        lax.rem(lax.div(row, jnp.int32(1 << d)), jnp.int32(2)) * (1 << digits - 1 - d)
        for d in range(digits)
    )


def reversed_bits(row, digits):
    return sum((row >> d & 1) << digits - 1 - d for d in range(digits))


def transposed_blocks(tiles, width):
    tiles = list(tiles)
    block = lax.broadcasted_iota(jnp.int32, tiles[0].shape, tiles[0].ndim - 1) // width
    lanes = tiles[0].shape[-1]
    step = len(tiles) // 2
    while step:
        high = (block & step) != 0
        for i in range(len(tiles)):
            if not i & step:
                low, up = tiles[i], tiles[i + step]
                if 2 * step * width == lanes:
                    swapped_part = pltpu.roll(jnp.where(high, low, up), step * width, low.ndim - 1)
                    tiles[i] = jnp.where(high, swapped_part, low)
                    tiles[i + step] = jnp.where(high, up, swapped_part)
                    continue
                tiles[i] = jnp.where(high, pltpu.roll(up, step * width, low.ndim - 1), low)
                tiles[i + step] = jnp.where(
                    high, up, pltpu.roll(low, lanes - step * width, low.ndim - 1)
                )
        step //= 2
    return tiles


def exchange_kernel(
    ngroup, nplane, capacity, blocks,
    coef, live, bricks, xy, out, out_places, data, raw, ready, spots, zsend, zrecv, psend, precv,
    ssend, srecv, loaded,
):
    group, plane = lax.axis_index("zg"), lax.axis_index("zl")
    quads = capacity // 4
    depth = data.shape[1]
    load = pltpu.make_async_copy(bricks, data, loaded)
    load.start()
    barrier = pltpu.get_barrier_semaphore()

    def greet(g, p):
        pl.semaphore_signal(barrier, inc=1, device_id=(g, p), device_id_type=MESH)

    for k in range(1, nplane):
        greet(group, lax.rem(plane + k, nplane))
    pl.when(group > 0)(lambda: greet(group - 1, plane))
    pl.when(group < ngroup - 1)(lambda: greet(group + 1, plane))
    ends = jnp.where(group > 0, 1, 0) + jnp.where(group < ngroup - 1, 1, 0)
    pl.semaphore_wait(barrier, nplane - 1 + ends)

    def along(side, t):
        chunk = jnp.where(side == 0, group - t, group + t)
        target = jnp.where(side == 0, group + 1, group - 1)
        inside = (chunk >= 0) & (chunk < ngroup) & (target >= 0) & (target < ngroup)
        safe = jnp.clip(chunk, 0, ngroup - 1)
        copy = pltpu.make_async_remote_copy(
            src_ref=raw.at[safe],
            dst_ref=raw.at[safe],
            send_sem=zsend.at[side, t],
            recv_sem=zrecv.at[side, t],
            device_id=(jnp.clip(target, 0, ngroup - 1), plane),
            device_id_type=MESH,
        )
        return inside, copy

    def to_peer(chunk, k):
        return pltpu.make_async_remote_copy(
            src_ref=ready.at[chunk, k],
            dst_ref=out.at[plane, chunk],
            send_sem=psend.at[chunk, k],
            recv_sem=precv.at[chunk, k],
            device_id=(group, lax.rem(plane + k, nplane)),
            device_id_type=MESH,
        )

    def sums(chunk, peer, target):
        first = ((group * ngroup + chunk) * nplane + peer) * 2 * depth
        real = [coef[first + 2 * z] for z in range(depth)]
        imag = [coef[first + 2 * z + 1] for z in range(depth)]
        for quad in range(quads):
            parts = []
            for table in (real, imag):
                for parity in range(2):
                    summed = None
                    for z in range(parity, depth, 2):
                        term = raw[chunk, pl.ds((quad * depth + z) * 8, 8)] * table[z]
                        summed = term if summed is None else summed + term
                    parts.append(summed)
            tiles = (parts[0] + parts[1], parts[2] + parts[3], parts[0] - parts[1], parts[2] - parts[3])
            for i, tile in enumerate(transposed_blocks(tiles, 32)):
                target[quad * 4 + i] = tile

    def share(chunk):
        def one(k, carry):
            sums(chunk, lax.rem(plane + k, nplane), ready.at[chunk, k])
            to_peer(chunk, k).start()
            return carry

        lax.fori_loop(1, nplane, one, 0)
        sums(chunk, plane, out.at[plane, chunk])

    load.wait()
    for quad in range(quads):
        for z in range(0, depth, 8):
            for half in range(2):
                tiles = []
                for slot in range(quad * 4, quad * 4 + 4):
                    keep = jnp.where(slot < live[0, 0], 1.0, 0.0)
                    tiles.append(data[slot, z : z + 8, half * 128 : half * 128 + 128] * keep)
                for i, tile in enumerate(transposed_blocks(tiles, 32)):
                    row = (quad * depth + z) * 8 + half * 4 + i
                    raw[group, pl.ds(row, 8, stride=8), :] = tile
    place = (xy[1:2, :] * blocks + xy[0:1, :]).astype(jnp.float32)
    place = jnp.concatenate([place, jnp.zeros((1, 128 - capacity), jnp.float32)], axis=1)
    raw[group, pl.ds(quads * depth * 8, 8)] = jnp.broadcast_to(place, (8, 128))
    for side in range(2):
        inside, copy = along(side, 0)
        pl.when(inside)(copy.start)
    share(group)

    def arrival(i, carry):
        t, side = i // 2, lax.rem(i, 2)
        chunk = jnp.where(side == 0, group - 1 - t, group + 1 + t)

        @pl.when((chunk >= 0) & (chunk < ngroup))
        def _():
            safe = jnp.clip(chunk, 0, ngroup - 1)
            pltpu.make_async_remote_copy(
                src_ref=raw.at[safe],
                dst_ref=raw.at[safe],
                send_sem=zsend.at[side, t],
                recv_sem=zrecv.at[side, t],
                device_id=(group, plane),
                device_id_type=MESH,
            ).wait_recv()

            @pl.when(t < ngroup - 2)
            def _():
                inside, copy = along(side, jnp.minimum(t + 1, ngroup - 2))
                pl.when(inside)(copy.start)

            share(safe)

        return carry

    lax.fori_loop(0, 2 * (ngroup - 1), arrival, 0)

    spots[...] = jnp.zeros_like(spots)
    for chunk in range(ngroup):
        spots[chunk : chunk + 1] = raw[chunk, pl.ds(quads * depth * 8, 1)]
    out_places[plane] = spots[...]

    def spots_to(k):
        return pltpu.make_async_remote_copy(
            src_ref=spots,
            dst_ref=out_places.at[plane],
            send_sem=ssend.at[k],
            recv_sem=srecv.at[k],
            device_id=(group, lax.rem(plane + k, nplane)),
            device_id_type=MESH,
        )

    for k in range(1, nplane):
        spots_to(k).start()

    for side in range(2):
        for t in range(ngroup - 1):
            inside, copy = along(side, t)
            pl.when(inside)(copy.wait_send)

    def finish(i, carry):
        copy = to_peer(i // (nplane - 1), 1 + lax.rem(i, nplane - 1))
        copy.wait_send()
        copy.wait_recv()
        return carry

    lax.fori_loop(0, ngroup * (nplane - 1), finish, 0)
    for k in range(1, nplane):
        spots_to(k).wait_send()
        spots_to(k).wait_recv()


def split(values):
    high = values.astype(jnp.bfloat16)
    return high, (values - high.astype(jnp.float32)).astype(jnp.bfloat16)


def spectrum_kernel(
    nplane, ngroup, capacity, blocks, evens, scale,
    places, along_z, bricks, along_x, along_y, tx, ty, out_real, out_imag,
    grid, rows, lines,
):
    half = rows.shape[-1] // 2
    width = rows.shape[-1]
    device = lax.axis_index("zg") * nplane + lax.axis_index("zl")
    total = along_z.shape[0]

    def clear(i, carry):
        grid[pl.ds(i * 32, 32)] = jnp.zeros((32,) + grid.shape[1:], jnp.float32)
        return carry

    lax.fori_loop(0, grid.shape[0] // 32, clear, 0)

    def place(i, carry):
        chunk, pair = i // (nplane // 2), lax.rem(i, nplane // 2)
        slots = [(pair * 2 + n, c) for n in range(2) for c in range(capacity)]
        ids = [places[(source * ngroup + chunk) * capacity + c] for source, c in slots]
        values = [grid[at] + bricks[source, chunk, c] for at, (source, c) in zip(ids, slots)]
        for at, value in zip(ids, values):
            grid[at] = value
        return carry

    lax.fori_loop(0, nplane * ngroup // 2, place, 0)

    batch = 2

    def arrange(step, carry):
        for h in range(2):
            tiles = []
            for i in range(8):
                first, second = (
                    jnp.stack([grid[(step * batch + n) * blocks + at + i] for n in range(batch)])
                    for at in (h * 8, h * 8 + 16)
                )
                tiles.append((first + second, first - second))
            for side in range(2):
                lines_of = transposed_blocks([pair[side] for pair in tiles], 16)
                for j in range(8):
                    kz, ri, parity = j // 4, j // 2 % 2, j % 2
                    lanes = pl.ds(ri * half + h * 128, 128)
                    at = pl.ds(pl.multiple_of(step * batch * 8, batch * 8), batch * 8)
                    rows[side, kz, parity, at, lanes] = lines_of[j].reshape(-1, 128)
        return carry

    lax.fori_loop(0, blocks // batch, arrange, 0)

    def product(a, b, dims):
        return lax.dot_general(a, b, (dims, ((), ())), preferred_element_type=jnp.float32)

    padded = along_x.shape[1]
    for parity in range(2):
        for odd in range(2):
            table = tx.at[odd]
            count = table.shape[0] // 2
            for kz in range(ZLOC):
                high, low = split(rows[odd, kz, parity])
                both = product(table[...], high, ((1,), (1,)))
                first = both[:count] + (both[count:] + product(table[:count], low, ((1,), (1,))))
                at = pl.ds((odd * ZLOC + kz) * padded, padded)
                lines[parity, at, :half] = first[:padded]
                lines[parity, at, half:] = first[padded:]

    results = []
    for parity in range(2):
        high, low = split(lines[parity])
        count = high.shape[0]
        both = product(jnp.concatenate([high, low], axis=0), ty[parity, 0], ((1,), (0,)))
        results.append(both[:count] + (both[count:] + product(high, ty[parity, 1], ((1,), (0,)))))
    lines[0] = results[0] + results[1]
    lines[1] = results[0] - results[1]

    tiles = width // 128
    for odd in range(2):
        for kz in range(ZLOC):
            at = pl.ds((odd * ZLOC + kz) * padded, padded)
            for tile in range(tiles):
                lanes = pl.ds(tile * 128, 128)
                denom = along_z[kz_of(device * ZLOC + kz, total)] + along_x[odd] + along_y[:, lanes] + SCREEN
                factor = scale / denom
                sign, lane = tile // (tiles // 2), tile % (tiles // 2) * 128
                for out, start in ((out_real, 0), (out_imag, half)):
                    value = lines[sign, at, pl.ds(start + lane, 128)] * factor
                    row = (odd * tiles + tile) * ZLOC + kz
                    out[pl.ds(row, evens[odd], stride=2 * tiles * ZLOC), :] = value[: evens[odd]]


def parted(table):
    high = table.astype(ml_dtypes.bfloat16)
    low = (table - high.astype(np.float64)).astype(ml_dtypes.bfloat16)
    return high, low


def x_tables(width):
    tables = []
    for odd in range(2):
        padded = -(-(width // 4 + 1) // 8) * 8
        kx = 2 * np.arange(padded)[:, None] + odd
        angles = 2 * np.pi / width * (kx * np.arange(width // 2)[None, :] % width)
        cosine, sine = np.cos(angles), np.sin(angles)
        tables.append(np.concatenate(parted(np.block([[cosine, sine], [-sine, cosine]]))))
    return tables


def y_tables(width):
    tables = []
    for parity in range(2):
        y = 2 * np.arange(width // 2)[:, None] + parity
        angles = 2 * np.pi / width * (y * np.arange(width // 2)[None, :] % width)
        cosine, sine = np.cos(angles), np.sin(angles)
        tables.append(np.stack(parted(np.block([[cosine, -sine], [sine, cosine]]))))
    return np.stack(tables)


def on_device_once(brick_data, brick_xy, brick_live):
    capacity, brick, area = brick_data.shape
    ngroup, nplane = lax.axis_size("zg"), lax.axis_size("zl")
    total = ZLOC * ngroup * nplane
    width = PLANE
    blocks = width // brick
    quads = capacity // 4
    turns = np.arange(total) / total
    kz = np.array([reversed_bits(row, bit_count(total)) for row in range(0, total, ZLOC)])
    angles = kz.reshape(ngroup, 1, nplane, 1) * np.arange(ngroup * brick).reshape(-1, 1, brick)
    angles = 2 * np.pi / total * (angles % total)
    coef = np.stack([np.cos(angles), -np.sin(angles)], axis=-1).astype(np.float32).reshape(-1)
    along_z = jnp.asarray((4 * np.sin(np.pi * turns) ** 2).astype(np.float32))

    vmem = pl.BlockSpec(memory_space=pltpu.VMEM)
    smem = pl.BlockSpec(memory_space=pltpu.SMEM)
    hbm = pl.BlockSpec(memory_space=pltpu.HBM)
    arrived, places = pl.pallas_call(
        functools.partial(exchange_kernel, ngroup, nplane, capacity, blocks),
        out_shape=(
            jax.ShapeDtypeStruct((nplane, ngroup, capacity, 8, 128), jnp.float32),
            jax.ShapeDtypeStruct((nplane, 8, 128), jnp.float32),
        ),
        in_specs=[smem, smem, hbm, vmem],
        out_specs=(vmem, vmem),
        scratch_shapes=[
            pltpu.VMEM(brick_data.shape, jnp.float32),
            pltpu.VMEM((ngroup, (quads * brick + 1) * 8, 128), jnp.float32),
            pltpu.VMEM((ngroup, nplane, capacity, 8, 128), jnp.float32),
            pltpu.VMEM((8, 128), jnp.float32),
            pltpu.SemaphoreType.DMA((2, ngroup - 1)),
            pltpu.SemaphoreType.DMA((2, ngroup - 1)),
            pltpu.SemaphoreType.DMA((ngroup, nplane)),
            pltpu.SemaphoreType.DMA((ngroup, nplane)),
            pltpu.SemaphoreType.DMA((nplane,)),
            pltpu.SemaphoreType.DMA((nplane,)),
            pltpu.SemaphoreType.DMA,
        ],
        compiler_params=pltpu.CompilerParams(
            collective_id=0, has_side_effects=True, vmem_limit_bytes=16 * 2**20
        ),
        cost_estimate=pl.CostEstimate(
            flops=0, bytes_accessed=64 * 2**20, transcendentals=0
        ),
        name="exchange",
    )(jnp.asarray(coef), brick_live, brick_data, brick_xy)

    places = places[:, :ngroup, :capacity].astype(jnp.int32).reshape(-1)
    tx = np.stack(x_tables(width))
    evens = (width // 4 + 1, width // 4)
    axis = 4 * np.sin(np.pi * np.arange(width) / width) ** 2
    along_x = np.zeros((2, tx.shape[1] // 4, 128), np.float32)
    for odd in range(2):
        along_x[odd, : evens[odd]] = axis[odd : width // 2 + 1 : 2][:, None]
    along_y = axis[None, :].astype(np.float32)

    ty = y_tables(width)
    tables = [jnp.asarray(t) for t in (along_x, along_y, tx, ty)]
    kx_count = width // 2 + 1
    out = jax.ShapeDtypeStruct((kx_count * width // 128 * ZLOC, 128), jnp.float32)
    scale = -1.0 / math.sqrt(width * width * total)
    results = pl.pallas_call(
        functools.partial(spectrum_kernel, nplane, ngroup, capacity, blocks, evens, scale),
        out_shape=(out, out),
        in_specs=[smem, smem] + [vmem] * 5,
        out_specs=(vmem, vmem),
        scratch_shapes=[
            pltpu.VMEM((blocks * blocks, 8, 128), jnp.float32),
            pltpu.VMEM((2, ZLOC, 2, width // 2, width), jnp.float32),
            pltpu.VMEM((2, 2 * ZLOC * along_x.shape[1], width), jnp.float32),
        ],
        compiler_params=pltpu.CompilerParams(vmem_limit_bytes=32 * 2**20),
        name="spectrum",
    )(places, along_z, arrived, *tables)

    def ordered(result):
        result = result.reshape(kx_count, width // 128, ZLOC, 128)
        return jnp.transpose(result, (2, 0, 1, 3)).reshape(ZLOC, kx_count, width)

    return tuple(ordered(result) for result in results)


def on_device(brick_data, brick_xy, brick_live):
    layers = brick_live.shape[0]
    slots, brick, area = brick_data.shape
    nplane, ngroup = lax.axis_size("zl"), lax.axis_size("zg")
    one_layer = layers == 1 and nplane * ZLOC == brick and brick == 16 and slots == 16
    fits = slots * nplane * ngroup * area * 2 * ZLOC * 4 <= 4 * 2**20
    if one_layer and fits and ngroup > 1:
        return on_device_once(brick_data, brick_xy, brick_live)
    return on_device_wide(brick_data, brick_xy, brick_live)


def solution(mesh):
    in_specs = (P(("zg", "zl"), None, None), P(None, ("zg", "zl")), P(None, ("zg", "zl")))
    out_specs = (P(("zg", "zl"), None, None), P(("zg", "zl"), None, None))
    return jax.shard_map(
        on_device, mesh=mesh, in_specs=in_specs, out_specs=out_specs, check_vma=False
    )
```

```python
import functools
import math

import jax
import jax.numpy as jnp
import ml_dtypes
import numpy as np
from jax import lax
from jax.experimental import pallas as pl
from jax.experimental.pallas import tpu as pltpu
from jax.sharding import PartitionSpec as P

PLANE = 512
ZLOC = 2


SCREEN = 0.25
HIGHEST = lax.Precision.HIGHEST
MESH = pl.DeviceIdType.MESH


def swapped(array, axis, distance):
    return lax.ppermute(array, axis, [(i, i ^ 1 << distance) for i in range(lax.axis_size(axis))])


def bit_count(number):
    return number.bit_length() - 1


def reverse_bits(values, digits):
    result = jnp.zeros_like(values)
    for digit in range(digits):
        result = result | (values >> digit & 1) << digits - 1 - digit
    return result


def dft_tables(length, freq_count):
    points = jnp.arange(length, dtype=jnp.int32)[:, None]
    freqs = jnp.arange(freq_count, dtype=jnp.int32)[None, :]
    angles = 2.0 * jnp.pi / length * (points * freqs % length).astype(jnp.float32)
    return (jnp.cos(angles), jnp.sin(angles))


def rotate(values, angles):
    cosine = jnp.cos(angles)
    sine = jnp.sin(angles)
    return (values[0] * cosine + values[1] * sine, values[1] * cosine - values[0] * sine)


def section_angles(z_rows, half, total):
    exponent = z_rows % half * (total // (2 * half))
    return (2.0 * jnp.pi / total * exponent.astype(jnp.float32))[:, None, None]


def combine_pair(mine, theirs, upper, angles):
    summed = (mine[0] + theirs[0], mine[1] + theirs[1])
    turned = rotate((theirs[0] - mine[0], theirs[1] - mine[1]), angles)
    return (jnp.where(upper, turned[0], summed[0]), jnp.where(upper, turned[1], summed[1]))


def local_sections(values, total):
    count = values[0].shape[0]
    shape = values[0].shape
    half = count // 2
    while half >= 1:
        split_real = values[0].reshape((count // (2 * half), 2, half) + shape[1:])
        split_imag = values[1].reshape((count // (2 * half), 2, half) + shape[1:])
        offsets = jnp.arange(half, dtype=jnp.int32) * (total // (2 * half))
        angles = (2.0 * jnp.pi / total * offsets.astype(jnp.float32))[None, :, None, None]
        summed_real = split_real[:, 0] + split_real[:, 1]
        summed_imag = split_imag[:, 0] + split_imag[:, 1]
        turned = rotate(
            (split_real[:, 0] - split_real[:, 1], split_imag[:, 0] - split_imag[:, 1]), angles
        )
        values = (
            jnp.stack([summed_real, turned[0]], axis=1).reshape(shape),
            jnp.stack([summed_imag, turned[1]], axis=1).reshape(shape),
        )
        half = half // 2
    return values


def on_device_wide(brick_data, brick_xy, brick_live):
    layers = brick_live.shape[0]
    capacity = brick_data.shape[0] // layers
    brick = brick_data.shape[1]
    area = brick_data.shape[2]
    zlocal = ZLOC
    per_layer = brick // zlocal
    ngroup = lax.axis_size("zg")
    nplane = lax.axis_size("zl")
    total = zlocal * ngroup * nplane
    width = PLANE
    blocks = width // brick
    kx_count = width // 2 + 1
    group_idx = lax.axis_index("zg")
    plane_idx = lax.axis_index("zl")
    live = (jnp.arange(capacity, dtype=jnp.int32)[None, :] < brick_live).astype(jnp.float32)
    masked = (
        brick_data.reshape(layers, capacity, per_layer, zlocal, area) * live[:, :, None, None, None]
    )
    outgoing = jnp.transpose(masked, (0, 2, 1, 3, 4)).reshape(
        layers * per_layer, capacity, zlocal, area
    )
    block_ids = (
        (brick_xy[1] * blocks + brick_xy[0]).astype(jnp.float32).reshape(layers, 1, capacity)
    )
    block_out = jnp.broadcast_to(block_ids, (layers, per_layer, capacity)).reshape(
        layers * per_layer, capacity
    )
    pieces, places = (
        lax.all_to_all(outgoing, "zl", split_axis=0, concat_axis=0, tiled=True),
        lax.all_to_all(block_out, "zl", split_axis=0, concat_axis=0, tiled=True),
    )
    slot_ids = places.astype(jnp.int32).reshape(-1)
    incoming = jnp.transpose(pieces, (2, 0, 1, 3)).reshape(zlocal, -1, area)
    blockgrid = (
        jnp.zeros((zlocal, blocks * blocks, area), jnp.float32).at[:, slot_ids, :].add(incoming)
    )
    blockgrid = blockgrid.reshape(zlocal, blocks, blocks, brick, brick)
    cos_x, sin_x = dft_tables(width, kx_count)
    cos_x = cos_x.reshape(blocks, brick, kx_count)
    sin_x = sin_x.reshape(blocks, brick, kx_count)
    first_real = jnp.einsum("zabuv,bvk->zkau", blockgrid, cos_x, precision=HIGHEST).reshape(
        zlocal * kx_count, width
    )
    first_imag = -jnp.einsum("zabuv,bvk->zkau", blockgrid, sin_x, precision=HIGHEST).reshape(
        zlocal * kx_count, width
    )
    cos_y, sin_y = dft_tables(width, width)
    second_real = jnp.dot(first_real, cos_y, precision=HIGHEST) + jnp.dot(
        first_imag, sin_y, precision=HIGHEST
    )
    second_imag = jnp.dot(first_imag, cos_y, precision=HIGHEST) - jnp.dot(
        first_real, sin_y, precision=HIGHEST
    )
    values = (
        second_real.reshape(zlocal, kx_count, width),
        second_imag.reshape(zlocal, kx_count, width),
    )
    device = group_idx * nplane + plane_idx
    z_rows = device * zlocal + jnp.arange(zlocal, dtype=jnp.int32)
    gbits = bit_count(ngroup)
    pbits = bit_count(nplane)
    for level in reversed(range(gbits)):
        half = zlocal * nplane * (1 << level)
        theirs = swapped((values[0], values[1]), "zg", level)
        upper = group_idx >> level & 1 == 1
        values = combine_pair(values, theirs, upper, section_angles(z_rows, half, total))
    plane_values = values
    for level in reversed(range(pbits)):
        half = zlocal * (1 << level)
        theirs = swapped((plane_values[0], plane_values[1]), "zl", level)
        upper = plane_idx >> level & 1 == 1
        plane_values = combine_pair(
            plane_values, theirs, upper, section_angles(z_rows, half, total)
        )
    plane_values = local_sections(plane_values, total)
    values = plane_values
    kz_rows = reverse_bits(z_rows, bit_count(total))
    along_z = 4.0 * jnp.sin(jnp.pi * kz_rows.astype(jnp.float32) / total) ** 2
    along_x = 4.0 * jnp.sin(jnp.pi * jnp.arange(kx_count, dtype=jnp.float32) / width) ** 2
    along_y = 4.0 * jnp.sin(jnp.pi * jnp.arange(width, dtype=jnp.float32) / width) ** 2
    denom = along_z[:, None, None] + along_x[None, :, None] + along_y[None, None, :] + SCREEN
    factor = -(1.0 / math.sqrt(width * width * total)) / denom
    return (values[0] * factor, values[1] * factor)


def kz_of(row, total):
    digits = bit_count(total)
    return sum(
        lax.rem(lax.div(row, jnp.int32(1 << d)), jnp.int32(2)) * (1 << digits - 1 - d)
        for d in range(digits)
    )


def reversed_bits(row, digits):
    return sum((row >> d & 1) << digits - 1 - d for d in range(digits))


def transposed_blocks(tiles, width):
    tiles = list(tiles)
    block = lax.broadcasted_iota(jnp.int32, tiles[0].shape, tiles[0].ndim - 1) // width
    lanes = tiles[0].shape[-1]
    step = len(tiles) // 2
    while step:
        high = (block & step) != 0
        for i in range(len(tiles)):
            if not i & step:
                low, up = tiles[i], tiles[i + step]
                if 2 * step * width == lanes:
                    swapped_part = pltpu.roll(jnp.where(high, low, up), step * width, low.ndim - 1)
                    tiles[i] = jnp.where(high, swapped_part, low)
                    tiles[i + step] = jnp.where(high, up, swapped_part)
                    continue
                tiles[i] = jnp.where(high, pltpu.roll(up, step * width, low.ndim - 1), low)
                tiles[i + step] = jnp.where(
                    high, up, pltpu.roll(low, lanes - step * width, low.ndim - 1)
                )
        step //= 2
    return tiles


def exchange_kernel(
    ngroup, nplane, capacity, blocks,
    coef, live, bricks, xy, out, out_places, data, raw, ready, spots, zsend, zrecv, psend, precv,
    ssend, srecv, loaded,
):
    group, plane = lax.axis_index("zg"), lax.axis_index("zl")
    quads = capacity // 4
    depth = data.shape[1]
    load = pltpu.make_async_copy(bricks, data, loaded)
    load.start()
    barrier = pltpu.get_barrier_semaphore()

    def greet(g, p):
        pl.semaphore_signal(barrier, inc=1, device_id=(g, p), device_id_type=MESH)

    for k in range(1, nplane):
        greet(group, lax.rem(plane + k, nplane))
    pl.when(group > 0)(lambda: greet(group - 1, plane))
    pl.when(group < ngroup - 1)(lambda: greet(group + 1, plane))
    ends = jnp.where(group > 0, 1, 0) + jnp.where(group < ngroup - 1, 1, 0)
    pl.semaphore_wait(barrier, nplane - 1 + ends)

    def along(side, t):
        chunk = jnp.where(side == 0, group - t, group + t)
        target = jnp.where(side == 0, group + 1, group - 1)
        inside = (chunk >= 0) & (chunk < ngroup) & (target >= 0) & (target < ngroup)
        safe = jnp.clip(chunk, 0, ngroup - 1)
        copy = pltpu.make_async_remote_copy(
            src_ref=raw.at[safe],
            dst_ref=raw.at[safe],
            send_sem=zsend.at[side, t],
            recv_sem=zrecv.at[side, t],
            device_id=(jnp.clip(target, 0, ngroup - 1), plane),
            device_id_type=MESH,
        )
        return inside, copy

    def to_peer(chunk, k):
        return pltpu.make_async_remote_copy(
            src_ref=ready.at[chunk, k],
            dst_ref=out.at[plane, chunk],
            send_sem=psend.at[chunk, k],
            recv_sem=precv.at[chunk, k],
            device_id=(group, lax.rem(plane + k, nplane)),
            device_id_type=MESH,
        )

    def keep(chunk):
        return pltpu.make_async_copy(ready.at[chunk, 0], out.at[plane, chunk], psend.at[chunk, 0])

    def sums(chunk, peer, target):
        first = ((group * ngroup + chunk) * nplane + peer) * 2 * depth
        real = [coef[first + 2 * z] for z in range(depth)]
        imag = [coef[first + 2 * z + 1] for z in range(depth)]
        for quad in range(quads):
            parts = []
            for table in (real, imag):
                for parity in range(2):
                    summed = None
                    for z in range(parity, depth, 2):
                        term = raw[chunk, pl.ds((quad * depth + z) * 8, 8)] * table[z]
                        summed = term if summed is None else summed + term
                    parts.append(summed)
            tiles = (parts[0] + parts[1], parts[2] + parts[3], parts[0] - parts[1], parts[2] - parts[3])
            for i, tile in enumerate(transposed_blocks(tiles, 32)):
                target[quad * 4 + i] = tile

    def share(chunk):
        def one(k, carry):
            sums(chunk, lax.rem(plane + k, nplane), ready.at[chunk, k])
            to_peer(chunk, k).start()
            return carry

        lax.fori_loop(1, nplane, one, 0)
        sums(chunk, plane, ready.at[chunk, 0])
        keep(chunk).start()

    load.wait()
    for quad in range(quads):
        for z in range(0, depth, 8):
            for half in range(2):
                tiles = []
                for slot in range(quad * 4, quad * 4 + 4):
                    alive = jnp.where(slot < live[0, 0], 1.0, 0.0)
                    tiles.append(data[slot, z : z + 8, half * 128 : half * 128 + 128] * alive)
                for i, tile in enumerate(transposed_blocks(tiles, 32)):
                    row = (quad * depth + z) * 8 + half * 4 + i
                    raw[group, pl.ds(row, 8, stride=8), :] = tile
    place = (xy[1:2, :] * blocks + xy[0:1, :]).astype(jnp.float32)
    place = jnp.concatenate([place, jnp.zeros((1, 128 - capacity), jnp.float32)], axis=1)
    raw[group, pl.ds(quads * depth * 8, 8)] = jnp.broadcast_to(place, (8, 128))
    for side in range(2):
        inside, copy = along(side, 0)
        pl.when(inside)(copy.start)
    share(group)

    def arrival(i, carry):
        t, side = i // 2, lax.rem(i, 2)
        chunk = jnp.where(side == 0, group - 1 - t, group + 1 + t)

        @pl.when((chunk >= 0) & (chunk < ngroup))
        def _():
            safe = jnp.clip(chunk, 0, ngroup - 1)
            pltpu.make_async_remote_copy(
                src_ref=raw.at[safe],
                dst_ref=raw.at[safe],
                send_sem=zsend.at[side, t],
                recv_sem=zrecv.at[side, t],
                device_id=(group, plane),
                device_id_type=MESH,
            ).wait_recv()

            @pl.when(t < ngroup - 2)
            def _():
                inside, copy = along(side, jnp.minimum(t + 1, ngroup - 2))
                pl.when(inside)(copy.start)

            share(safe)

        return carry

    lax.fori_loop(0, 2 * (ngroup - 1), arrival, 0)

    spots[...] = jnp.zeros_like(spots)
    for chunk in range(ngroup):
        spots[chunk : chunk + 1] = raw[chunk, pl.ds(quads * depth * 8, 1)].astype(jnp.int32)
    own_spots = pltpu.make_async_copy(spots, out_places.at[plane], ssend.at[0])
    own_spots.start()

    def spots_to(k):
        return pltpu.make_async_remote_copy(
            src_ref=spots,
            dst_ref=out_places.at[plane],
            send_sem=ssend.at[k],
            recv_sem=srecv.at[k],
            device_id=(group, lax.rem(plane + k, nplane)),
            device_id_type=MESH,
        )

    for k in range(1, nplane):
        spots_to(k).start()

    for side in range(2):
        for t in range(ngroup - 1):
            inside, copy = along(side, t)
            pl.when(inside)(copy.wait_send)

    def finish(i, carry):
        copy = to_peer(i // (nplane - 1), 1 + lax.rem(i, nplane - 1))
        copy.wait_send()
        copy.wait_recv()
        return carry

    lax.fori_loop(0, ngroup * (nplane - 1), finish, 0)
    own_spots.wait()
    for chunk in range(ngroup):
        keep(chunk).wait()
    for k in range(1, nplane):
        spots_to(k).wait_send()
        spots_to(k).wait_recv()


def split(values):
    high = values.astype(jnp.bfloat16)
    return high, (values - high.astype(jnp.float32)).astype(jnp.bfloat16)


def spectrum_kernel(
    nplane, ngroup, capacity, blocks, evens, total, scale,
    places_hbm, bricks_hbm, tx_hbm, ty_hbm, out_real, out_imag,
    grid, rows, lines, places, bricks, tx, ty, loaded,
):
    half = rows.shape[-1] // 2
    width = rows.shape[-1]
    device = lax.axis_index("zg") * nplane + lax.axis_index("zl")
    loads = [pltpu.make_async_copy(places_hbm, places, loaded.at[0])]
    for chunk in range(ngroup):
        loads.append(
            pltpu.make_async_copy(
                bricks_hbm.at[:, chunk], bricks.at[:, chunk], loaded.at[1 + chunk]
            )
        )
    loads.append(pltpu.make_async_copy(tx_hbm, tx, loaded.at[1 + ngroup]))
    loads.append(pltpu.make_async_copy(ty_hbm, ty, loaded.at[2 + ngroup]))
    for load in loads:
        load.start()

    def clear(i, carry):
        grid[pl.ds(i * 32, 32)] = jnp.zeros((32,) + grid.shape[1:], jnp.float32)
        return carry

    lax.fori_loop(0, grid.shape[0] // 32, clear, 0)

    def place(chunk, pair):
        slots = [(pair * 2 + n, c) for n in range(2) for c in range(capacity)]
        ids = [places[source, chunk, c] for source, c in slots]
        values = [grid[at] + bricks[source, chunk, c] for at, (source, c) in zip(ids, slots)]
        for at, value in zip(ids, values):
            grid[at] = value

    loads[0].wait()
    for chunk in range(ngroup):
        loads[1 + chunk].wait()
        lax.fori_loop(0, nplane // 2, lambda pair, carry: (place(chunk, pair), carry)[1], 0)

    batch = 2

    def arrange(step, carry):
        for h in range(2):
            tiles = []
            for i in range(8):
                first, second = (
                    jnp.stack([grid[(step * batch + n) * blocks + at + i] for n in range(batch)])
                    for at in (h * 8, h * 8 + 16)
                )
                tiles.append((first + second, first - second))
            for side in range(2):
                lines_of = transposed_blocks([pair[side] for pair in tiles], 16)
                for j in range(8):
                    kz, ri, parity = j // 4, j // 2 % 2, j % 2
                    lanes = pl.ds(ri * half + h * 128, 128)
                    at = pl.ds(pl.multiple_of(step * batch * 8, batch * 8), batch * 8)
                    rows[side, kz, parity, at, lanes] = lines_of[j].reshape(-1, 128)
        return carry

    lax.fori_loop(0, blocks // batch, arrange, 0)
    loads[1 + ngroup].wait()

    def product(a, b, dims):
        return lax.dot_general(a, b, (dims, ((), ())), preferred_element_type=jnp.float32)

    padded = tx.shape[1] // 4
    for parity in range(2):
        for odd in range(2):
            table = tx.at[odd]
            count = table.shape[0] // 2
            for kz in range(ZLOC):
                high, low = split(rows[odd, kz, parity])
                both = product(table[...], high, ((1,), (1,)))
                first = both[:count] + (both[count:] + product(table[:count], low, ((1,), (1,))))
                at = pl.ds((odd * ZLOC + kz) * padded, padded)
                lines[parity, at, :half] = first[:padded]
                lines[parity, at, half:] = first[padded:]

    loads[2 + ngroup].wait()
    results = []
    for parity in range(2):
        high, low = split(lines[parity])
        count = high.shape[0]
        both = product(jnp.concatenate([high, low], axis=0), ty[parity, 0], ((1,), (0,)))
        results.append(both[:count] + (both[count:] + product(high, ty[parity, 1], ((1,), (0,)))))
    lines[0] = results[0] + results[1]
    lines[1] = results[0] - results[1]

    def along(index, count):
        return 4.0 * jnp.sin(jnp.pi * index.astype(jnp.float32) / count) ** 2

    tiles = width // 128
    for odd in range(2):
        down = lax.broadcasted_iota(jnp.int32, (padded, 1), 0) * 2 + odd
        along_x = jnp.broadcast_to(along(down, width), (padded, 128))
        for kz in range(ZLOC):
            turn = jnp.full((8, 128), kz_of(device * ZLOC + kz, total), jnp.int32)
            along_z = along(turn, total)[:1]
            at = pl.ds((odd * ZLOC + kz) * padded, padded)
            for tile in range(tiles):
                across = lax.broadcasted_iota(jnp.int32, (8, 128), 1) + tile * 128
                denom = along_z + along_x + along(across, width)[:1] + SCREEN
                factor = scale / denom
                sign, lane = tile // (tiles // 2), tile % (tiles // 2) * 128
                for out, start in ((out_real, 0), (out_imag, half)):
                    value = lines[sign, at, pl.ds(start + lane, 128)] * factor
                    row = (odd * tiles + tile) * ZLOC + kz
                    out[pl.ds(row, evens[odd], stride=2 * tiles * ZLOC), :] = value[: evens[odd]]


def parted(table):
    high = table.astype(ml_dtypes.bfloat16)
    low = (table - high.astype(np.float64)).astype(ml_dtypes.bfloat16)
    return high, low


def x_tables(width):
    tables = []
    for odd in range(2):
        padded = -(-(width // 4 + 1) // 8) * 8
        kx = 2 * np.arange(padded)[:, None] + odd
        angles = 2 * np.pi / width * (kx * np.arange(width // 2)[None, :] % width)
        cosine, sine = np.cos(angles), np.sin(angles)
        tables.append(np.concatenate(parted(np.block([[cosine, sine], [-sine, cosine]]))))
    return tables


def y_tables(width):
    tables = []
    for parity in range(2):
        y = 2 * np.arange(width // 2)[:, None] + parity
        angles = 2 * np.pi / width * (y * np.arange(width // 2)[None, :] % width)
        cosine, sine = np.cos(angles), np.sin(angles)
        tables.append(np.stack(parted(np.block([[cosine, -sine], [sine, cosine]]))))
    return np.stack(tables)


def on_device_once(brick_data, brick_xy, brick_live):
    capacity, brick, area = brick_data.shape
    ngroup, nplane = lax.axis_size("zg"), lax.axis_size("zl")
    total = ZLOC * ngroup * nplane
    width = PLANE
    blocks = width // brick
    quads = capacity // 4
    kz = np.array([reversed_bits(row, bit_count(total)) for row in range(0, total, ZLOC)])
    angles = kz.reshape(ngroup, 1, nplane, 1) * np.arange(ngroup * brick).reshape(-1, 1, brick)
    angles = 2 * np.pi / total * (angles % total)
    coef = np.stack([np.cos(angles), -np.sin(angles)], axis=-1).astype(np.float32).reshape(-1)

    vmem = pl.BlockSpec(memory_space=pltpu.VMEM)
    smem = pl.BlockSpec(memory_space=pltpu.SMEM)
    anywhere = pl.BlockSpec(memory_space=pl.ANY)
    arrived, places = pl.pallas_call(
        functools.partial(exchange_kernel, ngroup, nplane, capacity, blocks),
        out_shape=(
            jax.ShapeDtypeStruct((nplane, ngroup, capacity, 8, 128), jnp.float32),
            jax.ShapeDtypeStruct((nplane, 8, 128), jnp.int32),
        ),
        in_specs=[smem, smem, anywhere, vmem],
        out_specs=(anywhere, anywhere),
        scratch_shapes=[
            pltpu.VMEM(brick_data.shape, jnp.float32),
            pltpu.VMEM((ngroup, (quads * brick + 1) * 8, 128), jnp.float32),
            pltpu.VMEM((ngroup, nplane, capacity, 8, 128), jnp.float32),
            pltpu.VMEM((8, 128), jnp.int32),
            pltpu.SemaphoreType.DMA((2, ngroup - 1)),
            pltpu.SemaphoreType.DMA((2, ngroup - 1)),
            pltpu.SemaphoreType.DMA((ngroup, nplane)),
            pltpu.SemaphoreType.DMA((ngroup, nplane)),
            pltpu.SemaphoreType.DMA((nplane,)),
            pltpu.SemaphoreType.DMA((nplane,)),
            pltpu.SemaphoreType.DMA,
        ],
        compiler_params=pltpu.CompilerParams(
            collective_id=0, has_side_effects=True, vmem_limit_bytes=60 * 2**20
        ),
        name="exchange",
    )(jnp.asarray(coef), brick_live, brick_data, brick_xy)

    tx = np.stack(x_tables(width))
    evens = (width // 4 + 1, width // 4)
    ty = y_tables(width)
    kx_count = width // 2 + 1
    out = jax.ShapeDtypeStruct((kx_count * width // 128 * ZLOC, 128), jnp.float32)
    scale = -1.0 / math.sqrt(width * width * total)
    results = pl.pallas_call(
        functools.partial(spectrum_kernel, nplane, ngroup, capacity, blocks, evens, total, scale),
        out_shape=(out, out),
        in_specs=[anywhere] * 4,
        out_specs=(vmem, vmem),
        scratch_shapes=[
            pltpu.VMEM((blocks * blocks, 8, 128), jnp.float32),
            pltpu.VMEM((2, ZLOC, 2, width // 2, width), jnp.float32),
            pltpu.VMEM((2, ZLOC * tx.shape[1] // 2, width), jnp.float32),
            pltpu.SMEM(places.shape, jnp.int32),
            pltpu.VMEM(arrived.shape, jnp.float32),
            pltpu.VMEM(tx.shape, tx.dtype),
            pltpu.VMEM(ty.shape, ty.dtype),
            pltpu.SemaphoreType.DMA((3 + ngroup,)),
        ],
        compiler_params=pltpu.CompilerParams(vmem_limit_bytes=60 * 2**20),
        name="spectrum",
    )(places, arrived, jnp.asarray(tx), jnp.asarray(ty))

    def ordered(result):
        result = result.reshape(kx_count, width // 128, ZLOC, 128)
        return jnp.transpose(result, (2, 0, 1, 3)).reshape(ZLOC, kx_count, width)

    return tuple(ordered(result) for result in results)


def on_device(brick_data, brick_xy, brick_live):
    layers = brick_live.shape[0]
    slots, brick, area = brick_data.shape
    nplane, ngroup = lax.axis_size("zl"), lax.axis_size("zg")
    one_layer = layers == 1 and nplane * ZLOC == brick and brick == 16 and slots == 16
    fits = slots * nplane * ngroup * area * 2 * ZLOC * 4 <= 4 * 2**20
    if one_layer and fits and ngroup > 1:
        return on_device_once(brick_data, brick_xy, brick_live)
    return on_device_wide(brick_data, brick_xy, brick_live)


def solution(mesh):
    in_specs = (P(("zg", "zl"), None, None), P(None, ("zg", "zl")), P(None, ("zg", "zl")))
    out_specs = (P(("zg", "zl"), None, None), P(("zg", "zl"), None, None))
    return jax.shard_map(
        on_device, mesh=mesh, in_specs=in_specs, out_specs=out_specs, check_vma=False
    )
```

```python
import functools
import math

import jax
import jax.numpy as jnp
import ml_dtypes
import numpy as np
from jax import lax
from jax.experimental import pallas as pl
from jax.experimental.pallas import tpu as pltpu
from jax.sharding import PartitionSpec as P

PLANE = 512
ZLOC = 2


SCREEN = 0.25
HIGHEST = lax.Precision.HIGHEST
MESH = pl.DeviceIdType.MESH


def swapped(array, axis, distance):
    return lax.ppermute(array, axis, [(i, i ^ 1 << distance) for i in range(lax.axis_size(axis))])


def bit_count(number):
    return number.bit_length() - 1


def reverse_bits(values, digits):
    result = jnp.zeros_like(values)
    for digit in range(digits):
        result = result | (values >> digit & 1) << digits - 1 - digit
    return result


def dft_tables(length, freq_count):
    points = jnp.arange(length, dtype=jnp.int32)[:, None]
    freqs = jnp.arange(freq_count, dtype=jnp.int32)[None, :]
    angles = 2.0 * jnp.pi / length * (points * freqs % length).astype(jnp.float32)
    return (jnp.cos(angles), jnp.sin(angles))


def rotate(values, angles):
    cosine = jnp.cos(angles)
    sine = jnp.sin(angles)
    return (values[0] * cosine + values[1] * sine, values[1] * cosine - values[0] * sine)


def section_angles(z_rows, half, total):
    exponent = z_rows % half * (total // (2 * half))
    return (2.0 * jnp.pi / total * exponent.astype(jnp.float32))[:, None, None]


def combine_pair(mine, theirs, upper, angles):
    summed = (mine[0] + theirs[0], mine[1] + theirs[1])
    turned = rotate((theirs[0] - mine[0], theirs[1] - mine[1]), angles)
    return (jnp.where(upper, turned[0], summed[0]), jnp.where(upper, turned[1], summed[1]))


def local_sections(values, total):
    count = values[0].shape[0]
    shape = values[0].shape
    half = count // 2
    while half >= 1:
        split_real = values[0].reshape((count // (2 * half), 2, half) + shape[1:])
        split_imag = values[1].reshape((count // (2 * half), 2, half) + shape[1:])
        offsets = jnp.arange(half, dtype=jnp.int32) * (total // (2 * half))
        angles = (2.0 * jnp.pi / total * offsets.astype(jnp.float32))[None, :, None, None]
        summed_real = split_real[:, 0] + split_real[:, 1]
        summed_imag = split_imag[:, 0] + split_imag[:, 1]
        turned = rotate(
            (split_real[:, 0] - split_real[:, 1], split_imag[:, 0] - split_imag[:, 1]), angles
        )
        values = (
            jnp.stack([summed_real, turned[0]], axis=1).reshape(shape),
            jnp.stack([summed_imag, turned[1]], axis=1).reshape(shape),
        )
        half = half // 2
    return values


def on_device_wide(brick_data, brick_xy, brick_live):
    layers = brick_live.shape[0]
    capacity = brick_data.shape[0] // layers
    brick = brick_data.shape[1]
    area = brick_data.shape[2]
    zlocal = ZLOC
    per_layer = brick // zlocal
    ngroup = lax.axis_size("zg")
    nplane = lax.axis_size("zl")
    total = zlocal * ngroup * nplane
    width = PLANE
    blocks = width // brick
    kx_count = width // 2 + 1
    group_idx = lax.axis_index("zg")
    plane_idx = lax.axis_index("zl")
    live = (jnp.arange(capacity, dtype=jnp.int32)[None, :] < brick_live).astype(jnp.float32)
    masked = (
        brick_data.reshape(layers, capacity, per_layer, zlocal, area) * live[:, :, None, None, None]
    )
    outgoing = jnp.transpose(masked, (0, 2, 1, 3, 4)).reshape(
        layers * per_layer, capacity, zlocal, area
    )
    block_ids = (
        (brick_xy[1] * blocks + brick_xy[0]).astype(jnp.float32).reshape(layers, 1, capacity)
    )
    block_out = jnp.broadcast_to(block_ids, (layers, per_layer, capacity)).reshape(
        layers * per_layer, capacity
    )
    pieces, places = (
        lax.all_to_all(outgoing, "zl", split_axis=0, concat_axis=0, tiled=True),
        lax.all_to_all(block_out, "zl", split_axis=0, concat_axis=0, tiled=True),
    )
    slot_ids = places.astype(jnp.int32).reshape(-1)
    incoming = jnp.transpose(pieces, (2, 0, 1, 3)).reshape(zlocal, -1, area)
    blockgrid = (
        jnp.zeros((zlocal, blocks * blocks, area), jnp.float32).at[:, slot_ids, :].add(incoming)
    )
    blockgrid = blockgrid.reshape(zlocal, blocks, blocks, brick, brick)
    cos_x, sin_x = dft_tables(width, kx_count)
    cos_x = cos_x.reshape(blocks, brick, kx_count)
    sin_x = sin_x.reshape(blocks, brick, kx_count)
    first_real = jnp.einsum("zabuv,bvk->zkau", blockgrid, cos_x, precision=HIGHEST).reshape(
        zlocal * kx_count, width
    )
    first_imag = -jnp.einsum("zabuv,bvk->zkau", blockgrid, sin_x, precision=HIGHEST).reshape(
        zlocal * kx_count, width
    )
    cos_y, sin_y = dft_tables(width, width)
    second_real = jnp.dot(first_real, cos_y, precision=HIGHEST) + jnp.dot(
        first_imag, sin_y, precision=HIGHEST
    )
    second_imag = jnp.dot(first_imag, cos_y, precision=HIGHEST) - jnp.dot(
        first_real, sin_y, precision=HIGHEST
    )
    values = (
        second_real.reshape(zlocal, kx_count, width),
        second_imag.reshape(zlocal, kx_count, width),
    )
    device = group_idx * nplane + plane_idx
    z_rows = device * zlocal + jnp.arange(zlocal, dtype=jnp.int32)
    gbits = bit_count(ngroup)
    pbits = bit_count(nplane)
    for level in reversed(range(gbits)):
        half = zlocal * nplane * (1 << level)
        theirs = swapped((values[0], values[1]), "zg", level)
        upper = group_idx >> level & 1 == 1
        values = combine_pair(values, theirs, upper, section_angles(z_rows, half, total))
    plane_values = values
    for level in reversed(range(pbits)):
        half = zlocal * (1 << level)
        theirs = swapped((plane_values[0], plane_values[1]), "zl", level)
        upper = plane_idx >> level & 1 == 1
        plane_values = combine_pair(
            plane_values, theirs, upper, section_angles(z_rows, half, total)
        )
    plane_values = local_sections(plane_values, total)
    values = plane_values
    kz_rows = reverse_bits(z_rows, bit_count(total))
    along_z = 4.0 * jnp.sin(jnp.pi * kz_rows.astype(jnp.float32) / total) ** 2
    along_x = 4.0 * jnp.sin(jnp.pi * jnp.arange(kx_count, dtype=jnp.float32) / width) ** 2
    along_y = 4.0 * jnp.sin(jnp.pi * jnp.arange(width, dtype=jnp.float32) / width) ** 2
    denom = along_z[:, None, None] + along_x[None, :, None] + along_y[None, None, :] + SCREEN
    factor = -(1.0 / math.sqrt(width * width * total)) / denom
    return (values[0] * factor, values[1] * factor)


def kz_of(row, total):
    digits = bit_count(total)
    return sum(
        lax.rem(lax.div(row, jnp.int32(1 << d)), jnp.int32(2)) * (1 << digits - 1 - d)
        for d in range(digits)
    )


def reversed_bits(row, digits):
    return sum((row >> d & 1) << digits - 1 - d for d in range(digits))


def transposed_blocks(tiles, width):
    tiles = list(tiles)
    block = lax.broadcasted_iota(jnp.int32, tiles[0].shape, tiles[0].ndim - 1) // width
    lanes = tiles[0].shape[-1]
    step = len(tiles) // 2
    while step:
        high = (block & step) != 0
        for i in range(len(tiles)):
            if not i & step:
                low, up = tiles[i], tiles[i + step]
                if 2 * step * width == lanes:
                    swapped_part = pltpu.roll(jnp.where(high, low, up), step * width, low.ndim - 1)
                    tiles[i] = jnp.where(high, swapped_part, low)
                    tiles[i + step] = jnp.where(high, up, swapped_part)
                    continue
                tiles[i] = jnp.where(high, pltpu.roll(up, step * width, low.ndim - 1), low)
                tiles[i + step] = jnp.where(
                    high, up, pltpu.roll(low, lanes - step * width, low.ndim - 1)
                )
        step //= 2
    return tiles


def exchange_kernel(
    ngroup, nplane, capacity, blocks,
    coef, live, bricks, xy, out, out_places, data, raw, ready, spots, zsend, zrecv, psend, precv,
    ssend, srecv, loaded,
):
    group, plane = lax.axis_index("zg"), lax.axis_index("zl")
    quads = capacity // 4
    depth = data.shape[1]
    load = pltpu.make_async_copy(bricks, data, loaded)
    load.start()
    barrier = pltpu.get_barrier_semaphore()

    def greet(g, p):
        pl.semaphore_signal(barrier, inc=1, device_id=(g, p), device_id_type=MESH)

    for k in range(1, nplane):
        greet(group, lax.rem(plane + k, nplane))
    pl.when(group > 0)(lambda: greet(group - 1, plane))
    pl.when(group < ngroup - 1)(lambda: greet(group + 1, plane))
    ends = jnp.where(group > 0, 1, 0) + jnp.where(group < ngroup - 1, 1, 0)
    pl.semaphore_wait(barrier, nplane - 1 + ends)

    def along(side, t):
        chunk = jnp.where(side == 0, group - t, group + t)
        target = jnp.where(side == 0, group + 1, group - 1)
        inside = (chunk >= 0) & (chunk < ngroup) & (target >= 0) & (target < ngroup)
        safe = jnp.clip(chunk, 0, ngroup - 1)
        copy = pltpu.make_async_remote_copy(
            src_ref=raw.at[safe],
            dst_ref=raw.at[safe],
            send_sem=zsend.at[side, t],
            recv_sem=zrecv.at[side, t],
            device_id=(jnp.clip(target, 0, ngroup - 1), plane),
            device_id_type=MESH,
        )
        return inside, copy

    def to_peer(chunk, k):
        return pltpu.make_async_remote_copy(
            src_ref=ready.at[chunk, k],
            dst_ref=out.at[plane, chunk],
            send_sem=psend.at[chunk, k],
            recv_sem=precv.at[chunk, k],
            device_id=(group, lax.rem(plane + k, nplane)),
            device_id_type=MESH,
        )

    def keep(chunk):
        return pltpu.make_async_copy(ready.at[chunk, 0], out.at[plane, chunk], psend.at[chunk, 0])

    def sums(chunk, peer, target):
        first = ((group * ngroup + chunk) * nplane + peer) * 2 * depth
        real = [coef[first + 2 * z] for z in range(depth)]
        imag = [coef[first + 2 * z + 1] for z in range(depth)]
        for quad in range(quads):
            parts = []
            for table in (real, imag):
                for parity in range(2):
                    summed = None
                    for z in range(parity, depth, 2):
                        term = raw[chunk, pl.ds((quad * depth + z) * 8, 8)] * table[z]
                        summed = term if summed is None else summed + term
                    parts.append(summed)
            tiles = (parts[0] + parts[1], parts[2] + parts[3], parts[0] - parts[1], parts[2] - parts[3])
            for i, tile in enumerate(transposed_blocks(tiles, 32)):
                target[quad * 4 + i] = tile

    def share(chunk):
        def one(k, carry):
            sums(chunk, lax.rem(plane + k, nplane), ready.at[chunk, k])
            to_peer(chunk, k).start()
            return carry

        lax.fori_loop(1, nplane, one, 0)
        sums(chunk, plane, ready.at[chunk, 0])
        keep(chunk).start()

    load.wait()
    for quad in range(quads):
        for z in range(0, depth, 8):
            for half in range(2):
                tiles = []
                for slot in range(quad * 4, quad * 4 + 4):
                    alive = jnp.where(slot < live[0, 0], 1.0, 0.0)
                    tiles.append(data[slot, z : z + 8, half * 128 : half * 128 + 128] * alive)
                for i, tile in enumerate(transposed_blocks(tiles, 32)):
                    row = (quad * depth + z) * 8 + half * 4 + i
                    raw[group, pl.ds(row, 8, stride=8), :] = tile
    place = (xy[1:2, :] * blocks + xy[0:1, :]).astype(jnp.float32)
    place = jnp.concatenate([place, jnp.zeros((1, 128 - capacity), jnp.float32)], axis=1)
    raw[group, pl.ds(quads * depth * 8, 8)] = jnp.broadcast_to(place, (8, 128))
    for side in range(2):
        inside, copy = along(side, 0)
        pl.when(inside)(copy.start)
    share(group)

    def arrival(i, carry):
        t, side = i // 2, lax.rem(i, 2)
        chunk = jnp.where(side == 0, group - 1 - t, group + 1 + t)

        @pl.when((chunk >= 0) & (chunk < ngroup))
        def _():
            safe = jnp.clip(chunk, 0, ngroup - 1)
            pltpu.make_async_remote_copy(
                src_ref=raw.at[safe],
                dst_ref=raw.at[safe],
                send_sem=zsend.at[side, t],
                recv_sem=zrecv.at[side, t],
                device_id=(group, plane),
                device_id_type=MESH,
            ).wait_recv()

            @pl.when(t < ngroup - 2)
            def _():
                inside, copy = along(side, jnp.minimum(t + 1, ngroup - 2))
                pl.when(inside)(copy.start)

            share(safe)

        return carry

    lax.fori_loop(0, 2 * (ngroup - 1), arrival, 0)

    spots[...] = jnp.zeros_like(spots)
    for chunk in range(ngroup):
        spots[chunk : chunk + 1] = raw[chunk, pl.ds(quads * depth * 8, 1)].astype(jnp.int32)
    own_spots = pltpu.make_async_copy(spots, out_places.at[plane], ssend.at[0])
    own_spots.start()

    def spots_to(k):
        return pltpu.make_async_remote_copy(
            src_ref=spots,
            dst_ref=out_places.at[plane],
            send_sem=ssend.at[k],
            recv_sem=srecv.at[k],
            device_id=(group, lax.rem(plane + k, nplane)),
            device_id_type=MESH,
        )

    for k in range(1, nplane):
        spots_to(k).start()

    for side in range(2):
        for t in range(ngroup - 1):
            inside, copy = along(side, t)
            pl.when(inside)(copy.wait_send)

    own_spots.wait()
    for k in range(1, nplane):
        spots_to(k).wait_send()
        spots_to(k).wait_recv()

    def finish(chunk):
        keep(chunk).wait()

        def one(k, carry):
            copy = to_peer(chunk, k)
            copy.wait_send()
            copy.wait_recv()
            return carry

        lax.fori_loop(1, nplane, one, 0)

    finish(group)

    def farther(i, carry):
        t, side = i // 2, lax.rem(i, 2)
        chunk = jnp.where(side == 0, group - 1 - t, group + 1 + t)
        pl.when((chunk >= 0) & (chunk < ngroup))(lambda: finish(jnp.clip(chunk, 0, ngroup - 1)))
        return carry

    lax.fori_loop(0, 2 * (ngroup - 1), farther, 0)


def split(values):
    high = values.astype(jnp.bfloat16)
    return high, (values - high.astype(jnp.float32)).astype(jnp.bfloat16)


def spectrum_kernel(
    nplane, ngroup, capacity, blocks, evens, total, scale,
    places_hbm, bricks_hbm, tx_hbm, ty_hbm, real_hbm, imag_hbm,
    grid, rows, lines, places, bricks, tx, ty, out_real, out_imag, loaded, stored,
):
    half = rows.shape[-1] // 2
    width = rows.shape[-1]
    device = lax.axis_index("zg") * nplane + lax.axis_index("zl")
    loads = [pltpu.make_async_copy(places_hbm, places, loaded.at[0])]
    for chunk in range(ngroup):
        loads.append(
            pltpu.make_async_copy(
                bricks_hbm.at[:, chunk], bricks.at[:, chunk], loaded.at[1 + chunk]
            )
        )
    loads.append(pltpu.make_async_copy(tx_hbm, tx, loaded.at[1 + ngroup]))
    loads.append(pltpu.make_async_copy(ty_hbm, ty, loaded.at[2 + ngroup]))
    for load in loads:
        load.start()

    def clear(i, carry):
        grid[pl.ds(i * 32, 32)] = jnp.zeros((32,) + grid.shape[1:], jnp.float32)
        return carry

    lax.fori_loop(0, grid.shape[0] // 32, clear, 0)

    def place(chunk, pair):
        slots = [(pair * 2 + n, c) for n in range(2) for c in range(capacity)]
        ids = [places[source, chunk, c] for source, c in slots]
        values = [grid[at] + bricks[source, chunk, c] for at, (source, c) in zip(ids, slots)]
        for at, value in zip(ids, values):
            grid[at] = value

    loads[0].wait()
    for chunk in range(ngroup):
        loads[1 + chunk].wait()
        lax.fori_loop(0, nplane // 2, lambda pair, carry: (place(chunk, pair), carry)[1], 0)

    batch = 2

    def arrange(step, carry):
        for h in range(2):
            tiles = []
            for i in range(8):
                first, second = (
                    jnp.stack([grid[(step * batch + n) * blocks + at + i] for n in range(batch)])
                    for at in (h * 8, h * 8 + 16)
                )
                tiles.append((first + second, first - second))
            for side in range(2):
                lines_of = transposed_blocks([pair[side] for pair in tiles], 16)
                for j in range(8):
                    kz, ri, parity = j // 4, j // 2 % 2, j % 2
                    lanes = pl.ds(ri * half + h * 128, 128)
                    at = pl.ds(pl.multiple_of(step * batch * 8, batch * 8), batch * 8)
                    rows[side, kz, parity, at, lanes] = lines_of[j].reshape(-1, 128)
        return carry

    lax.fori_loop(0, blocks // batch, arrange, 0)
    loads[1 + ngroup].wait()

    def product(a, b, dims):
        return lax.dot_general(a, b, (dims, ((), ())), preferred_element_type=jnp.float32)

    padded = tx.shape[1] // 4
    for parity in range(2):
        for odd in range(2):
            table = tx.at[odd]
            count = table.shape[0] // 2
            for kz in range(ZLOC):
                high, low = split(rows[odd, kz, parity])
                both = product(table[...], high, ((1,), (1,)))
                first = both[:count] + (both[count:] + product(table[:count], low, ((1,), (1,))))
                at = pl.ds((odd * ZLOC + kz) * padded, padded)
                lines[parity, at, :half] = first[:padded]
                lines[parity, at, half:] = first[padded:]

    loads[2 + ngroup].wait()
    results = []
    for parity in range(2):
        high, low = split(lines[parity])
        count = high.shape[0]
        both = product(jnp.concatenate([high, low], axis=0), ty[parity, 0], ((1,), (0,)))
        results.append(both[:count] + (both[count:] + product(high, ty[parity, 1], ((1,), (0,)))))
    lines[0] = results[0] + results[1]
    lines[1] = results[0] - results[1]

    def along(index, count):
        return 4.0 * jnp.sin(jnp.pi * index.astype(jnp.float32) / count) ** 2

    tiles = width // 128
    line = tiles * ZLOC
    stores = []
    for low, high in ((0, evens[1] // 2), (evens[1] // 2, padded)):
        for odd in range(2):
            count = min(high, evens[odd]) - low
            index = lax.broadcasted_iota(jnp.int32, (high - low, 1), 0) + low
            along_x = jnp.broadcast_to(along(index * 2 + odd, width), (high - low, 128))
            for kz in range(ZLOC):
                turn = jnp.full((8, 128), kz_of(device * ZLOC + kz, total), jnp.int32)
                along_z = along(turn, total)[:1]
                at = pl.ds((odd * ZLOC + kz) * padded + low, high - low)
                for tile in range(tiles):
                    across = lax.broadcasted_iota(jnp.int32, (8, 128), 1) + tile * 128
                    denom = along_z + along_x + along(across, width)[:1] + SCREEN
                    factor = scale / denom
                    sign, lane = tile // (tiles // 2), tile % (tiles // 2) * 128
                    for out, start in ((out_real, 0), (out_imag, half)):
                        value = lines[sign, at, pl.ds(start + lane, 128)] * factor
                        row = (low * 2 + odd) * line + tile * ZLOC + kz
                        out[pl.ds(row, count, stride=2 * line), :] = value[:count]
        first, last = low * 2 * line, min(high * 2 * line, out_real.shape[0])
        for i, (source, target) in enumerate(((out_real, real_hbm), (out_imag, imag_hbm))):
            span = pl.ds(first, last - first)
            stores.append(
                pltpu.make_async_copy(
                    source.at[span], target.at[span], stored.at[len(stores)]
                )
            )
            stores[-1].start()
    for store in stores:
        store.wait()


def parted(table):
    high = table.astype(ml_dtypes.bfloat16)
    low = (table - high.astype(np.float64)).astype(ml_dtypes.bfloat16)
    return high, low


def x_tables(width):
    tables = []
    for odd in range(2):
        padded = -(-(width // 4 + 1) // 8) * 8
        kx = 2 * np.arange(padded)[:, None] + odd
        angles = 2 * np.pi / width * (kx * np.arange(width // 2)[None, :] % width)
        cosine, sine = np.cos(angles), np.sin(angles)
        tables.append(np.concatenate(parted(np.block([[cosine, sine], [-sine, cosine]]))))
    return tables


def y_tables(width):
    tables = []
    for parity in range(2):
        y = 2 * np.arange(width // 2)[:, None] + parity
        angles = 2 * np.pi / width * (y * np.arange(width // 2)[None, :] % width)
        cosine, sine = np.cos(angles), np.sin(angles)
        tables.append(np.stack(parted(np.block([[cosine, -sine], [sine, cosine]]))))
    return np.stack(tables)


def on_device_once(brick_data, brick_xy, brick_live):
    capacity, brick, area = brick_data.shape
    ngroup, nplane = lax.axis_size("zg"), lax.axis_size("zl")
    total = ZLOC * ngroup * nplane
    width = PLANE
    blocks = width // brick
    quads = capacity // 4
    kz = np.array([reversed_bits(row, bit_count(total)) for row in range(0, total, ZLOC)])
    angles = kz.reshape(ngroup, 1, nplane, 1) * np.arange(ngroup * brick).reshape(-1, 1, brick)
    angles = 2 * np.pi / total * (angles % total)
    coef = np.stack([np.cos(angles), -np.sin(angles)], axis=-1).astype(np.float32).reshape(-1)

    vmem = pl.BlockSpec(memory_space=pltpu.VMEM)
    smem = pl.BlockSpec(memory_space=pltpu.SMEM)
    anywhere = pl.BlockSpec(memory_space=pl.ANY)
    arrived, places = pl.pallas_call(
        functools.partial(exchange_kernel, ngroup, nplane, capacity, blocks),
        out_shape=(
            jax.ShapeDtypeStruct((nplane, ngroup, capacity, 8, 128), jnp.float32),
            jax.ShapeDtypeStruct((nplane, 8, 128), jnp.int32),
        ),
        in_specs=[smem, smem, anywhere, vmem],
        out_specs=(anywhere, anywhere),
        scratch_shapes=[
            pltpu.VMEM(brick_data.shape, jnp.float32),
            pltpu.VMEM((ngroup, (quads * brick + 1) * 8, 128), jnp.float32),
            pltpu.VMEM((ngroup, nplane, capacity, 8, 128), jnp.float32),
            pltpu.VMEM((8, 128), jnp.int32),
            pltpu.SemaphoreType.DMA((2, ngroup - 1)),
            pltpu.SemaphoreType.DMA((2, ngroup - 1)),
            pltpu.SemaphoreType.DMA((ngroup, nplane)),
            pltpu.SemaphoreType.DMA((ngroup, nplane)),
            pltpu.SemaphoreType.DMA((nplane,)),
            pltpu.SemaphoreType.DMA((nplane,)),
            pltpu.SemaphoreType.DMA,
        ],
        compiler_params=pltpu.CompilerParams(
            collective_id=0, has_side_effects=True, vmem_limit_bytes=60 * 2**20
        ),
        name="exchange",
    )(jnp.asarray(coef), brick_live, brick_data, brick_xy)

    tx = np.stack(x_tables(width))
    evens = (width // 4 + 1, width // 4)
    ty = y_tables(width)
    kx_count = width // 2 + 1
    out = jax.ShapeDtypeStruct((kx_count * width // 128 * ZLOC, 128), jnp.float32)
    scale = -1.0 / math.sqrt(width * width * total)
    results = pl.pallas_call(
        functools.partial(spectrum_kernel, nplane, ngroup, capacity, blocks, evens, total, scale),
        out_shape=(out, out),
        in_specs=[anywhere] * 4,
        out_specs=(anywhere, anywhere),
        scratch_shapes=[
            pltpu.VMEM((blocks * blocks, 8, 128), jnp.float32),
            pltpu.VMEM((2, ZLOC, 2, width // 2, width), jnp.float32),
            pltpu.VMEM((2, ZLOC * tx.shape[1] // 2, width), jnp.float32),
            pltpu.SMEM(places.shape, jnp.int32),
            pltpu.VMEM(arrived.shape, jnp.float32),
            pltpu.VMEM(tx.shape, tx.dtype),
            pltpu.VMEM(ty.shape, ty.dtype),
            pltpu.VMEM(out.shape, jnp.float32),
            pltpu.VMEM(out.shape, jnp.float32),
            pltpu.SemaphoreType.DMA((3 + ngroup,)),
            pltpu.SemaphoreType.DMA((4,)),
        ],
        compiler_params=pltpu.CompilerParams(vmem_limit_bytes=60 * 2**20),
        name="spectrum",
    )(places, arrived, jnp.asarray(tx), jnp.asarray(ty))

    def ordered(result):
        result = result.reshape(kx_count, width // 128, ZLOC, 128)
        return jnp.transpose(result, (2, 0, 1, 3)).reshape(ZLOC, kx_count, width)

    return tuple(ordered(result) for result in results)


def on_device(brick_data, brick_xy, brick_live):
    layers = brick_live.shape[0]
    slots, brick, area = brick_data.shape
    nplane, ngroup = lax.axis_size("zl"), lax.axis_size("zg")
    one_layer = layers == 1 and nplane * ZLOC == brick and brick == 16 and slots == 16
    fits = slots * nplane * ngroup * area * 2 * ZLOC * 4 <= 4 * 2**20
    if one_layer and fits and ngroup > 1:
        return on_device_once(brick_data, brick_xy, brick_live)
    return on_device_wide(brick_data, brick_xy, brick_live)


def solution(mesh):
    in_specs = (P(("zg", "zl"), None, None), P(None, ("zg", "zl")), P(None, ("zg", "zl")))
    out_specs = (P(("zg", "zl"), None, None), P(("zg", "zl"), None, None))
    return jax.shard_map(
        on_device, mesh=mesh, in_specs=in_specs, out_specs=out_specs, check_vma=False
    )
```

```python
import functools
import math

import jax
import jax.numpy as jnp
import ml_dtypes
import numpy as np
from jax import lax
from jax.experimental import pallas as pl
from jax.experimental.pallas import tpu as pltpu
from jax.sharding import PartitionSpec as P

PLANE = 512
ZLOC = 2


SCREEN = 0.25
HIGHEST = lax.Precision.HIGHEST
MESH = pl.DeviceIdType.MESH


def swapped(array, axis, distance):
    return lax.ppermute(array, axis, [(i, i ^ 1 << distance) for i in range(lax.axis_size(axis))])


def bit_count(number):
    return number.bit_length() - 1


def reverse_bits(values, digits):
    result = jnp.zeros_like(values)
    for digit in range(digits):
        result = result | (values >> digit & 1) << digits - 1 - digit
    return result


def dft_tables(length, freq_count):
    points = jnp.arange(length, dtype=jnp.int32)[:, None]
    freqs = jnp.arange(freq_count, dtype=jnp.int32)[None, :]
    angles = 2.0 * jnp.pi / length * (points * freqs % length).astype(jnp.float32)
    return (jnp.cos(angles), jnp.sin(angles))


def rotate(values, angles):
    cosine = jnp.cos(angles)
    sine = jnp.sin(angles)
    return (values[0] * cosine + values[1] * sine, values[1] * cosine - values[0] * sine)


def section_angles(z_rows, half, total):
    exponent = z_rows % half * (total // (2 * half))
    return (2.0 * jnp.pi / total * exponent.astype(jnp.float32))[:, None, None]


def combine_pair(mine, theirs, upper, angles):
    summed = (mine[0] + theirs[0], mine[1] + theirs[1])
    turned = rotate((theirs[0] - mine[0], theirs[1] - mine[1]), angles)
    return (jnp.where(upper, turned[0], summed[0]), jnp.where(upper, turned[1], summed[1]))


def local_sections(values, total):
    count = values[0].shape[0]
    shape = values[0].shape
    half = count // 2
    while half >= 1:
        split_real = values[0].reshape((count // (2 * half), 2, half) + shape[1:])
        split_imag = values[1].reshape((count // (2 * half), 2, half) + shape[1:])
        offsets = jnp.arange(half, dtype=jnp.int32) * (total // (2 * half))
        angles = (2.0 * jnp.pi / total * offsets.astype(jnp.float32))[None, :, None, None]
        summed_real = split_real[:, 0] + split_real[:, 1]
        summed_imag = split_imag[:, 0] + split_imag[:, 1]
        turned = rotate(
            (split_real[:, 0] - split_real[:, 1], split_imag[:, 0] - split_imag[:, 1]), angles
        )
        values = (
            jnp.stack([summed_real, turned[0]], axis=1).reshape(shape),
            jnp.stack([summed_imag, turned[1]], axis=1).reshape(shape),
        )
        half = half // 2
    return values


def on_device_wide(brick_data, brick_xy, brick_live):
    layers = brick_live.shape[0]
    capacity = brick_data.shape[0] // layers
    brick = brick_data.shape[1]
    area = brick_data.shape[2]
    zlocal = ZLOC
    per_layer = brick // zlocal
    ngroup = lax.axis_size("zg")
    nplane = lax.axis_size("zl")
    total = zlocal * ngroup * nplane
    width = PLANE
    blocks = width // brick
    kx_count = width // 2 + 1
    group_idx = lax.axis_index("zg")
    plane_idx = lax.axis_index("zl")
    live = (jnp.arange(capacity, dtype=jnp.int32)[None, :] < brick_live).astype(jnp.float32)
    masked = (
        brick_data.reshape(layers, capacity, per_layer, zlocal, area) * live[:, :, None, None, None]
    )
    outgoing = jnp.transpose(masked, (0, 2, 1, 3, 4)).reshape(
        layers * per_layer, capacity, zlocal, area
    )
    block_ids = (
        (brick_xy[1] * blocks + brick_xy[0]).astype(jnp.float32).reshape(layers, 1, capacity)
    )
    block_out = jnp.broadcast_to(block_ids, (layers, per_layer, capacity)).reshape(
        layers * per_layer, capacity
    )
    pieces, places = (
        lax.all_to_all(outgoing, "zl", split_axis=0, concat_axis=0, tiled=True),
        lax.all_to_all(block_out, "zl", split_axis=0, concat_axis=0, tiled=True),
    )
    slot_ids = places.astype(jnp.int32).reshape(-1)
    incoming = jnp.transpose(pieces, (2, 0, 1, 3)).reshape(zlocal, -1, area)
    blockgrid = (
        jnp.zeros((zlocal, blocks * blocks, area), jnp.float32).at[:, slot_ids, :].add(incoming)
    )
    blockgrid = blockgrid.reshape(zlocal, blocks, blocks, brick, brick)
    cos_x, sin_x = dft_tables(width, kx_count)
    cos_x = cos_x.reshape(blocks, brick, kx_count)
    sin_x = sin_x.reshape(blocks, brick, kx_count)
    first_real = jnp.einsum("zabuv,bvk->zkau", blockgrid, cos_x, precision=HIGHEST).reshape(
        zlocal * kx_count, width
    )
    first_imag = -jnp.einsum("zabuv,bvk->zkau", blockgrid, sin_x, precision=HIGHEST).reshape(
        zlocal * kx_count, width
    )
    cos_y, sin_y = dft_tables(width, width)
    second_real = jnp.dot(first_real, cos_y, precision=HIGHEST) + jnp.dot(
        first_imag, sin_y, precision=HIGHEST
    )
    second_imag = jnp.dot(first_imag, cos_y, precision=HIGHEST) - jnp.dot(
        first_real, sin_y, precision=HIGHEST
    )
    values = (
        second_real.reshape(zlocal, kx_count, width),
        second_imag.reshape(zlocal, kx_count, width),
    )
    device = group_idx * nplane + plane_idx
    z_rows = device * zlocal + jnp.arange(zlocal, dtype=jnp.int32)
    gbits = bit_count(ngroup)
    pbits = bit_count(nplane)
    for level in reversed(range(gbits)):
        half = zlocal * nplane * (1 << level)
        theirs = swapped((values[0], values[1]), "zg", level)
        upper = group_idx >> level & 1 == 1
        values = combine_pair(values, theirs, upper, section_angles(z_rows, half, total))
    plane_values = values
    for level in reversed(range(pbits)):
        half = zlocal * (1 << level)
        theirs = swapped((plane_values[0], plane_values[1]), "zl", level)
        upper = plane_idx >> level & 1 == 1
        plane_values = combine_pair(
            plane_values, theirs, upper, section_angles(z_rows, half, total)
        )
    plane_values = local_sections(plane_values, total)
    values = plane_values
    kz_rows = reverse_bits(z_rows, bit_count(total))
    along_z = 4.0 * jnp.sin(jnp.pi * kz_rows.astype(jnp.float32) / total) ** 2
    along_x = 4.0 * jnp.sin(jnp.pi * jnp.arange(kx_count, dtype=jnp.float32) / width) ** 2
    along_y = 4.0 * jnp.sin(jnp.pi * jnp.arange(width, dtype=jnp.float32) / width) ** 2
    denom = along_z[:, None, None] + along_x[None, :, None] + along_y[None, None, :] + SCREEN
    factor = -(1.0 / math.sqrt(width * width * total)) / denom
    return (values[0] * factor, values[1] * factor)


def kz_of(row, total):
    digits = bit_count(total)
    return sum(
        lax.rem(lax.div(row, jnp.int32(1 << d)), jnp.int32(2)) * (1 << digits - 1 - d)
        for d in range(digits)
    )


def reversed_bits(row, digits):
    return sum((row >> d & 1) << digits - 1 - d for d in range(digits))


def transposed_blocks(tiles, width):
    tiles = list(tiles)
    block = lax.broadcasted_iota(jnp.int32, tiles[0].shape, tiles[0].ndim - 1) // width
    lanes = tiles[0].shape[-1]
    step = len(tiles) // 2
    while step:
        high = (block & step) != 0
        for i in range(len(tiles)):
            if not i & step:
                low, up = tiles[i], tiles[i + step]
                if 2 * step * width == lanes:
                    swapped_part = pltpu.roll(jnp.where(high, low, up), step * width, low.ndim - 1)
                    tiles[i] = jnp.where(high, swapped_part, low)
                    tiles[i + step] = jnp.where(high, up, swapped_part)
                    continue
                tiles[i] = jnp.where(high, pltpu.roll(up, step * width, low.ndim - 1), low)
                tiles[i + step] = jnp.where(
                    high, up, pltpu.roll(low, lanes - step * width, low.ndim - 1)
                )
        step //= 2
    return tiles


def exchange_kernel(
    ngroup, nplane, capacity, blocks,
    coef, live, bricks, xy, out, out_places, data, raw, ready, mine, theirs, spots, zsend, zrecv, psend, precv,
    ssend, srecv, lsend, lrecv, loaded,
):
    group, plane = lax.axis_index("zg"), lax.axis_index("zl")
    quads = capacity // 4
    depth = data.shape[1]
    load = pltpu.make_async_copy(bricks, data, loaded)
    load.start()
    barrier = pltpu.get_barrier_semaphore()

    def greet(g, p):
        pl.semaphore_signal(barrier, inc=1, device_id=(g, p), device_id_type=MESH)

    for k in range(1, nplane):
        greet(group, lax.rem(plane + k, nplane))
    for k in range(1, ngroup):
        greet(lax.rem(group + k, ngroup), plane)
    pl.semaphore_wait(barrier, nplane - 1 + ngroup - 1)

    def along(side, t):
        chunk = jnp.where(side == 0, group - t, group + t)
        target = jnp.where(side == 0, group + 1, group - 1)
        inside = (chunk >= 0) & (chunk < ngroup) & (target >= 0) & (target < ngroup)
        safe = jnp.clip(chunk, 0, ngroup - 1)
        copy = pltpu.make_async_remote_copy(
            src_ref=raw.at[safe],
            dst_ref=raw.at[safe],
            send_sem=zsend.at[side, t],
            recv_sem=zrecv.at[side, t],
            device_id=(jnp.clip(target, 0, ngroup - 1), plane),
            device_id_type=MESH,
        )
        return inside, copy

    def to_peer(chunk, k):
        return pltpu.make_async_remote_copy(
            src_ref=ready.at[chunk, k],
            dst_ref=out.at[plane, chunk],
            send_sem=psend.at[chunk, k],
            recv_sem=precv.at[chunk, k],
            device_id=(group, lax.rem(plane + k, nplane)),
            device_id_type=MESH,
        )

    def keep(chunk):
        return pltpu.make_async_copy(ready.at[chunk, 0], out.at[plane, chunk], psend.at[chunk, 0])

    def sums(chunk, peer, target):
        first = ((group * ngroup + chunk) * nplane + peer) * 2 * depth
        real = [coef[first + 2 * z] for z in range(depth)]
        imag = [coef[first + 2 * z + 1] for z in range(depth)]
        for quad in range(quads):
            parts = []
            for table in (real, imag):
                for parity in range(2):
                    summed = None
                    for z in range(parity, depth, 2):
                        term = raw[chunk, pl.ds((quad * depth + z) * 8, 8)] * table[z]
                        summed = term if summed is None else summed + term
                    parts.append(summed)
            tiles = (parts[0] + parts[1], parts[2] + parts[3], parts[0] - parts[1], parts[2] - parts[3])
            for i, tile in enumerate(transposed_blocks(tiles, 32)):
                target[quad * 4 + i] = tile

    def share(chunk):
        def one(k, carry):
            sums(chunk, lax.rem(plane + k, nplane), ready.at[chunk, k])
            to_peer(chunk, k).start()
            return carry

        lax.fori_loop(1, nplane, one, 0)
        sums(chunk, plane, ready.at[chunk, 0])
        keep(chunk).start()

    place = xy[1:2, :] * blocks + xy[0:1, :]
    place = jnp.concatenate([place, jnp.zeros((1, 128 - capacity), jnp.int32)], axis=1)
    mine[...] = jnp.broadcast_to(place, mine.shape)

    def line_to(k):
        return pltpu.make_async_remote_copy(
            src_ref=mine,
            dst_ref=theirs.at[k],
            send_sem=lsend.at[k],
            recv_sem=lrecv.at[k],
            device_id=(lax.rem(group + k, ngroup), plane),
            device_id_type=MESH,
        )

    for k in range(1, ngroup):
        line_to(k).start()
    load.wait()
    for quad in range(quads):
        for z in range(0, depth, 8):
            for half in range(2):
                tiles = []
                for slot in range(quad * 4, quad * 4 + 4):
                    alive = jnp.where(slot < live[0, 0], 1.0, 0.0)
                    tiles.append(data[slot, z : z + 8, half * 128 : half * 128 + 128] * alive)
                for i, tile in enumerate(transposed_blocks(tiles, 32)):
                    row = (quad * depth + z) * 8 + half * 4 + i
                    raw[group, pl.ds(row, 8, stride=8), :] = tile
    for side in range(2):
        inside, copy = along(side, 0)
        pl.when(inside)(copy.start)
    share(group)
    line = [line_to(k) for k in range(1, ngroup)]
    for copy in line:
        copy.wait_recv()
    spots[...] = jnp.zeros_like(spots)
    spots[pl.ds(group, 1)] = mine[:1]
    for k in range(1, ngroup):
        source = lax.rem(group + ngroup - k, ngroup)
        spots[pl.ds(source, 1)] = theirs[k, :1]
    own_spots = pltpu.make_async_copy(spots, out_places.at[plane], ssend.at[0])
    own_spots.start()

    def spots_to(k):
        return pltpu.make_async_remote_copy(
            src_ref=spots,
            dst_ref=out_places.at[plane],
            send_sem=ssend.at[k],
            recv_sem=srecv.at[k],
            device_id=(group, lax.rem(plane + k, nplane)),
            device_id_type=MESH,
        )

    for k in range(1, nplane):
        spots_to(k).start()

    def arrival(i, carry):
        t, side = i // 2, lax.rem(i, 2)
        chunk = jnp.where(side == 0, group - 1 - t, group + 1 + t)

        @pl.when((chunk >= 0) & (chunk < ngroup))
        def _():
            safe = jnp.clip(chunk, 0, ngroup - 1)
            pltpu.make_async_remote_copy(
                src_ref=raw.at[safe],
                dst_ref=raw.at[safe],
                send_sem=zsend.at[side, t],
                recv_sem=zrecv.at[side, t],
                device_id=(group, plane),
                device_id_type=MESH,
            ).wait_recv()

            @pl.when(t < ngroup - 2)
            def _():
                inside, copy = along(side, jnp.minimum(t + 1, ngroup - 2))
                pl.when(inside)(copy.start)

            share(safe)

        return carry

    lax.fori_loop(0, 2 * (ngroup - 1), arrival, 0)

    for side in range(2):
        for t in range(ngroup - 1):
            inside, copy = along(side, t)
            pl.when(inside)(copy.wait_send)

    own_spots.wait()
    for copy in line:
        copy.wait_send()
    for k in range(1, nplane):
        spots_to(k).wait_send()
        spots_to(k).wait_recv()

    def finish(chunk):
        keep(chunk).wait()

        def one(k, carry):
            copy = to_peer(chunk, k)
            copy.wait_send()
            copy.wait_recv()
            return carry

        lax.fori_loop(1, nplane, one, 0)

    finish(group)

    def farther(i, carry):
        t, side = i // 2, lax.rem(i, 2)
        chunk = jnp.where(side == 0, group - 1 - t, group + 1 + t)
        pl.when((chunk >= 0) & (chunk < ngroup))(lambda: finish(jnp.clip(chunk, 0, ngroup - 1)))
        return carry

    lax.fori_loop(0, 2 * (ngroup - 1), farther, 0)


def split(values):
    high = values.astype(jnp.bfloat16)
    return high, (values - high.astype(jnp.float32)).astype(jnp.bfloat16)


def spectrum_kernel(
    nplane, ngroup, capacity, blocks, evens, total, scale,
    places_hbm, bricks_hbm, tx_hbm, ty_hbm, real_hbm, imag_hbm,
    grid, rows, lines, places, bricks, tx, ty, out_real, out_imag, loaded, stored,
):
    half = rows.shape[-1] // 2
    width = rows.shape[-1]
    device = lax.axis_index("zg") * nplane + lax.axis_index("zl")
    loads = [pltpu.make_async_copy(places_hbm, places, loaded.at[0])]
    for chunk in range(ngroup):
        loads.append(
            pltpu.make_async_copy(
                bricks_hbm.at[:, chunk], bricks.at[:, chunk], loaded.at[1 + chunk]
            )
        )
    loads.append(pltpu.make_async_copy(tx_hbm, tx, loaded.at[1 + ngroup]))
    loads.append(pltpu.make_async_copy(ty_hbm, ty, loaded.at[2 + ngroup]))
    for load in loads:
        load.start()

    def clear(i, carry):
        grid[pl.ds(i * 32, 32)] = jnp.zeros((32,) + grid.shape[1:], jnp.float32)
        return carry

    lax.fori_loop(0, grid.shape[0] // 32, clear, 0)

    def place(chunk, pair):
        slots = [(pair * 2 + n, c) for n in range(2) for c in range(capacity)]
        ids = [places[source, chunk, c] for source, c in slots]
        values = [grid[at] + bricks[source, chunk, c] for at, (source, c) in zip(ids, slots)]
        for at, value in zip(ids, values):
            grid[at] = value

    loads[0].wait()
    for chunk in range(ngroup):
        loads[1 + chunk].wait()
        lax.fori_loop(0, nplane // 2, lambda pair, carry: (place(chunk, pair), carry)[1], 0)

    batch = 2

    def arrange(step, carry):
        for h in range(2):
            tiles = []
            for i in range(8):
                first, second = (
                    jnp.stack([grid[(step * batch + n) * blocks + at + i] for n in range(batch)])
                    for at in (h * 8, h * 8 + 16)
                )
                tiles.append((first + second, first - second))
            for side in range(2):
                lines_of = transposed_blocks([pair[side] for pair in tiles], 16)
                for j in range(8):
                    kz, ri, parity = j // 4, j // 2 % 2, j % 2
                    lanes = pl.ds(ri * half + h * 128, 128)
                    at = pl.ds(pl.multiple_of(step * batch * 8, batch * 8), batch * 8)
                    rows[side, kz, parity, at, lanes] = lines_of[j].reshape(-1, 128)
        return carry

    lax.fori_loop(0, blocks // batch, arrange, 0)
    loads[1 + ngroup].wait()

    def product(a, b, dims):
        return lax.dot_general(a, b, (dims, ((), ())), preferred_element_type=jnp.float32)

    padded = tx.shape[1] // 4
    for parity in range(2):
        for odd in range(2):
            table = tx.at[odd]
            count = table.shape[0] // 2
            for kz in range(ZLOC):
                high, low = split(rows[odd, kz, parity])
                both = product(table[...], high, ((1,), (1,)))
                first = both[:count] + (both[count:] + product(table[:count], low, ((1,), (1,))))
                at = pl.ds((odd * ZLOC + kz) * padded, padded)
                lines[parity, at, :half] = first[:padded]
                lines[parity, at, half:] = first[padded:]

    loads[2 + ngroup].wait()
    results = []
    for parity in range(2):
        high, low = split(lines[parity])
        count = high.shape[0]
        both = product(jnp.concatenate([high, low], axis=0), ty[parity, 0], ((1,), (0,)))
        results.append(both[:count] + (both[count:] + product(high, ty[parity, 1], ((1,), (0,)))))
    lines[0] = results[0] + results[1]
    lines[1] = results[0] - results[1]

    def along(index, count):
        return 4.0 * jnp.sin(jnp.pi * index.astype(jnp.float32) / count) ** 2

    tiles = width // 128
    line = tiles * ZLOC
    stores = []
    for low, high in ((0, evens[1] // 2), (evens[1] // 2, padded)):
        for odd in range(2):
            count = min(high, evens[odd]) - low
            index = lax.broadcasted_iota(jnp.int32, (high - low, 1), 0) + low
            along_x = jnp.broadcast_to(along(index * 2 + odd, width), (high - low, 128))
            for kz in range(ZLOC):
                turn = jnp.full((8, 128), kz_of(device * ZLOC + kz, total), jnp.int32)
                along_z = along(turn, total)[:1]
                at = pl.ds((odd * ZLOC + kz) * padded + low, high - low)
                for tile in range(tiles):
                    across = lax.broadcasted_iota(jnp.int32, (8, 128), 1) + tile * 128
                    denom = along_z + along_x + along(across, width)[:1] + SCREEN
                    factor = scale / denom
                    sign, lane = tile // (tiles // 2), tile % (tiles // 2) * 128
                    for out, start in ((out_real, 0), (out_imag, half)):
                        value = lines[sign, at, pl.ds(start + lane, 128)] * factor
                        row = (low * 2 + odd) * line + tile * ZLOC + kz
                        out[pl.ds(row, count, stride=2 * line), :] = value[:count]
        first, last = low * 2 * line, min(high * 2 * line, out_real.shape[0])
        for i, (source, target) in enumerate(((out_real, real_hbm), (out_imag, imag_hbm))):
            span = pl.ds(first, last - first)
            stores.append(
                pltpu.make_async_copy(
                    source.at[span], target.at[span], stored.at[len(stores)]
                )
            )
            stores[-1].start()
    for store in stores:
        store.wait()


def parted(table):
    high = table.astype(ml_dtypes.bfloat16)
    low = (table - high.astype(np.float64)).astype(ml_dtypes.bfloat16)
    return high, low


def x_tables(width):
    tables = []
    for odd in range(2):
        padded = -(-(width // 4 + 1) // 8) * 8
        kx = 2 * np.arange(padded)[:, None] + odd
        angles = 2 * np.pi / width * (kx * np.arange(width // 2)[None, :] % width)
        cosine, sine = np.cos(angles), np.sin(angles)
        tables.append(np.concatenate(parted(np.block([[cosine, sine], [-sine, cosine]]))))
    return tables


def y_tables(width):
    tables = []
    for parity in range(2):
        y = 2 * np.arange(width // 2)[:, None] + parity
        angles = 2 * np.pi / width * (y * np.arange(width // 2)[None, :] % width)
        cosine, sine = np.cos(angles), np.sin(angles)
        tables.append(np.stack(parted(np.block([[cosine, -sine], [sine, cosine]]))))
    return np.stack(tables)


def on_device_once(brick_data, brick_xy, brick_live):
    capacity, brick, area = brick_data.shape
    ngroup, nplane = lax.axis_size("zg"), lax.axis_size("zl")
    total = ZLOC * ngroup * nplane
    width = PLANE
    blocks = width // brick
    quads = capacity // 4
    kz = np.array([reversed_bits(row, bit_count(total)) for row in range(0, total, ZLOC)])
    angles = kz.reshape(ngroup, 1, nplane, 1) * np.arange(ngroup * brick).reshape(-1, 1, brick)
    angles = 2 * np.pi / total * (angles % total)
    coef = np.stack([np.cos(angles), -np.sin(angles)], axis=-1).astype(np.float32).reshape(-1)

    vmem = pl.BlockSpec(memory_space=pltpu.VMEM)
    smem = pl.BlockSpec(memory_space=pltpu.SMEM)
    anywhere = pl.BlockSpec(memory_space=pl.ANY)
    arrived, places = pl.pallas_call(
        functools.partial(exchange_kernel, ngroup, nplane, capacity, blocks),
        out_shape=(
            jax.ShapeDtypeStruct((nplane, ngroup, capacity, 8, 128), jnp.float32),
            jax.ShapeDtypeStruct((nplane, 8, 128), jnp.int32),
        ),
        in_specs=[smem, smem, anywhere, vmem],
        out_specs=(anywhere, anywhere),
        scratch_shapes=[
            pltpu.VMEM(brick_data.shape, jnp.float32),
            pltpu.VMEM((ngroup, quads * brick * 8, 128), jnp.float32),
            pltpu.VMEM((ngroup, nplane, capacity, 8, 128), jnp.float32),
            pltpu.VMEM((8, 128), jnp.int32),
            pltpu.VMEM((ngroup, 8, 128), jnp.int32),
            pltpu.VMEM((8, 128), jnp.int32),
            pltpu.SemaphoreType.DMA((2, ngroup - 1)),
            pltpu.SemaphoreType.DMA((2, ngroup - 1)),
            pltpu.SemaphoreType.DMA((ngroup, nplane)),
            pltpu.SemaphoreType.DMA((ngroup, nplane)),
            pltpu.SemaphoreType.DMA((nplane,)),
            pltpu.SemaphoreType.DMA((nplane,)),
            pltpu.SemaphoreType.DMA((ngroup,)),
            pltpu.SemaphoreType.DMA((ngroup,)),
            pltpu.SemaphoreType.DMA,
        ],
        compiler_params=pltpu.CompilerParams(
            collective_id=0, has_side_effects=True, vmem_limit_bytes=60 * 2**20
        ),
        name="exchange",
    )(jnp.asarray(coef), brick_live, brick_data, brick_xy)

    tx = np.stack(x_tables(width))
    evens = (width // 4 + 1, width // 4)
    ty = y_tables(width)
    kx_count = width // 2 + 1
    out = jax.ShapeDtypeStruct((kx_count * width // 128 * ZLOC, 128), jnp.float32)
    scale = -1.0 / math.sqrt(width * width * total)
    results = pl.pallas_call(
        functools.partial(spectrum_kernel, nplane, ngroup, capacity, blocks, evens, total, scale),
        out_shape=(out, out),
        in_specs=[anywhere] * 4,
        out_specs=(anywhere, anywhere),
        scratch_shapes=[
            pltpu.VMEM((blocks * blocks, 8, 128), jnp.float32),
            pltpu.VMEM((2, ZLOC, 2, width // 2, width), jnp.float32),
            pltpu.VMEM((2, ZLOC * tx.shape[1] // 2, width), jnp.float32),
            pltpu.SMEM(places.shape, jnp.int32),
            pltpu.VMEM(arrived.shape, jnp.float32),
            pltpu.VMEM(tx.shape, tx.dtype),
            pltpu.VMEM(ty.shape, ty.dtype),
            pltpu.VMEM(out.shape, jnp.float32),
            pltpu.VMEM(out.shape, jnp.float32),
            pltpu.SemaphoreType.DMA((3 + ngroup,)),
            pltpu.SemaphoreType.DMA((4,)),
        ],
        compiler_params=pltpu.CompilerParams(vmem_limit_bytes=60 * 2**20),
        name="spectrum",
    )(places, arrived, jnp.asarray(tx), jnp.asarray(ty))

    def ordered(result):
        result = result.reshape(kx_count, width // 128, ZLOC, 128)
        return jnp.transpose(result, (2, 0, 1, 3)).reshape(ZLOC, kx_count, width)

    return tuple(ordered(result) for result in results)


def on_device(brick_data, brick_xy, brick_live):
    layers = brick_live.shape[0]
    slots, brick, area = brick_data.shape
    nplane, ngroup = lax.axis_size("zl"), lax.axis_size("zg")
    one_layer = layers == 1 and nplane * ZLOC == brick and brick == 16 and slots == 16
    fits = slots * nplane * ngroup * area * 2 * ZLOC * 4 <= 4 * 2**20
    if one_layer and fits and ngroup > 1:
        return on_device_once(brick_data, brick_xy, brick_live)
    return on_device_wide(brick_data, brick_xy, brick_live)


def solution(mesh):
    in_specs = (P(("zg", "zl"), None, None), P(None, ("zg", "zl")), P(None, ("zg", "zl")))
    out_specs = (P(("zg", "zl"), None, None), P(("zg", "zl"), None, None))
    return jax.shard_map(
        on_device, mesh=mesh, in_specs=in_specs, out_specs=out_specs, check_vma=False
    )
```

```python
import functools
import math

import jax
import jax.numpy as jnp
import ml_dtypes
import numpy as np
from jax import lax
from jax.experimental import pallas as pl
from jax.experimental.pallas import tpu as pltpu
from jax.sharding import PartitionSpec as P

PLANE = 512
ZLOC = 2


SCREEN = 0.25
HIGHEST = lax.Precision.HIGHEST
MESH = pl.DeviceIdType.MESH


def swapped(array, axis, distance):
    return lax.ppermute(array, axis, [(i, i ^ 1 << distance) for i in range(lax.axis_size(axis))])


def bit_count(number):
    return number.bit_length() - 1


def reverse_bits(values, digits):
    result = jnp.zeros_like(values)
    for digit in range(digits):
        result = result | (values >> digit & 1) << digits - 1 - digit
    return result


def dft_tables(length, freq_count):
    points = jnp.arange(length, dtype=jnp.int32)[:, None]
    freqs = jnp.arange(freq_count, dtype=jnp.int32)[None, :]
    angles = 2.0 * jnp.pi / length * (points * freqs % length).astype(jnp.float32)
    return (jnp.cos(angles), jnp.sin(angles))


def rotate(values, angles):
    cosine = jnp.cos(angles)
    sine = jnp.sin(angles)
    return (values[0] * cosine + values[1] * sine, values[1] * cosine - values[0] * sine)


def section_angles(z_rows, half, total):
    exponent = z_rows % half * (total // (2 * half))
    return (2.0 * jnp.pi / total * exponent.astype(jnp.float32))[:, None, None]


def combine_pair(mine, theirs, upper, angles):
    summed = (mine[0] + theirs[0], mine[1] + theirs[1])
    turned = rotate((theirs[0] - mine[0], theirs[1] - mine[1]), angles)
    return (jnp.where(upper, turned[0], summed[0]), jnp.where(upper, turned[1], summed[1]))


def local_sections(values, total):
    count = values[0].shape[0]
    shape = values[0].shape
    half = count // 2
    while half >= 1:
        split_real = values[0].reshape((count // (2 * half), 2, half) + shape[1:])
        split_imag = values[1].reshape((count // (2 * half), 2, half) + shape[1:])
        offsets = jnp.arange(half, dtype=jnp.int32) * (total // (2 * half))
        angles = (2.0 * jnp.pi / total * offsets.astype(jnp.float32))[None, :, None, None]
        summed_real = split_real[:, 0] + split_real[:, 1]
        summed_imag = split_imag[:, 0] + split_imag[:, 1]
        turned = rotate(
            (split_real[:, 0] - split_real[:, 1], split_imag[:, 0] - split_imag[:, 1]), angles
        )
        values = (
            jnp.stack([summed_real, turned[0]], axis=1).reshape(shape),
            jnp.stack([summed_imag, turned[1]], axis=1).reshape(shape),
        )
        half = half // 2
    return values


def on_device_wide(brick_data, brick_xy, brick_live):
    layers = brick_live.shape[0]
    capacity = brick_data.shape[0] // layers
    brick = brick_data.shape[1]
    area = brick_data.shape[2]
    zlocal = ZLOC
    per_layer = brick // zlocal
    ngroup = lax.axis_size("zg")
    nplane = lax.axis_size("zl")
    total = zlocal * ngroup * nplane
    width = PLANE
    blocks = width // brick
    kx_count = width // 2 + 1
    group_idx = lax.axis_index("zg")
    plane_idx = lax.axis_index("zl")
    live = (jnp.arange(capacity, dtype=jnp.int32)[None, :] < brick_live).astype(jnp.float32)
    masked = (
        brick_data.reshape(layers, capacity, per_layer, zlocal, area) * live[:, :, None, None, None]
    )
    outgoing = jnp.transpose(masked, (0, 2, 1, 3, 4)).reshape(
        layers * per_layer, capacity, zlocal, area
    )
    block_ids = (
        (brick_xy[1] * blocks + brick_xy[0]).astype(jnp.float32).reshape(layers, 1, capacity)
    )
    block_out = jnp.broadcast_to(block_ids, (layers, per_layer, capacity)).reshape(
        layers * per_layer, capacity
    )
    pieces, places = (
        lax.all_to_all(outgoing, "zl", split_axis=0, concat_axis=0, tiled=True),
        lax.all_to_all(block_out, "zl", split_axis=0, concat_axis=0, tiled=True),
    )
    slot_ids = places.astype(jnp.int32).reshape(-1)
    incoming = jnp.transpose(pieces, (2, 0, 1, 3)).reshape(zlocal, -1, area)
    blockgrid = (
        jnp.zeros((zlocal, blocks * blocks, area), jnp.float32).at[:, slot_ids, :].add(incoming)
    )
    blockgrid = blockgrid.reshape(zlocal, blocks, blocks, brick, brick)
    cos_x, sin_x = dft_tables(width, kx_count)
    cos_x = cos_x.reshape(blocks, brick, kx_count)
    sin_x = sin_x.reshape(blocks, brick, kx_count)
    first_real = jnp.einsum("zabuv,bvk->zkau", blockgrid, cos_x, precision=HIGHEST).reshape(
        zlocal * kx_count, width
    )
    first_imag = -jnp.einsum("zabuv,bvk->zkau", blockgrid, sin_x, precision=HIGHEST).reshape(
        zlocal * kx_count, width
    )
    cos_y, sin_y = dft_tables(width, width)
    second_real = jnp.dot(first_real, cos_y, precision=HIGHEST) + jnp.dot(
        first_imag, sin_y, precision=HIGHEST
    )
    second_imag = jnp.dot(first_imag, cos_y, precision=HIGHEST) - jnp.dot(
        first_real, sin_y, precision=HIGHEST
    )
    values = (
        second_real.reshape(zlocal, kx_count, width),
        second_imag.reshape(zlocal, kx_count, width),
    )
    device = group_idx * nplane + plane_idx
    z_rows = device * zlocal + jnp.arange(zlocal, dtype=jnp.int32)
    gbits = bit_count(ngroup)
    pbits = bit_count(nplane)
    for level in reversed(range(gbits)):
        half = zlocal * nplane * (1 << level)
        theirs = swapped((values[0], values[1]), "zg", level)
        upper = group_idx >> level & 1 == 1
        values = combine_pair(values, theirs, upper, section_angles(z_rows, half, total))
    plane_values = values
    for level in reversed(range(pbits)):
        half = zlocal * (1 << level)
        theirs = swapped((plane_values[0], plane_values[1]), "zl", level)
        upper = plane_idx >> level & 1 == 1
        plane_values = combine_pair(
            plane_values, theirs, upper, section_angles(z_rows, half, total)
        )
    plane_values = local_sections(plane_values, total)
    values = plane_values
    kz_rows = reverse_bits(z_rows, bit_count(total))
    along_z = 4.0 * jnp.sin(jnp.pi * kz_rows.astype(jnp.float32) / total) ** 2
    along_x = 4.0 * jnp.sin(jnp.pi * jnp.arange(kx_count, dtype=jnp.float32) / width) ** 2
    along_y = 4.0 * jnp.sin(jnp.pi * jnp.arange(width, dtype=jnp.float32) / width) ** 2
    denom = along_z[:, None, None] + along_x[None, :, None] + along_y[None, None, :] + SCREEN
    factor = -(1.0 / math.sqrt(width * width * total)) / denom
    return (values[0] * factor, values[1] * factor)


def kz_of(row, total):
    digits = bit_count(total)
    return sum(
        lax.rem(lax.div(row, jnp.int32(1 << d)), jnp.int32(2)) * (1 << digits - 1 - d)
        for d in range(digits)
    )


def reversed_bits(row, digits):
    return sum((row >> d & 1) << digits - 1 - d for d in range(digits))


def transposed_blocks(tiles, width):
    tiles = list(tiles)
    block = lax.broadcasted_iota(jnp.int32, tiles[0].shape, tiles[0].ndim - 1) // width
    lanes = tiles[0].shape[-1]
    step = len(tiles) // 2
    while step:
        high = (block & step) != 0
        for i in range(len(tiles)):
            if not i & step:
                low, up = tiles[i], tiles[i + step]
                if 2 * step * width == lanes:
                    swapped_part = pltpu.roll(jnp.where(high, low, up), step * width, low.ndim - 1)
                    tiles[i] = jnp.where(high, swapped_part, low)
                    tiles[i + step] = jnp.where(high, up, swapped_part)
                    continue
                tiles[i] = jnp.where(high, pltpu.roll(up, step * width, low.ndim - 1), low)
                tiles[i + step] = jnp.where(
                    high, up, pltpu.roll(low, lanes - step * width, low.ndim - 1)
                )
        step //= 2
    return tiles


def exchange_kernel(
    ngroup, nplane, capacity, blocks,
    coef, live, bricks, xy, out, out_places, data, raw, ready, mine, theirs, spots, zsend, zrecv, psend, precv,
    ssend, srecv, lsend, lrecv, loaded,
):
    group, plane = lax.axis_index("zg"), lax.axis_index("zl")
    quads = capacity // 4
    depth = data.shape[1]
    load = pltpu.make_async_copy(bricks, data, loaded)
    load.start()
    barrier = pltpu.get_barrier_semaphore()

    def greet(g, p):
        pl.semaphore_signal(barrier, inc=1, device_id=(g, p), device_id_type=MESH)

    for k in range(1, nplane):
        greet(group, lax.rem(plane + k, nplane))
    for k in range(1, ngroup):
        greet(lax.rem(group + k, ngroup), plane)
    pl.semaphore_wait(barrier, nplane - 1 + ngroup - 1)

    def along(side, t):
        chunk = jnp.where(side == 0, group - t, group + t)
        target = jnp.where(side == 0, group + 1, group - 1)
        inside = (chunk >= 0) & (chunk < ngroup) & (target >= 0) & (target < ngroup)
        safe = jnp.clip(chunk, 0, ngroup - 1)
        copy = pltpu.make_async_remote_copy(
            src_ref=raw.at[safe],
            dst_ref=raw.at[safe],
            send_sem=zsend.at[side, t],
            recv_sem=zrecv.at[side, t],
            device_id=(jnp.clip(target, 0, ngroup - 1), plane),
            device_id_type=MESH,
        )
        return inside, copy

    def to_peer(chunk, k):
        return pltpu.make_async_remote_copy(
            src_ref=ready.at[chunk, k],
            dst_ref=out.at[plane, chunk],
            send_sem=psend.at[chunk, k],
            recv_sem=precv.at[chunk, k],
            device_id=(group, lax.rem(plane + k, nplane)),
            device_id_type=MESH,
        )

    def keep(chunk):
        return pltpu.make_async_copy(ready.at[chunk, 0], out.at[plane, chunk], psend.at[chunk, 0])

    def sums(chunk, peer, target):
        first = ((group * ngroup + chunk) * nplane + peer) * 2 * depth
        real = [coef[first + 2 * z] for z in range(depth)]
        imag = [coef[first + 2 * z + 1] for z in range(depth)]
        for quad in range(quads):
            parts = []
            for table in (real, imag):
                for parity in range(2):
                    summed = None
                    for z in range(parity, depth, 2):
                        term = raw[chunk, pl.ds((quad * depth + z) * 8, 8)] * table[z]
                        summed = term if summed is None else summed + term
                    parts.append(summed)
            tiles = (parts[0] + parts[1], parts[2] + parts[3], parts[0] - parts[1], parts[2] - parts[3])
            for i, tile in enumerate(transposed_blocks(tiles, 32)):
                target[quad * 4 + i] = tile

    def share(chunk):
        def one(k, carry):
            sums(chunk, lax.rem(plane + k, nplane), ready.at[chunk, k])
            to_peer(chunk, k).start()
            return carry

        lax.fori_loop(1, nplane, one, 0)
        sums(chunk, plane, ready.at[chunk, 0])
        keep(chunk).start()

    place = xy[1:2, :] * blocks + xy[0:1, :]
    place = jnp.concatenate([place, jnp.zeros((1, 128 - capacity), jnp.int32)], axis=1)
    mine[...] = jnp.broadcast_to(place, mine.shape)

    def line_to(k):
        return pltpu.make_async_remote_copy(
            src_ref=mine,
            dst_ref=theirs.at[k],
            send_sem=lsend.at[k],
            recv_sem=lrecv.at[k],
            device_id=(lax.rem(group + k, ngroup), plane),
            device_id_type=MESH,
        )

    for k in range(1, ngroup):
        line_to(k).start()
    load.wait()
    for quad in range(quads):
        for z in range(0, depth, 8):
            for half in range(2):
                tiles = []
                for slot in range(quad * 4, quad * 4 + 4):
                    alive = jnp.where(slot < live[0, 0], 1.0, 0.0)
                    tiles.append(data[slot, z : z + 8, half * 128 : half * 128 + 128] * alive)
                for i, tile in enumerate(transposed_blocks(tiles, 32)):
                    row = (quad * depth + z) * 8 + half * 4 + i
                    raw[group, pl.ds(row, 8, stride=8), :] = tile
    for side in range(2):
        inside, copy = along(side, 0)
        pl.when(inside)(copy.start)
    share(group)
    line = [line_to(k) for k in range(1, ngroup)]
    for copy in line:
        copy.wait_recv()
    spots[...] = jnp.zeros_like(spots)
    spots[pl.ds(group, 1)] = mine[:1]
    for k in range(1, ngroup):
        source = lax.rem(group + ngroup - k, ngroup)
        spots[pl.ds(source, 1)] = theirs[k, :1]
    own_spots = pltpu.make_async_copy(spots, out_places.at[plane], ssend.at[0])
    own_spots.start()

    def spots_to(k):
        return pltpu.make_async_remote_copy(
            src_ref=spots,
            dst_ref=out_places.at[plane],
            send_sem=ssend.at[k],
            recv_sem=srecv.at[k],
            device_id=(group, lax.rem(plane + k, nplane)),
            device_id_type=MESH,
        )

    for k in range(1, nplane):
        spots_to(k).start()

    def arrival(i, carry):
        t, side = i // 2, lax.rem(i, 2)
        chunk = jnp.where(side == 0, group - 1 - t, group + 1 + t)

        @pl.when((chunk >= 0) & (chunk < ngroup))
        def _():
            safe = jnp.clip(chunk, 0, ngroup - 1)
            pltpu.make_async_remote_copy(
                src_ref=raw.at[safe],
                dst_ref=raw.at[safe],
                send_sem=zsend.at[side, t],
                recv_sem=zrecv.at[side, t],
                device_id=(group, plane),
                device_id_type=MESH,
            ).wait_recv()

            @pl.when(t < ngroup - 2)
            def _():
                inside, copy = along(side, jnp.minimum(t + 1, ngroup - 2))
                pl.when(inside)(copy.start)

            share(safe)

        return carry

    lax.fori_loop(0, 2 * (ngroup - 1), arrival, 0)

    for side in range(2):
        for t in range(ngroup - 1):
            inside, copy = along(side, t)
            pl.when(inside)(copy.wait_send)

    own_spots.wait()
    for copy in line:
        copy.wait_send()
    for k in range(1, nplane):
        spots_to(k).wait_send()
        spots_to(k).wait_recv()

    def finish(chunk):
        keep(chunk).wait()

        def one(k, carry):
            copy = to_peer(chunk, k)
            copy.wait_send()
            copy.wait_recv()
            return carry

        lax.fori_loop(1, nplane, one, 0)

    finish(group)

    def farther(i, carry):
        t, side = i // 2, lax.rem(i, 2)
        chunk = jnp.where(side == 0, group - 1 - t, group + 1 + t)
        pl.when((chunk >= 0) & (chunk < ngroup))(lambda: finish(jnp.clip(chunk, 0, ngroup - 1)))
        return carry

    lax.fori_loop(0, 2 * (ngroup - 1), farther, 0)


def split(values):
    high = values.astype(jnp.bfloat16)
    return high, (values - high.astype(jnp.float32)).astype(jnp.bfloat16)


def spectrum_kernel(
    nplane, ngroup, capacity, blocks, evens, total, scale,
    places_hbm, bricks_hbm, tx_hbm, ty_hbm, real_hbm, imag_hbm,
    grid, rows, lines, places, bricks, tx, ty, out_real, out_imag, loaded, stored,
):
    half = rows.shape[-1] // 2
    width = rows.shape[-1]
    device = lax.axis_index("zg") * nplane + lax.axis_index("zl")
    loads = [pltpu.make_async_copy(places_hbm, places, loaded.at[0])]
    for chunk in range(ngroup):
        loads.append(
            pltpu.make_async_copy(
                bricks_hbm.at[:, chunk], bricks.at[:, chunk], loaded.at[1 + chunk]
            )
        )
    loads.append(pltpu.make_async_copy(tx_hbm, tx, loaded.at[1 + ngroup]))
    loads.append(pltpu.make_async_copy(ty_hbm, ty, loaded.at[2 + ngroup]))
    for load in loads:
        load.start()

    def clear(i, carry):
        grid[pl.ds(i * 32, 32)] = jnp.zeros((32,) + grid.shape[1:], jnp.float32)
        return carry

    lax.fori_loop(0, grid.shape[0] // 32, clear, 0)

    def place(chunk, pair):
        slots = [(pair * 2 + n, c) for n in range(2) for c in range(capacity)]
        ids = [places[source, chunk, c] for source, c in slots]
        values = [grid[at] + bricks[source, chunk, c] for at, (source, c) in zip(ids, slots)]
        for at, value in zip(ids, values):
            grid[at] = value

    loads[0].wait()
    for chunk in range(ngroup):
        loads[1 + chunk].wait()
        lax.fori_loop(0, nplane // 2, lambda pair, carry: (place(chunk, pair), carry)[1], 0)

    batch = 4

    def arrange(step, carry):
        for h in range(2):
            tiles = []
            for i in range(8):
                first, second = (
                    jnp.stack([grid[(step * batch + n) * blocks + at + i] for n in range(batch)])
                    for at in (h * 8, h * 8 + 16)
                )
                tiles.append((first + second, first - second))
            for side in range(2):
                lines_of = transposed_blocks([pair[side] for pair in tiles], 16)
                for j in range(8):
                    kz, ri, parity = j // 4, j // 2 % 2, j % 2
                    lanes = pl.ds(ri * half + h * 128, 128)
                    at = pl.ds(pl.multiple_of(step * batch * 8, batch * 8), batch * 8)
                    rows[side, kz, parity, at, lanes] = lines_of[j].reshape(-1, 128)
        return carry

    lax.fori_loop(0, blocks // batch, arrange, 0)
    loads[1 + ngroup].wait()

    def product(a, b, dims):
        return lax.dot_general(a, b, (dims, ((), ())), preferred_element_type=jnp.float32)

    padded = tx.shape[1] // 4
    for parity in range(2):
        for odd in range(2):
            table = tx.at[odd]
            count = table.shape[0] // 2
            for kz in range(ZLOC):
                high, low = split(rows[odd, kz, parity])
                both = product(table[...], high, ((1,), (1,)))
                first = both[:count] + (both[count:] + product(table[:count], low, ((1,), (1,))))
                at = pl.ds((odd * ZLOC + kz) * padded, padded)
                lines[parity, at, :half] = first[:padded]
                lines[parity, at, half:] = first[padded:]

    loads[2 + ngroup].wait()
    results = []
    for parity in range(2):
        high, low = split(lines[parity])
        count = high.shape[0]
        both = product(jnp.concatenate([high, low], axis=0), ty[parity, 0], ((1,), (0,)))
        results.append(both[:count] + (both[count:] + product(high, ty[parity, 1], ((1,), (0,)))))
    lines[0] = results[0] + results[1]
    lines[1] = results[0] - results[1]

    def along(index, count):
        return 4.0 * jnp.sin(jnp.pi * index.astype(jnp.float32) / count) ** 2

    tiles = width // 128
    line = tiles * ZLOC
    stores = []
    for low, high in ((0, evens[1] // 2), (evens[1] // 2, padded)):
        for odd in range(2):
            count = min(high, evens[odd]) - low
            index = lax.broadcasted_iota(jnp.int32, (high - low, 1), 0) + low
            along_x = jnp.broadcast_to(along(index * 2 + odd, width), (high - low, 128))
            for kz in range(ZLOC):
                turn = jnp.full((8, 128), kz_of(device * ZLOC + kz, total), jnp.int32)
                along_z = along(turn, total)[:1]
                at = pl.ds((odd * ZLOC + kz) * padded + low, high - low)
                for tile in range(tiles):
                    across = lax.broadcasted_iota(jnp.int32, (8, 128), 1) + tile * 128
                    denom = along_z + along_x + along(across, width)[:1] + SCREEN
                    factor = scale / denom
                    sign, lane = tile // (tiles // 2), tile % (tiles // 2) * 128
                    for out, start in ((out_real, 0), (out_imag, half)):
                        value = lines[sign, at, pl.ds(start + lane, 128)] * factor
                        row = (low * 2 + odd) * line + tile * ZLOC + kz
                        out[pl.ds(row, count, stride=2 * line), :] = value[:count]
        first, last = low * 2 * line, min(high * 2 * line, out_real.shape[0])
        for i, (source, target) in enumerate(((out_real, real_hbm), (out_imag, imag_hbm))):
            span = pl.ds(first, last - first)
            stores.append(
                pltpu.make_async_copy(
                    source.at[span], target.at[span], stored.at[len(stores)]
                )
            )
            stores[-1].start()
    for store in stores:
        store.wait()


def parted(table):
    high = table.astype(ml_dtypes.bfloat16)
    low = (table - high.astype(np.float64)).astype(ml_dtypes.bfloat16)
    return high, low


def x_tables(width):
    tables = []
    for odd in range(2):
        padded = -(-(width // 4 + 1) // 8) * 8
        kx = 2 * np.arange(padded)[:, None] + odd
        angles = 2 * np.pi / width * (kx * np.arange(width // 2)[None, :] % width)
        cosine, sine = np.cos(angles), np.sin(angles)
        tables.append(np.concatenate(parted(np.block([[cosine, sine], [-sine, cosine]]))))
    return tables


def y_tables(width):
    tables = []
    for parity in range(2):
        y = 2 * np.arange(width // 2)[:, None] + parity
        angles = 2 * np.pi / width * (y * np.arange(width // 2)[None, :] % width)
        cosine, sine = np.cos(angles), np.sin(angles)
        tables.append(np.stack(parted(np.block([[cosine, -sine], [sine, cosine]]))))
    return np.stack(tables)


def on_device_once(brick_data, brick_xy, brick_live):
    capacity, brick, area = brick_data.shape
    ngroup, nplane = lax.axis_size("zg"), lax.axis_size("zl")
    total = ZLOC * ngroup * nplane
    width = PLANE
    blocks = width // brick
    quads = capacity // 4
    kz = np.array([reversed_bits(row, bit_count(total)) for row in range(0, total, ZLOC)])
    angles = kz.reshape(ngroup, 1, nplane, 1) * np.arange(ngroup * brick).reshape(-1, 1, brick)
    angles = 2 * np.pi / total * (angles % total)
    coef = np.stack([np.cos(angles), -np.sin(angles)], axis=-1).astype(np.float32).reshape(-1)

    vmem = pl.BlockSpec(memory_space=pltpu.VMEM)
    smem = pl.BlockSpec(memory_space=pltpu.SMEM)
    anywhere = pl.BlockSpec(memory_space=pl.ANY)
    arrived, places = pl.pallas_call(
        functools.partial(exchange_kernel, ngroup, nplane, capacity, blocks),
        out_shape=(
            jax.ShapeDtypeStruct((nplane, ngroup, capacity, 8, 128), jnp.float32),
            jax.ShapeDtypeStruct((nplane, 8, 128), jnp.int32),
        ),
        in_specs=[smem, smem, anywhere, vmem],
        out_specs=(anywhere, anywhere),
        scratch_shapes=[
            pltpu.VMEM(brick_data.shape, jnp.float32),
            pltpu.VMEM((ngroup, quads * brick * 8, 128), jnp.float32),
            pltpu.VMEM((ngroup, nplane, capacity, 8, 128), jnp.float32),
            pltpu.VMEM((8, 128), jnp.int32),
            pltpu.VMEM((ngroup, 8, 128), jnp.int32),
            pltpu.VMEM((8, 128), jnp.int32),
            pltpu.SemaphoreType.DMA((2, ngroup - 1)),
            pltpu.SemaphoreType.DMA((2, ngroup - 1)),
            pltpu.SemaphoreType.DMA((ngroup, nplane)),
            pltpu.SemaphoreType.DMA((ngroup, nplane)),
            pltpu.SemaphoreType.DMA((nplane,)),
            pltpu.SemaphoreType.DMA((nplane,)),
            pltpu.SemaphoreType.DMA((ngroup,)),
            pltpu.SemaphoreType.DMA((ngroup,)),
            pltpu.SemaphoreType.DMA,
        ],
        compiler_params=pltpu.CompilerParams(
            collective_id=0, has_side_effects=True, vmem_limit_bytes=60 * 2**20
        ),
        name="exchange",
    )(jnp.asarray(coef), brick_live, brick_data, brick_xy)

    tx = np.stack(x_tables(width))
    evens = (width // 4 + 1, width // 4)
    ty = y_tables(width)
    kx_count = width // 2 + 1
    out = jax.ShapeDtypeStruct((kx_count * width // 128 * ZLOC, 128), jnp.float32)
    scale = -1.0 / math.sqrt(width * width * total)
    results = pl.pallas_call(
        functools.partial(spectrum_kernel, nplane, ngroup, capacity, blocks, evens, total, scale),
        out_shape=(out, out),
        in_specs=[anywhere] * 4,
        out_specs=(anywhere, anywhere),
        scratch_shapes=[
            pltpu.VMEM((blocks * blocks, 8, 128), jnp.float32),
            pltpu.VMEM((2, ZLOC, 2, width // 2, width), jnp.float32),
            pltpu.VMEM((2, ZLOC * tx.shape[1] // 2, width), jnp.float32),
            pltpu.SMEM(places.shape, jnp.int32),
            pltpu.VMEM(arrived.shape, jnp.float32),
            pltpu.VMEM(tx.shape, tx.dtype),
            pltpu.VMEM(ty.shape, ty.dtype),
            pltpu.VMEM(out.shape, jnp.float32),
            pltpu.VMEM(out.shape, jnp.float32),
            pltpu.SemaphoreType.DMA((3 + ngroup,)),
            pltpu.SemaphoreType.DMA((4,)),
        ],
        compiler_params=pltpu.CompilerParams(vmem_limit_bytes=60 * 2**20),
        name="spectrum",
    )(places, arrived, jnp.asarray(tx), jnp.asarray(ty))

    def ordered(result):
        result = result.reshape(kx_count, width // 128, ZLOC, 128)
        return jnp.transpose(result, (2, 0, 1, 3)).reshape(ZLOC, kx_count, width)

    return tuple(ordered(result) for result in results)


def on_device(brick_data, brick_xy, brick_live):
    layers = brick_live.shape[0]
    slots, brick, area = brick_data.shape
    nplane, ngroup = lax.axis_size("zl"), lax.axis_size("zg")
    one_layer = layers == 1 and nplane * ZLOC == brick and brick == 16 and slots == 16
    fits = slots * nplane * ngroup * area * 2 * ZLOC * 4 <= 4 * 2**20
    if one_layer and fits and ngroup > 1:
        return on_device_once(brick_data, brick_xy, brick_live)
    return on_device_wide(brick_data, brick_xy, brick_live)


def solution(mesh):
    in_specs = (P(("zg", "zl"), None, None), P(None, ("zg", "zl")), P(None, ("zg", "zl")))
    out_specs = (P(("zg", "zl"), None, None), P(("zg", "zl"), None, None))
    return jax.shard_map(
        on_device, mesh=mesh, in_specs=in_specs, out_specs=out_specs, check_vma=False
    )
```
